256 devices in a mesh: seq: 32 (over z, y), head: 8 (over x, core).
Axes of the slice: x: 4, y: 4, z: 8, core: 2. Of those that a mesh axis runs over, the one named last changes fastest.
Arguments:
- tokens: bfloat16 [16384, 4096], P('seq', 'head'), may hold values from -6 to 6
- w_zx: bfloat16 [4096, 2, 8192], P('seq', None, 'head'), may hold values from -0.09375 to 0.09375
- w_bc: bfloat16 [4096, 2, 1024], P('seq', None, 'head'), may hold values from -0.09375 to 0.09375
- w_dt: bfloat16 [4096, 128], P('seq', 'head'), may hold values from -0.09375 to 0.09375
- conv_x: bfloat16 [4, 8192], P(None, 'head'), may hold values from -3 to 3
- conv_bc: bfloat16 [4, 2, 1024], P(None, None, 'head'), may hold values from -3 to 3
- dt_bias: float32 [128], P('head'), may hold values from -1 to 1
- a_log: float32 [128], P('head'), may hold values from -13 to -1.8
- d_skip: float32 [128], P('head'), may hold values from 0.5 to 1.5
- norm_gain: bfloat16 [8192], P('head'), may hold values from 0.099609375 to 1.8984375
- w_out: bfloat16 [8192, 4096], P('head'), may hold values from -0.09375 to 0.09375
Outputs:
- mixed: bfloat16 [16384, 4096], P('seq', 'head')
The draws below stay inside these ranges and needn't reach their ends.
All inputs are finite; a program needn't handle non-finite values.
Results may differ from the reference program's by a relative error of at most 0.017.
Values may be sent and summed in bfloat16 or wider, within the bound.
No kernel may reach another device: no remote copies, remote signals or barrier semaphores. Data moves between devices by JAX's collectives and lax.ppermute only.
A program may use at most 128 MiB of HBM per device.

```python
import math
import jax
import jax.numpy as jnp
from jax import lax

D = 4096
H = 128
P_SIZE = 64
N = 128
G = 8
K = 4
Q = 128
DI = 8192
GN = 1024
TOKENS = 16384
N_HEAD = 8


def draw_a_log(key, part):
    key = jax.random.fold_in(key, 7)
    lowest = math.log(0.1 / TOKENS)
    highest = math.log(0.15)
    uniform_part = jax.random.uniform(key, (H,), jnp.float32)
    return (lowest + (highest - lowest) * uniform_part).astype(jnp.float32)


def with_spikes(entries, stream_key, source, target, shards_of, factor):
    owner, partner = [(jnp.arange(entries.shape[position]) // (entries.shape[position] // shards_of)).reshape([-1 if axis == position else 1 for axis in range(entries.ndim)]) for position in (source, target)]
    chosen = jax.random.permutation(stream_key, shards_of)[partner]
    strong = (owner == chosen) | (owner == (partner + shards_of // 2) % shards_of)
    return jnp.where(strong, factor * entries, entries)


def level_of(stream_key, shape, split, least, high):
    loudness = 1.0
    for position, parts in split:
        heights = jax.random.uniform(jax.random.fold_in(jax.random.fold_in(stream_key, 6), position), (parts,), jnp.float32, least / len(split), high / len(split))
        loudness = loudness * jnp.repeat(jnp.exp(heights), shape[position] // parts).reshape((-1,) + (1,) * (len(shape) - 1 - position))
    return loudness


def noise(stream_key, extent, width, limit, cuts=(), kind=jnp.bfloat16):
    factor_of = level_of(stream_key, extent, cuts, -0.22, 0.18) if cuts else 1.0
    entries = jax.random.normal(stream_key, extent, jnp.float32) * width * factor_of
    return jnp.minimum(jnp.maximum(entries, -limit), limit).astype(kind)


def bell_draw_with(rng, dims, scale, limit, split, heavy, kind=jnp.bfloat16):
    result = scale * jax.random.normal(rng, dims, jnp.float32)
    if split:
        result = result * level_of(rng, dims, split, -0.22, 0.18)
    return jnp.clip(with_spikes(result, jax.random.fold_in(rng, 3), *heavy), -limit, limit).astype(kind)


def setup_inputs(seed: int = 0) -> dict:
    splits = jax.random.split(jax.random.key(seed), 12)
    tokens = noise(splits[0], (TOKENS, D), 1.0, 6.0, ((0, 32), (1, 8)))
    w_zx = noise(splits[1], (D, 2, DI), D ** -0.5, 0.09375, ((0, 32), (2, 8)))
    w_bc = noise(splits[2], (D, 2, GN), D ** -0.5, 0.09375, ((0, 32), (2, 8)))
    w_dt = noise(splits[3], (D, H), D ** -0.5, 0.09375, ((0, 32), (1, 8)))
    conv_x = noise(splits[4], (K, DI), K ** -0.5, 3.0, ((1, 8),))
    conv_bc = noise(splits[5], (K, 2, GN), K ** -0.5, 3.0, ((2, 8),))
    dt_bias = jnp.clip(jax.random.uniform(splits[6], (H,), jnp.float32, -1.0, 1.0) * level_of(splits[6], (H,), ((0, 8),), -0.4, 0.0), -1.0, 1.0)
    a_log = draw_a_log(jax.random.fold_in(splits[11], 71), 0)
    d_skip = jnp.clip(0.5 + 1.0 * jax.random.uniform(splits[8], (H,), jnp.float32) ** level_of(splits[8], (H,), ((0, 8),), -0.2, 0.2), 0.5, 1.5)
    norm_gain = jnp.clip(1.0 + 0.18 * jax.random.normal(splits[9], (DI,), jnp.float32), 0.099609375, 1.8984375).astype(jnp.bfloat16)
    w_out = bell_draw_with(splits[10], (DI, D), DI ** -0.5, 0.09375, ((0, 8),), (0, 1, 8, 2.0))
    return dict(tokens=tokens, w_zx=w_zx, w_bc=w_bc, w_dt=w_dt, conv_x=conv_x, conv_bc=conv_bc, dt_bias=dt_bias, a_log=a_log, d_skip=d_skip, norm_gain=norm_gain, w_out=w_out)


EPSILON = 1e-05
HIGHEST = lax.Precision.HIGHEST

def conv_silu(padded, weight):
    tap_count = weight.shape[0]
    out_rows = padded.shape[0] - tap_count + 1
    summed = jnp.zeros((out_rows, padded.shape[1]), jnp.float32)
    for tap_index in range(tap_count):
        summed = summed + weight[tap_index].astype(jnp.float32) * padded[tap_index:tap_index + out_rows].astype(jnp.float32)
    return jax.nn.silu(summed).astype(jnp.bfloat16)

def block_step(ssm_state, pieces):
    x_part, b_part, c_part, decay_rate, step_size = pieces
    block_rows = decay_rate.shape[0]
    running = jnp.cumsum(decay_rate, axis=0)
    scores = jnp.einsum('ign,jgn->ijg', c_part.astype(jnp.float32), b_part.astype(jnp.float32), precision=HIGHEST)
    spread = running[:, None] - running[None, :]
    causal = (lax.broadcasted_iota(jnp.int32, (block_rows, block_rows), 0) >= lax.broadcasted_iota(jnp.int32, (block_rows, block_rows), 1))[:, :, None, None]
    kernel = jnp.where(causal, jnp.exp(jnp.where(causal, spread, 0.0)), 0.0)
    mixing = (kernel * step_size[None] * scores[:, :, :, None]).astype(jnp.bfloat16)
    within = jnp.einsum('ijgh,jghp->ighp', mixing.astype(jnp.float32), x_part.astype(jnp.float32), precision=HIGHEST)
    carried = jnp.exp(running)[..., None] * jnp.einsum('ign,ghpn->ighp', c_part.astype(jnp.float32), ssm_state, precision=HIGHEST)
    to_end = jnp.exp(running[-1][None] - running) * step_size
    weighted = (x_part.astype(jnp.float32) * to_end[..., None]).astype(jnp.bfloat16)
    increment = jnp.einsum('jghp,jgn->ghpn', weighted.astype(jnp.float32), b_part.astype(jnp.float32), precision=HIGHEST)
    return (jnp.exp(running[-1])[..., None, None] * ssm_state + increment, within + carried)

def reference(tokens, w_zx, w_bc, w_dt, conv_x, conv_bc, dt_bias, a_log, d_skip, norm_gain, w_out):
    inner_width = DI // N_HEAD
    bc_width = GN // N_HEAD
    head_count = H // N_HEAD
    per_group = H // G
    groups = head_count // per_group
    block_count = TOKENS // Q

    def as_blocks(value):
        return value.reshape((block_count, Q) + value.shape[1:])

    def one_shard(running_out, shard_index):
        zx_weight = lax.dynamic_slice_in_dim(w_zx, shard_index * inner_width, inner_width, 2)
        bc_weight = lax.dynamic_slice_in_dim(w_bc, shard_index * bc_width, bc_width, 2)
        dt_weight = lax.dynamic_slice_in_dim(w_dt, shard_index * head_count, head_count, 1)
        conv_xw = lax.dynamic_slice_in_dim(conv_x, shard_index * inner_width, inner_width, 1)
        conv_bcw = lax.dynamic_slice_in_dim(conv_bc, shard_index * bc_width, bc_width, 2).reshape(K, 2 * bc_width)
        bias_part = lax.dynamic_slice_in_dim(dt_bias, shard_index * head_count, head_count, 0)
        alog_part = lax.dynamic_slice_in_dim(a_log, shard_index * head_count, head_count, 0)
        skip_part = lax.dynamic_slice_in_dim(d_skip, shard_index * head_count, head_count, 0)
        gain_part = lax.dynamic_slice_in_dim(norm_gain, shard_index * inner_width, inner_width, 0)
        out_weight = lax.dynamic_slice_in_dim(w_out, shard_index * inner_width, inner_width, 0)
        zx_sum = jnp.dot(tokens, zx_weight.reshape(D, 2 * inner_width), preferred_element_type=jnp.float32)
        gate_act = zx_sum[:, :inner_width].astype(jnp.bfloat16)
        x_pre = zx_sum[:, inner_width:].astype(jnp.bfloat16)
        bc_pre = jnp.dot(tokens, bc_weight.reshape(D, 2 * bc_width), preferred_element_type=jnp.float32).astype(jnp.bfloat16)
        dt_raw = jnp.dot(tokens, dt_weight, preferred_element_type=jnp.float32)
        x_conv = conv_silu(jnp.pad(x_pre, ((K - 1, 0), (0, 0))), conv_xw)
        bc_conv = conv_silu(jnp.pad(bc_pre, ((K - 1, 0), (0, 0))), conv_bcw).reshape(TOKENS, 2, groups, N)
        x_heads = x_conv.reshape(TOKENS, groups, per_group, P_SIZE)
        step_size = jax.nn.softplus(dt_raw + bias_part)
        decay_rate = (-step_size * jnp.exp(alog_part)).reshape(TOKENS, groups, per_group)
        step_size = step_size.reshape(TOKENS, groups, per_group)
        start_state = jnp.zeros((groups, per_group, P_SIZE, N), jnp.float32)
        _, y_blocks = lax.scan(block_step, start_state, (as_blocks(x_heads), as_blocks(bc_conv[:, 0]), as_blocks(bc_conv[:, 1]), as_blocks(decay_rate), as_blocks(step_size)))
        mixed_heads = y_blocks.reshape(TOKENS, groups, per_group, P_SIZE) + skip_part.reshape(groups, per_group)[..., None] * x_heads.astype(jnp.float32)
        gated_out = mixed_heads * jax.nn.silu(gate_act.reshape(TOKENS, groups, per_group, P_SIZE).astype(jnp.float32))
        mean_square = lax.optimization_barrier(jnp.mean(gated_out * gated_out, axis=(2, 3), keepdims=True))
        hidden = (gated_out * lax.rsqrt(mean_square + EPSILON) * gain_part.reshape(groups, per_group, P_SIZE).astype(jnp.float32)).astype(jnp.bfloat16).reshape(TOKENS, inner_width)
        partial_value = jnp.dot(hidden, out_weight, preferred_element_type=jnp.float32).astype(jnp.bfloat16)
        partial_value = lax.optimization_barrier(partial_value)
        return (running_out + partial_value.astype(jnp.float32), None)
    running_out, _ = lax.scan(one_shard, jnp.zeros((TOKENS, D), jnp.float32), jnp.arange(N_HEAD, dtype=jnp.int32))
    return running_out.astype(jnp.bfloat16)
```

```python
import jax
import jax.numpy as jnp
from jax import lax
from jax.experimental import pallas as pl
from jax.experimental.pallas import tpu as pltpu
from jax.sharding import Mesh, PartitionSpec as P

EPSILON = 1e-05
BF = jnp.bfloat16
F32 = jnp.float32
MIB = 1024 * 1024

NZ, NY, NX, NC = 8, 4, 4, 2
ROWS = 512
HALF = ROWS // 2
FEAT = 512
HALO = 16
D = 4096
T = ROWS * NY
CH = 256
HD = 4
PS = 64
N = 128
Q = 128
NB = T // Q
W1 = 384
W2 = 256
STRIDE = ROWS + HALO
OFFSETS = (0, -1, 1, 2)


def shifted(value, axis, distance):
    n = lax.axis_size(axis)
    return lax.ppermute(value, axis, [(i, (i + distance) % n) for i in range(n)])


def sibling(value):
    return lax.ppermute(value, "c", [(0, 1), (1, 0)])


def gather_tokens(tokens):
    pairs = [(z * NY + NY - 1, (z + 1) * NY) for z in range(NZ - 1)]
    halo = lax.ppermute(tokens[ROWS - HALO :], ("z", "y"), pairs)
    a = jnp.concatenate([halo, tokens[:HALF]], axis=0)
    b = tokens[HALF:]
    a_s = jnp.stack([a, shifted(a, "x", 1), shifted(a, "x", -1), shifted(a, "x", 2)])
    b_s = jnp.stack([b, shifted(b, "y", 1), shifted(b, "y", -1), shifted(b, "y", 2)])
    a_r, a_l = shifted(a_s, "y", 1), shifted(a_s, "y", -1)
    b_r, b_l = shifted(b_s, "x", 1), shifted(b_s, "x", -1)
    a_2r, a_2l = shifted(a_r[:2], "y", 1), shifted(a_l[2:], "y", -1)
    b_2r, b_2l = shifted(b_r[:2], "x", 1), shifted(b_l[2:], "x", -1)
    own = [a_s, a_r, a_l, a_2r, a_2l, b_s, b_r, b_l, b_2r, b_2l]
    return own + [sibling(piece) for piece in own]


def tiles_of():
    out = []
    for j, dy in enumerate(OFFSETS):
        entries = []
        for core in range(2):
            base = 10 * core
            for i, dx in enumerate(OFFSETS):
                if j < 3:
                    entries.append((base + j, i, dx, core))
                else:
                    entries.append((base + 3 + i // 2, i % 2, dx, core))
        out.append((0, dy, entries))
    for j, dy in enumerate(OFFSETS):
        entries = []
        for core in range(2):
            base = 10 * core + 5
            for i, dx in enumerate(OFFSETS):
                if i < 3:
                    entries.append((base + i, j, dx, core))
                else:
                    entries.append((base + 3 + j // 2, j % 2, dx, core))
        out.append((1, dy, entries))
    return out


def token_copies(place, refs, tok, sems):
    x, y, c = place[0], place[1], place[2]
    result = []
    for number, (half, dy, entries) in enumerate(tiles_of()):
        yy = lax.rem(y + (dy + NY), NY)
        start = pl.multiple_of(yy * STRIDE + (HALF + HALO) * half, 16)
        size = HALF if half else HALF + HALO
        copies = []
        for k, (array, index, dx, core) in enumerate(entries):
            cc = 1 - c if core else c
            block = lax.rem(x + (dx + NX), NX) * NC + cc
            lane = pl.multiple_of(block * FEAT, FEAT)
            copies.append(
                pltpu.make_async_copy(
                    refs[array].at[index],
                    tok.at[pl.ds(start, size), pl.ds(lane, FEAT)],
                    sems.at[number, k],
                )
            )
        row = pl.multiple_of(yy * ROWS + HALF * half, HALF)
        result.append((start + (0 if half else HALO), row, copies))
    return result


def silu(v):
    return v / (1.0 + jnp.exp(-v))


def project_first(place, taps_bc, w_ref, *rest):
    refs, (x_ref, bc_ref, dt_ref, tok, bc_pre, sems) = rest[:20], rest[20:]
    work = token_copies(place, refs, tok, sems)
    for _, _, copies in work:
        for copy in copies:
            copy.start()
    for start, row, copies in work:
        for copy in copies:
            copy.wait()
        rows = tok[pl.ds(pl.multiple_of(start, 16), HALF), :]
        acc = jnp.dot(rows, w_ref[...], preferred_element_type=F32)
        x_ref[pl.ds(pl.multiple_of(row + HALO, 16), HALF), :] = acc[:, :CH].astype(BF)
        side = acc[:, CH:].T
        bc_pre[:, pl.ds(pl.multiple_of(row + 128, 128), HALF)] = side[:64].astype(BF).astype(F32)
        dt_ref[:, pl.ds(pl.multiple_of(row, 128), HALF)] = side[64:72]
    acc = jnp.dot(tok[:HALO, :], w_ref[...], preferred_element_type=F32)
    x_ref[:HALO, :] = acc[:, :CH].astype(BF)
    wide = jnp.concatenate([jnp.zeros((128 - HALO, 128), F32), acc[:, CH:]], axis=0)
    bc_pre[:, :128] = wide.T[:64].astype(BF).astype(F32)
    lane = lax.broadcasted_iota(jnp.int32, (64, 128), 1)
    for block in range(NB):
        before = bc_pre[:, block * 128 : block * 128 + 128]
        now = bc_pre[:, block * 128 + 128 : block * 128 + 256]
        total = taps_bc[:, 3:4] * now
        for back in (1, 2, 3):
            moved = jnp.where(
                lane < back, pltpu.roll(before, back, 1), pltpu.roll(now, back, 1)
            )
            total = total + taps_bc[:, 3 - back : 4 - back] * moved
        bc_ref[:, block * 128 : block * 128 + 128] = silu(total).astype(BF)


def project_second(place, w_ref, *rest):
    refs, (z_ref, tok, sems) = rest[:20], rest[20:]
    work = token_copies(place, refs, tok, sems)
    for _, _, copies in work:
        for copy in copies:
            copy.start()
    for start, row, copies in work:
        for copy in copies:
            copy.wait()
        rows = tok[pl.ds(pl.multiple_of(start, 16), HALF), :]
        acc = jnp.dot(rows, w_ref[...], preferred_element_type=F32)
        z_ref[pl.ds(row, HALF), :] = acc.astype(BF)


def run_projection(kernel, place, weights, pieces, extra, outs, scratch):
    return pl.pallas_call(
        kernel,
        out_shape=outs,
        in_specs=[pl.BlockSpec(memory_space=pltpu.SMEM)]
        + [pl.BlockSpec(memory_space=pltpu.VMEM)] * (len(extra) + 1)
        + [pl.BlockSpec(memory_space=pl.ANY)] * 20,
        out_specs=[pl.BlockSpec(memory_space=pltpu.VMEM)] * len(outs),
        scratch_shapes=[pltpu.VMEM((NY * STRIDE, D), BF)]
        + scratch
        + [pltpu.SemaphoreType.DMA((8, 8))],
        compiler_params=pltpu.CompilerParams(vmem_limit_bytes=48 * MIB),
        cost_estimate=pl.CostEstimate(
            flops=2 * T * D * weights.shape[1], bytes_accessed=20 * MIB, transcendentals=0
        ),
    )(place, *extra, weights, *pieces)


def conv_and_rates(x_ref, taps, dt_ref, bias, a_log, out_ref, run_ref, step_ref):
    for block in range(NB):
        window = x_ref[pl.ds(block * Q, Q + HALO), :].astype(F32)
        total = taps[3:4, :] * window[HALO:, :]
        for back in (1, 2, 3):
            total = total + taps[3 - back : 4 - back, :] * window[HALO - back : HALO - back + Q, :]
        out_ref[pl.ds(block * Q, Q), :] = silu(total).astype(BF)
    lane = lax.broadcasted_iota(jnp.int32, (8, Q), 1)
    factor = -jnp.exp(a_log[...])
    for block in range(NB):
        raw = dt_ref[:, block * Q : (block + 1) * Q] + bias[...]
        step = jnp.maximum(raw, 0.0) + jnp.log1p(jnp.exp(-jnp.abs(raw)))
        running = step * factor
        for distance in (1, 2, 4, 8, 16, 32, 64):
            running = running + jnp.where(lane < distance, 0.0, pltpu.roll(running, distance, 1))
        run_ref[:, block * Q : (block + 1) * Q] = running
        step_ref[:, block * Q : (block + 1) * Q] = step


def states(x_ref, b_ref, run_ref, step_ref, local_ref, end_ref):
    state = [jnp.zeros((N, PS), F32) for _ in range(HD)]
    full = jnp.zeros((8, Q), F32)
    for block in range(NB):
        at = slice(block * Q, (block + 1) * Q)
        running, step = run_ref[:, at], step_ref[:, at]
        last = running[:, Q - 1 : Q]
        weight = jnp.exp(last - running) * step
        decay = jnp.exp(last)
        b = b_ref[:N, at].astype(F32)
        for h in range(HD):
            local_ref[block, :, h * PS : (h + 1) * PS] = state[h].astype(BF)
            scaled = (b * weight[h : h + 1, :]).astype(BF)
            increment = jnp.dot(
                scaled, x_ref[at, h * PS : (h + 1) * PS], preferred_element_type=F32
            )
            state[h] = decay[h : h + 1, :] * state[h] + increment
        full = full + last
    for h in range(HD):
        end_ref[:N, h * PS : (h + 1) * PS] = state[h].astype(BF)
    whole = jnp.exp(full)
    high = whole.astype(BF)
    low = (whole - high.astype(F32)).astype(BF)
    row = jnp.concatenate([high, low], axis=0)
    end_ref[N:, :] = jnp.concatenate([row, row], axis=1)


def within(x_ref, bc_ref, run_ref, step_ref, skip, y_ref):
    below = lax.broadcasted_iota(jnp.int32, (Q, Q), 0) >= lax.broadcasted_iota(
        jnp.int32, (Q, Q), 1
    )
    for block in range(NB):
        at = slice(block * Q, (block + 1) * Q)
        running, step = run_ref[:, at], step_ref[:, at]
        columns = running.T
        scores = lax.dot_general(
            bc_ref[N:, at], bc_ref[:N, at], (((0,), (0,)), ((), ())), preferred_element_type=F32
        )
        for h in range(HD):
            spread = jnp.where(below, columns[:, h : h + 1] - running[h : h + 1, :], -1e30)
            mixing = (jnp.exp(spread) * step[h : h + 1, :] * scores).astype(BF)
            value = x_ref[at, h * PS : (h + 1) * PS]
            y = jnp.dot(mixing, value, preferred_element_type=F32)
            y_ref[at, h * PS : (h + 1) * PS] = (
                y + skip[:, h * PS : (h + 1) * PS] * value.astype(F32)
            )


def per_head(columns):
    return jnp.concatenate(
        [jnp.broadcast_to(columns[:, h : h + 1], (columns.shape[0], PS)) for h in range(HD)],
        axis=1,
    )


def over_channels(rows):
    return jnp.concatenate([rows[h : h + 1, :PS] for h in range(HD)], axis=1)


def carry(bc_ref, run_ref, local_ref, y_ref, z_ref, *rest):
    arrived, out_ref = rest[:-1], rest[-1]
    state = jnp.zeros((N, CH), F32)
    weight = jnp.ones((1, CH), F32)
    for ref in arrived:
        state = state + weight * ref[:N, :].astype(F32)
        decay = ref[N : N + 8, :].astype(F32) + ref[N + 8 : N + 16, :].astype(F32)
        weight = weight * over_channels(decay[:, :128])
    before = jnp.ones((1, CH), F32)
    for block in range(NB):
        at = slice(block * Q, (block + 1) * Q)
        running = run_ref[:, at]
        full = (local_ref[block].astype(F32) + before * state).astype(BF)
        carried = lax.dot_general(
            bc_ref[N:, at], full, (((0,), (0,)), ((), ())), preferred_element_type=F32
        )
        grown = jnp.exp(running)
        y = y_ref[at, :] + per_head(grown.T) * carried
        gate = silu(z_ref[at, :].astype(F32))
        out_ref[at, :] = (y * gate).astype(BF)
        last = jnp.broadcast_to(grown[:, Q - 1 : Q], (8, Q))
        before = before * over_channels(last)


def local_call(kernel, outs, *args, flops=1, limit=32):
    return pl.pallas_call(
        kernel,
        out_shape=outs,
        in_specs=[pl.BlockSpec(memory_space=pltpu.VMEM)] * len(args),
        out_specs=jax.tree.map(lambda _: pl.BlockSpec(memory_space=pltpu.VMEM), outs),
        compiler_params=pltpu.CompilerParams(vmem_limit_bytes=limit * MIB),
        cost_estimate=pl.CostEstimate(flops=flops, bytes_accessed=4 * MIB, transcendentals=0),
    )(*args)


def project_out(place, gain, w_ref, *rest):
    refs, (out_ref, hidden) = rest[:4], rest[4:]

    @pl.when(pl.program_id(0) == 0)
    def _():
        total = jnp.zeros((ROWS, 1), F32)
        for ref in refs:
            value = ref[...].astype(F32)
            total = total + jnp.sum(value * value, axis=1, keepdims=True)
        scale = lax.rsqrt(total / (NY * CH) + EPSILON)
        for ref, dy in zip(refs, OFFSETS):
            yy = lax.rem(place[1] + (dy + NY), NY)
            lanes = pl.ds(pl.multiple_of(yy * CH, CH), CH)
            hidden[:, lanes] = (ref[...].astype(F32) * scale * gain[:, lanes]).astype(BF)

    out_ref[...] = jnp.dot(hidden[...], w_ref[...], preferred_element_type=F32).astype(BF)[None]


def run_out(place, gain, w_out, parts):
    whole = lambda i: (0, 0)
    return pl.pallas_call(
        project_out,
        grid=(NX * NC,),
        out_shape=jax.ShapeDtypeStruct((NX * NC, ROWS, FEAT), BF),
        in_specs=[pl.BlockSpec(memory_space=pltpu.SMEM), pl.BlockSpec((1, NY * CH), whole)]
        + [pl.BlockSpec((NY * CH, FEAT), lambda i: (0, i))]
        + [pl.BlockSpec((ROWS, CH), whole)] * 4,
        out_specs=pl.BlockSpec((1, ROWS, FEAT), lambda i: (i, 0, 0)),
        scratch_shapes=[pltpu.VMEM((ROWS, NY * CH), BF)],
        compiler_params=pltpu.CompilerParams(vmem_limit_bytes=32 * MIB),
        cost_estimate=pl.CostEstimate(
            flops=2 * ROWS * NY * CH * D, bytes_accessed=16 * MIB, transcendentals=0
        ),
    )(place, gain, w_out, *parts)


def swapped_y(value):
    y = lax.axis_index("y")
    take = lambda d: lax.dynamic_index_in_dim(value, lax.rem(y + (d + NY), NY), 0, False)
    return [take(0), shifted(take(1), "y", 1), shifted(take(-1), "y", -1), shifted(take(2), "y", 2)]


def in_order_y(parts):
    y = lax.axis_index("y")
    stacked = jnp.stack([parts[0], parts[2], parts[3], parts[1]])
    return jnp.roll(stacked, y, axis=0)


def on_device(tokens, w_zx, w_bc, w_dt, conv_x, conv_bc, dt_bias, a_log, d_skip, norm_gain, w_out):
    y = lax.axis_index("y")
    place = jnp.stack([lax.axis_index("x"), y, lax.axis_index("c")]).astype(jnp.int32)
    rows = w_zx.shape[0]
    quarters = lambda v: jnp.moveaxis(v.reshape(rows, NY, -1), 1, 0)
    first = jnp.concatenate(
        [
            quarters(w_zx[:, 1]),
            quarters(w_bc.reshape(rows, -1)),
            quarters(w_dt),
            jnp.zeros((NY, rows, W1 - CH - 64 - HD), BF),
        ],
        axis=2,
    )
    both = jnp.concatenate([first, quarters(w_zx[:, 0])], axis=2)
    mixed_rows = in_order_y(swapped_y(both)).reshape(NY * rows, W1 + W2)
    weights_1 = lax.all_gather(mixed_rows[:, :W1], "z", axis=0, tiled=True)
    weights_2 = lax.all_gather(mixed_rows[:, W1:], "z", axis=0, tiled=True)

    mine = lambda v, n: lax.dynamic_slice_in_dim(v, y * n, n, 0)
    taps_x = lax.dynamic_slice_in_dim(conv_x, y * CH, CH, 1).astype(F32)
    taps_bc = mine(conv_bc.reshape(4, -1).T, 64).astype(F32)
    column = lambda v: jnp.pad(mine(v, HD), (0, 8 - HD)).reshape(8, 1)
    skip = jnp.repeat(mine(d_skip, HD), PS).reshape(1, CH)

    pieces = gather_tokens(tokens)
    shape = jax.ShapeDtypeStruct
    x_pre, bc_own, dt_raw = run_projection(
        project_first,
        place,
        weights_1,
        pieces,
        [taps_bc],
        [shape((T + HALO, CH), BF), shape((64, T), BF), shape((8, T), F32)],
        [pltpu.VMEM((64, T + 128), F32)],
    )
    bc_parts = [bc_own] + [shifted(bc_own, "y", d) for d in (1, -1, 2)]
    bc = in_order_y(bc_parts).reshape(2 * N, T)
    (gate_act,) = run_projection(
        project_second, place, weights_2, pieces, [], [shape((T, CH), BF)], []
    )
    x_conv, running, step = local_call(
        conv_and_rates,
        [shape((T, CH), BF), shape((8, T), F32), shape((8, T), F32)],
        x_pre,
        taps_x,
        dt_raw,
        column(dt_bias),
        column(a_log),
    )
    local, end = local_call(
        states, [shape((NB, N, CH), BF), shape((N + 16, CH), BF)], x_conv, bc, running, step
    )
    arrived = [
        lax.ppermute(end, "z", [(i, i + d) for i in range(NZ - d)]) for d in range(1, NZ)
    ]
    y_within = local_call(
        within, shape((T, CH), F32), x_conv, bc, running, step, skip, flops=10**9
    )
    gated = local_call(
        carry, shape((T, CH), BF), bc, running, local, y_within, gate_act, *arrived
    )
    parts = swapped_y(gated.reshape(NY, ROWS, CH))
    partial_value = run_out(place, norm_gain.astype(F32).reshape(1, -1), w_out, parts)
    return lax.psum_scatter(
        partial_value.reshape(NX * NC * ROWS, FEAT), ("x", "c"), scatter_dimension=0, tiled=True
    )


def solution(mesh):
    fine = Mesh(mesh.devices.reshape(NZ, NY, NX, NC), ("z", "y", "x", "c"))
    seq, head = ("z", "y"), ("x", "c")
    return jax.shard_map(
        on_device,
        mesh=fine,
        in_specs=(
            P(seq, head),
            P(seq, None, head),
            P(seq, None, head),
            P(seq, head),
            P(None, head),
            P(None, None, head),
            P(head),
            P(head),
            P(head),
            P(head),
            P(head, None),
        ),
        out_specs=P(seq, head),
        check_vma=False,
    )
```

```python
import jax
import jax.numpy as jnp
from jax import lax
from jax.experimental import pallas as pl
from jax.experimental.pallas import tpu as pltpu
from jax.sharding import Mesh, PartitionSpec as P

EPSILON = 1e-05
BF = jnp.bfloat16
F32 = jnp.float32
MIB = 1024 * 1024

NZ, NY, NX, NC = 8, 4, 4, 2
ROWS = 512
HALF = ROWS // 2
D = 4096
T = ROWS * NY
CH = 256
HD = 4
PS = 64
N = 128
Q = 128
NB = T // Q
W1 = 384
OFFSETS = (0, -1, 1, 2)
ALL = ("z", "y", "x", "c")
VMEM = pl.BlockSpec(memory_space=pltpu.VMEM)
SMEM = pl.BlockSpec(memory_space=pltpu.SMEM)
ANY = pl.BlockSpec(memory_space=pl.ANY)
HBM = pl.BlockSpec(memory_space=pltpu.HBM)
SHAPE = jax.ShapeDtypeStruct
SMALL = pl.CostEstimate(flops=1000, bytes_accessed=1000, transcendentals=0)


def shifted(value, axis, distance):
    n = lax.axis_size(axis)
    return lax.ppermute(value, axis, [(i, (i + distance) % n) for i in range(n)])


def sibling(value):
    return lax.ppermute(value, "c", [(0, 1), (1, 0)])


def routed(value, target):
    pairs = []
    for source in range(NZ * NY * NX * NC):
        rest, c = divmod(source, NC)
        rest, x = divmod(rest, NX)
        z, y = divmod(rest, NY)
        goal = target(z, y, x, c)
        if goal is not None:
            z, y, x, c = goal
            pairs.append((source, ((z * NY + y) * NX + x) * NC + c))
    return lax.ppermute(value, ALL, pairs)


def crossed(value, along_x, distance):
    def target(z, y, x, c):
        if c == along_x:
            return z, y, (x + distance) % NX, c
        return z, (y + distance) % NY, x, c

    return routed(value, target)


def over_y(v):
    return [v[0], shifted(v[1], "y", 1), shifted(v[3], "y", -1), shifted(v[2], "y", 2)]


def half_rows(tokens, c):
    early, late = tokens[:HALF], tokens[HALF:]
    got = sibling(jnp.where(c == 0, late, early))
    return jnp.where(
        c == 0,
        jnp.concatenate([early, got], axis=1),
        jnp.concatenate([got, late], axis=1),
    )


def gather_tokens(mine, first, second):
    mine, first = lax.optimization_barrier((mine, first))
    right, left = crossed(mine, 0, 1), crossed(mine, 0, -1)
    first = over_y(first)
    right, left, first, second = lax.optimization_barrier((right, left, first, second))
    middle = HALF // 2
    opposite = [crossed(right[:middle], 0, 1), crossed(left[middle:], 0, -1)]
    second = over_y(second)
    line = jnp.stack([mine, right, left, jnp.concatenate(opposite)])
    line, second = lax.optimization_barrier((line, second))
    right, left = crossed(line, 1, 1), crossed(line, 1, -1)
    pieces = [line, right, left, crossed(right[:2], 1, 1), crossed(left[2:], 1, -1)]
    return pieces, first, second


def place_of(place, i, j):
    x, y, c = place[0], place[1], place[2]
    first, second = OFFSETS[i] + 4, OFFSETS[j] + 4
    dx = jnp.where(c == 0, first, second)
    dy = jnp.where(c == 0, second, first)
    return lax.rem(y + dy, NY), lax.rem(x + dx, NX)


def load_operands(place, pieces, weights, lane, width, tok, w, sems):
    copies = []
    for rel, d in enumerate(OFFSETS):
        yy = lax.rem(place[1] + (d + NY), NY)
        for other in range(2):
            core = 1 - place[2] if other else place[2]
            copies.append(
                pltpu.make_async_copy(
                    weights.at[:, core, rel, :, pl.ds(lane, width)],
                    w.at[:, yy, :, pl.ds(other * width, width)],
                    sems.at[16 + rel * 2 + other],
                )
            )
    for j in range(4):
        for i in range(4):
            array, index = (pieces[j], i) if j < 3 else (pieces[3 + i // 2], i % 2)
            yy, xx = place_of(place, i, j)
            copies.append(
                pltpu.make_async_copy(
                    array.at[index],
                    tok.at[
                        pl.ds(pl.multiple_of(yy * HALF, HALF), HALF),
                        pl.ds(pl.multiple_of(xx * (D // NX), D // NX), D // NX),
                    ],
                    sems.at[j * 4 + i],
                )
            )
    for copy in copies:
        copy.start()
    for copy in copies:
        copy.wait()


def silu(v):
    return v / (1.0 + jnp.exp(-v))


def project_side(place, *refs):
    pieces, weights = refs[:5], refs[5]
    bc_own, dt_own, bc_other, dt_other, tok, w, sems = refs[6:]
    load_operands(place, pieces, weights, CH, 128, tok, w, sems)
    for k in range(NY):
        at = slice(k * HALF, (k + 1) * HALF)
        acc = jnp.dot(tok[at, :], w[...].reshape(D, 256), preferred_element_type=F32)
        for bc, dt, lane in ((bc_own, dt_own, 0), (bc_other, dt_other, 128)):
            side = acc[:, lane : lane + 128].T
            bc[:, at] = side[:64].astype(BF)
            dt[:, at] = side[64:72]


def project_wide(place, *refs):
    pieces, weights = refs[:5], refs[5]
    own, other, tok, w, sems = refs[6:]
    load_operands(place, pieces, weights, 0, CH, tok, w, sems)
    for k in range(NY):
        at = slice(k * HALF, (k + 1) * HALF)
        acc = jnp.dot(tok[at, :], w[...].reshape(D, 2 * CH), preferred_element_type=F32)
        own[k] = acc[:, :CH].astype(BF)
        other[k] = acc[:, CH:].astype(BF)


def run_projection(kernel, place, pieces, weights, width, outs):
    return pl.pallas_call(
        kernel,
        out_shape=outs,
        in_specs=[SMEM] + [ANY] * 5 + [HBM],
        out_specs=[VMEM] * len(outs),
        scratch_shapes=[
            pltpu.VMEM((NY * HALF, D), BF),
            pltpu.VMEM((NZ, NY, 128, 2 * width), BF),
            pltpu.SemaphoreType.DMA((24,)),
        ],
        compiler_params=pltpu.CompilerParams(vmem_limit_bytes=20 * MIB),
        cost_estimate=SMALL,
    )(place, *pieces, weights)


def local_call(kernel, outs, *args, scratch=(), limit=20):
    return pl.pallas_call(
        kernel,
        out_shape=outs,
        in_specs=[SMEM] + [VMEM] * (len(args) - 1),
        out_specs=[VMEM] * len(outs),
        scratch_shapes=list(scratch),
        compiler_params=pltpu.CompilerParams(vmem_limit_bytes=limit * MIB),
        cost_estimate=SMALL,
    )(*args)


def half_start(place, k, other):
    half = 1 - place[2] if other else place[2]
    return pl.multiple_of(k * ROWS + half * HALF, HALF)


def conv_and_rates(
    place, own, other, halo_1, halo_2, taps, dt_own, dt_other, bias, a_log, *rest
):
    out_ref, run_ref, step_ref, full, raw_full = rest
    full[:16, :] = (halo_1[...] + halo_2[...]).astype(F32)
    for k in range(NY):
        full[pl.ds(half_start(place, k, False) + 16, HALF), :] = own[k].astype(F32)
        full[pl.ds(half_start(place, k, True) + 16, HALF), :] = other[k].astype(F32)
        at = slice(k * HALF, (k + 1) * HALF)
        raw_full[:, pl.ds(half_start(place, k, False), HALF)] = dt_own[:, at]
        raw_full[:, pl.ds(half_start(place, k, True), HALF)] = dt_other[:, at]
    for block in range(NB):
        total = taps[3:4, :] * full[block * Q + 16 : block * Q + 16 + Q, :]
        for back in (1, 2, 3):
            start = block * Q + 16 - back
            total = total + taps[3 - back : 4 - back, :] * full[start : start + Q, :]
        out_ref[block * Q : (block + 1) * Q, :] = silu(total).astype(BF)
    lane = lax.broadcasted_iota(jnp.int32, (8, Q), 1)
    factor = -jnp.exp(a_log[...])
    for block in range(NB):
        at = slice(block * Q, (block + 1) * Q)
        raw = raw_full[:, at] + bias[...]
        step = jnp.maximum(raw, 0.0) + jnp.log1p(jnp.exp(-jnp.abs(raw)))
        running = step * factor
        for distance in (1, 2, 4, 8, 16, 32, 64):
            running = running + jnp.where(lane < distance, 0.0, pltpu.roll(running, distance, 1))
        run_ref[:, at] = running
        step_ref[:, at] = step


def states(place, x_ref, run_ref, step_ref, taps, *rest):
    parts, (bc_ref, local_ref, end_ref, full) = rest[:4], rest[4:]
    for part, d in zip(parts, OFFSETS):
        yy = lax.rem(place[1] + (d + NY), NY)
        row = pl.ds(pl.multiple_of(yy * 64, 64), 64)
        full[row, :Q] = part[:, :Q].astype(F32)
        for other in range(2):
            for k in range(NY):
                start = pl.multiple_of(half_start(place, k, other) + Q, Q)
                source = Q + (other * NY + k) * HALF
                full[row, pl.ds(start, HALF)] = part[:, source : source + HALF].astype(F32)
    lane = lax.broadcasted_iota(jnp.int32, (2 * N, Q), 1)
    state = [jnp.zeros((N, PS), F32) for _ in range(HD)]
    total_rate = jnp.zeros((8, Q), F32)
    for block in range(NB):
        at = slice(block * Q, (block + 1) * Q)
        before, now = full[:, at], full[:, (block + 1) * Q : (block + 2) * Q]
        total = taps[:, 3:4] * now
        for back in (1, 2, 3):
            moved = jnp.where(
                lane < back, pltpu.roll(before, back, 1), pltpu.roll(now, back, 1)
            )
            total = total + taps[:, 3 - back : 4 - back] * moved
        bc = silu(total).astype(BF)
        bc_ref[:, at] = bc
        b = bc[:N, :].astype(F32)
        running, step = run_ref[:, at], step_ref[:, at]
        last = running[:, Q - 1 : Q]
        weight = jnp.exp(last - running) * step
        decay = jnp.exp(last)
        for h in range(HD):
            local_ref[block, :, h * PS : (h + 1) * PS] = state[h].astype(BF)
            scaled = (b * weight[h : h + 1, :]).astype(BF)
            increment = jnp.dot(
                scaled, x_ref[at, h * PS : (h + 1) * PS], preferred_element_type=F32
            )
            state[h] = decay[h : h + 1, :] * state[h] + increment
        total_rate = total_rate + last
    for h in range(HD):
        end_ref[:N, h * PS : (h + 1) * PS] = state[h].astype(BF)
    whole = jnp.exp(total_rate)
    high = whole.astype(BF)
    low = (whole - high.astype(F32)).astype(BF)
    row = jnp.concatenate([high, low], axis=0)
    end_ref[N:, :] = jnp.concatenate([row, row], axis=1)


def within(place, x_ref, bc_ref, run_ref, step_ref, skip, y_ref):
    below = lax.broadcasted_iota(jnp.int32, (Q, Q), 0) >= lax.broadcasted_iota(
        jnp.int32, (Q, Q), 1
    )
    for block in range(NB):
        at = slice(block * Q, (block + 1) * Q)
        running, step = run_ref[:, at], step_ref[:, at]
        columns = running.T
        scores = lax.dot_general(
            bc_ref[N:, at], bc_ref[:N, at], (((0,), (0,)), ((), ())), preferred_element_type=F32
        )
        for h in range(HD):
            spread = jnp.where(below, columns[:, h : h + 1] - running[h : h + 1, :], -1e30)
            mixing = (jnp.exp(spread) * step[h : h + 1, :] * scores).astype(BF)
            value = x_ref[at, h * PS : (h + 1) * PS]
            y = jnp.dot(mixing, value, preferred_element_type=F32)
            y_ref[at, h * PS : (h + 1) * PS] = (
                y + skip[:, h * PS : (h + 1) * PS] * value.astype(F32)
            )


def per_head(columns):
    return jnp.concatenate(
        [jnp.broadcast_to(columns[:, h : h + 1], (columns.shape[0], PS)) for h in range(HD)],
        axis=1,
    )


def over_channels(rows):
    return jnp.concatenate([rows[h : h + 1, :PS] for h in range(HD)], axis=1)


def chained(arrived):
    state = jnp.zeros((N, CH), F32)
    weight = jnp.ones((1, CH), F32)
    for ref in arrived:
        state = state + weight * ref[:N, :].astype(F32)
        decay = ref[N : N + 8, :].astype(F32) + ref[N + 8 : N + 16, :].astype(F32)
        weight = weight * over_channels(decay[:, :128])
    return state, weight


def combine(place, end, first, second, third, out_ref):
    state, _ = chained((first, second, third))
    decay = end[N : N + 8, :].astype(F32) + end[N + 8 : N + 16, :].astype(F32)
    out_ref[...] = (end[:N, :].astype(F32) + over_channels(decay[:, :128]) * state).astype(BF)


def carry(place, bc_ref, run_ref, local_ref, y_ref, z_own, z_other, *rest):
    arrived, outs, (z_full, sorted_rows) = rest[:4], rest[4:12], rest[12:]
    for k in range(NY):
        z_full[pl.ds(half_start(place, k, False), HALF), :] = z_own[k]
        z_full[pl.ds(half_start(place, k, True), HALF), :] = z_other[k]
    state, weight = chained(arrived[:3])
    state = state + weight * arrived[3][...].astype(F32)
    before = jnp.ones((1, CH), F32)
    for block in range(NB):
        at = slice(block * Q, (block + 1) * Q)
        running = run_ref[:, at]
        full = (local_ref[block].astype(F32) + before * state).astype(BF)
        carried = lax.dot_general(
            bc_ref[N:, at], full, (((0,), (0,)), ((), ())), preferred_element_type=F32
        )
        grown = jnp.exp(running)
        y = y_ref[at, :] + per_head(grown.T) * carried
        gate = silu(z_full[at, :].astype(F32))
        yy, half, part = block // 4, block // 2 % 2, block % 2
        core = jnp.where(place[2] == half, 0, 1)
        rel = lax.rem(yy + NY - place[1], NY)
        sorted_rows[core, rel, part * Q : (part + 1) * Q, :] = (y * gate).astype(BF)
        last = jnp.broadcast_to(grown[:, Q - 1 : Q], (8, Q))
        before = before * over_channels(last)
    for core in range(2):
        for rel in range(NY):
            outs[core * NY + rel][...] = sorted_rows[core, rel]


def normed(place, gain_own, gain_other, parts, hidden):
    for group, gain in enumerate((gain_own, gain_other)):
        refs = parts[group * NY : group * NY + NY]
        total = jnp.zeros((HALF, 1), F32)
        for ref in refs:
            value = ref[...].astype(F32)
            total = total + jnp.sum(value * value, axis=1, keepdims=True)
        scale = lax.rsqrt(total / (NY * CH) + EPSILON)
        for ref, d in zip(refs, OFFSETS):
            yy = lax.rem(place[1] + (d + NY), NY)
            lanes = pl.ds(pl.multiple_of(yy * CH, CH), CH)
            hidden[group, :, lanes] = (ref[...].astype(F32) * scale * gain[:, lanes]).astype(BF)


def project_out_first(place, gain_own, gain_other, w_own, w_other, *rest):
    parts, (hidden, out_ref) = rest[:8], rest[8:]

    @pl.when(pl.program_id(0) == 0)
    def _():
        normed(place, gain_own, gain_other, parts, hidden)

    acc = jnp.dot(hidden[0], w_own[...], preferred_element_type=F32)
    acc = acc + jnp.dot(hidden[1], w_other[...], preferred_element_type=F32)
    out_ref[...] = acc.astype(BF)


def project_out(place, hidden, w_own, w_other, *outs):
    acc = jnp.dot(hidden[0], w_own[...], preferred_element_type=F32)
    acc = acc + jnp.dot(hidden[1], w_other[...], preferred_element_type=F32)
    outs[0][...] = acc.astype(outs[0].dtype)


def out_call(kernel, place, distance, kind, extra, w_own, w_other, more, with_hidden):
    tile = 512
    count = D // NX // tile
    block = lambda i, p: (0, lax.rem(p[0] + (distance + NX), NX) * count + i)
    whole = lambda v: pl.BlockSpec(v.shape, lambda i, p: (0,) * v.ndim)
    outs = [SHAPE((HALF, D // NX), kind)]
    out_specs = [pl.BlockSpec((HALF, tile), lambda i, p: (0, i))]
    if with_hidden:
        outs = [SHAPE((NC, HALF, NY * CH), BF)] + outs
        out_specs = [pl.BlockSpec((NC, HALF, NY * CH), lambda i, p: (0, 0, 0))] + out_specs
    w_spec = pl.BlockSpec((NY * CH, tile), block)
    return pl.pallas_call(
        kernel,
        out_shape=outs,
        grid_spec=pltpu.PrefetchScalarGridSpec(
            num_scalar_prefetch=1,
            grid=(count,),
            in_specs=[whole(v) for v in extra] + [w_spec] * 2 + [whole(v) for v in more],
            out_specs=out_specs,
        ),
        compiler_params=pltpu.CompilerParams(vmem_limit_bytes=20 * MIB),
        cost_estimate=SMALL,
    )(place, *extra, w_own, w_other, *more)


def finish(place, own, first, second, third, keep, give):
    lanes = lambda core: pl.ds(pl.multiple_of(core * 512, 512), 512)
    for core, ref in ((place[2], keep), (1 - place[2], give)):
        at = lanes(core)
        total = own[:, at] + first[:, at].astype(F32)
        total = total + second[:, at].astype(F32) + third[:, at].astype(F32)
        ref[...] = total.astype(BF)


def on_device(tokens, w_zx, w_bc, w_dt, conv_x, conv_bc, dt_bias, a_log, d_skip, norm_gain, w_out):
    y, c = lax.axis_index("y"), lax.axis_index("c")
    place = jnp.stack([lax.axis_index("x"), y, c]).astype(jnp.int32)
    rows = w_zx.shape[0]

    def quarter(value, distance, width, dim=1):
        start = lax.rem(y + (distance + NY), NY) * width
        return lax.dynamic_slice_in_dim(value, start, width, dim)

    def for_y(distance):
        zero = jnp.zeros((rows, W1 - CH - 64 - HD), BF)
        return jnp.concatenate(
            [
                quarter(w_zx[:, 1], distance, CH),
                quarter(w_bc.reshape(rows, -1), distance, 64),
                quarter(w_dt, distance, HD),
                zero,
            ],
            axis=1,
        )

    mine = half_rows(tokens, c)
    gate = lambda d: quarter(w_zx[:, 0], d, CH)
    pieces, first, second = gather_tokens(
        mine, [for_y(d) for d in range(NY)], [gate(d) for d in range(NY)]
    )
    weights_1 = lax.all_gather(jnp.concatenate(first), ("z", "c"), axis=0, tiled=True)
    weights_1 = weights_1.reshape(NZ, NC, NY, rows, W1)
    weights_2 = lax.all_gather(jnp.concatenate(second), ("z", "c"), axis=0, tiled=True)
    weights_2 = weights_2.reshape(NZ, NC, NY, rows, CH)

    taps_x = quarter(conv_x, 0, CH).astype(F32)
    taps_bc = conv_bc.reshape(4, -1).T.astype(F32)
    column = lambda v: jnp.pad(quarter(v, 0, HD, 0), (0, 8 - HD)).reshape(8, 1)
    skip = jnp.repeat(quarter(d_skip, 0, HD, 0), PS).reshape(1, CH)
    gain = norm_gain.astype(F32).reshape(1, -1)

    line, w_late, gain_late = lax.optimization_barrier((pieces[0], w_out, gain))
    pieces[0] = line
    w_other, gain_other = sibling(w_late), sibling(gain_late)
    pieces, w_other, gain_other = lax.optimization_barrier((pieces, w_other, gain_other))

    bc_own, dt_own, bc_give, dt_give = run_projection(
        project_side,
        place,
        pieces,
        weights_1,
        128,
        [SHAPE((64, NY * HALF), BF), SHAPE((8, NY * HALF), F32)] * 2,
    )
    bc_got = sibling(bc_give)
    halo = routed(
        bc_own[:, -Q:], lambda z, y, x, c: (z + 1, y, x, 1) if z + 1 < NZ and c == 1 else None
    ) + routed(
        bc_give[:, -Q:], lambda z, y, x, c: (z + 1, y, x, 0) if z + 1 < NZ and c == 1 else None
    )
    bc = jnp.concatenate([halo, bc_own, bc_got], axis=1)
    place_2, dt_own, dt_give, bc = lax.optimization_barrier((place, dt_own, dt_give, bc))
    dt_got = sibling(dt_give)
    bc_parts = [bc] + [shifted(bc, "y", d) for d in (1, -1, 2)]
    wide = [SHAPE((NY, HALF, CH), BF)] * 2
    x_own, x_give = run_projection(project_wide, place_2, pieces, weights_1, CH, wide)
    x_got = sibling(x_give)
    halo_own = routed(
        x_own[NY - 1, HALF - 16 :],
        lambda z, y, x, c: (z + 1, y, x, 1) if z + 1 < NZ and c == 1 else None,
    )
    halo_give = routed(
        x_give[NY - 1, HALF - 16 :],
        lambda z, y, x, c: (z + 1, y, x, 0) if z + 1 < NZ and c == 1 else None,
    )
    x_conv, running, step = local_call(
        conv_and_rates,
        [SHAPE((T, CH), BF), SHAPE((8, T), F32), SHAPE((8, T), F32)],
        place,
        x_own,
        x_got,
        halo_own,
        halo_give,
        taps_x,
        dt_own,
        dt_got,
        column(dt_bias),
        column(a_log),
        scratch=[pltpu.VMEM((T + 16, CH), F32), pltpu.VMEM((8, T), F32)],
    )
    bc_conv, local, end = local_call(
        states,
        [SHAPE((2 * N, T), BF), SHAPE((NB, N, CH), BF), SHAPE((N + 16, CH), BF)],
        place,
        x_conv,
        running,
        step,
        taps_bc,
        *bc_parts,
        scratch=[pltpu.VMEM((2 * N, T + Q), F32)],
    )
    near = [lax.ppermute(end, "z", [(i, i + d) for i in range(NZ - d)]) for d in (1, 2, 3)]
    (y_within,) = local_call(
        within, [SHAPE((T, CH), F32)], place, x_conv, bc_conv, running, step, skip
    )
    near, y_within = lax.optimization_barrier((near, y_within))
    (window,) = local_call(combine, [SHAPE((N, CH), BF)], place, end, *near)
    place_4, window = lax.optimization_barrier((place_2, window))
    far = lax.ppermute(window, "z", [(i, i + 4) for i in range(NZ - 4)])
    z_own, z_give = run_projection(project_wide, place_4, pieces, weights_2, CH, wide)
    z_got = sibling(z_give)
    sorted_rows = local_call(
        carry,
        [SHAPE((HALF, CH), BF)] * 8,
        place,
        bc_conv,
        running,
        local,
        y_within,
        z_own,
        z_got,
        *near,
        far,
        scratch=[pltpu.VMEM((T, CH), BF), pltpu.VMEM((NC, NY, HALF, CH), BF)],
    )
    keep, give = sorted_rows[:NY], [sibling(v) for v in sorted_rows[NY:]]

    parts = over_y(keep) + over_y(give)
    hidden, far = out_call(
        project_out_first, place, 2, BF, [gain, gain_other], w_out, w_other, parts, True
    )
    rest = lambda d, kind: out_call(
        project_out, place, d, kind, [hidden], w_out, w_other, [], False
    )[0]
    arrived_far = shifted(far, "x", 2)
    arrived_left = shifted(rest(1, BF), "x", 1)
    arrived_right = shifted(rest(-1, BF), "x", -1)
    stay, leave = local_call(
        finish,
        [SHAPE((HALF, 512), BF)] * 2,
        place,
        rest(0, F32),
        arrived_left,
        arrived_right,
        arrived_far,
    )
    got = sibling(leave)
    return jnp.where(c == 0, jnp.concatenate([stay, got]), jnp.concatenate([got, stay]))


def solution(mesh):
    fine = Mesh(mesh.devices.reshape(NZ, NY, NX, NC), ("z", "y", "x", "c"))
    seq, head = ("z", "y"), ("x", "c")
    return jax.shard_map(
        on_device,
        mesh=fine,
        in_specs=(
            P(seq, head),
            P(seq, None, head),
            P(seq, None, head),
            P(seq, head),
            P(None, head),
            P(None, None, head),
            P(head),
            P(head),
            P(head),
            P(head),
            P(head, None),
        ),
        out_specs=P(seq, head),
        check_vma=False,
    )
```

```python
import jax
import jax.numpy as jnp
from jax import lax
from jax.experimental import pallas as pl
from jax.experimental.pallas import tpu as pltpu
from jax.sharding import Mesh, PartitionSpec as P

EPSILON = 1e-05
BF = jnp.bfloat16
F32 = jnp.float32
MIB = 1024 * 1024

NZ, NY, NX, NC = 8, 4, 4, 2
ROWS = 512
HALF = ROWS // 2
D = 4096
T = ROWS * NY
CH = 256
HD = 4
PS = 64
N = 128
Q = 128
NB = T // Q
W1 = 384
OFFSETS = (0, -1, 1, 2)
ALL = ("z", "y", "x", "c")
VMEM = pl.BlockSpec(memory_space=pltpu.VMEM)
SMEM = pl.BlockSpec(memory_space=pltpu.SMEM)
ANY = pl.BlockSpec(memory_space=pl.ANY)
HBM = pl.BlockSpec(memory_space=pltpu.HBM)
SHAPE = jax.ShapeDtypeStruct
SMALL = pl.CostEstimate(flops=1000, bytes_accessed=1000, transcendentals=0)


def shifted(value, axis, distance):
    n = lax.axis_size(axis)
    return lax.ppermute(value, axis, [(i, (i + distance) % n) for i in range(n)])


def sibling(value):
    return lax.ppermute(value, "c", [(0, 1), (1, 0)])


def routed(value, target):
    pairs = []
    for source in range(NZ * NY * NX * NC):
        rest, c = divmod(source, NC)
        rest, x = divmod(rest, NX)
        z, y = divmod(rest, NY)
        goal = target(z, y, x, c)
        if goal is not None:
            z, y, x, c = goal
            pairs.append((source, ((z * NY + y) * NX + x) * NC + c))
    return lax.ppermute(value, ALL, pairs)


def crossed(value, along_x, distance):
    def target(z, y, x, c):
        if c == along_x:
            return z, y, (x + distance) % NX, c
        return z, (y + distance) % NY, x, c

    return routed(value, target)


def over_y(v):
    return [v[0], shifted(v[1], "y", 1), shifted(v[3], "y", -1), shifted(v[2], "y", 2)]


def half_rows(tokens, c):
    early, late = tokens[:HALF], tokens[HALF:]
    got = sibling(jnp.where(c == 0, late, early))
    return jnp.where(
        c == 0,
        jnp.concatenate([early, got], axis=1),
        jnp.concatenate([got, late], axis=1),
    )


def gather_tokens(mine, first, second):
    mine, first = lax.optimization_barrier((mine, first))
    right, left = crossed(mine, 0, 1), crossed(mine, 0, -1)
    first = over_y(first)
    right, left, first, second = lax.optimization_barrier((right, left, first, second))
    middle = HALF // 2
    opposite = [crossed(right[:middle], 0, 1), crossed(left[middle:], 0, -1)]
    second = over_y(second)
    near = jnp.stack([mine, right])
    away = jnp.stack([left, jnp.concatenate(opposite)])
    near, away, second = lax.optimization_barrier((near, away, second))
    near_r, away_l = crossed(near, 1, 1), crossed(away, 1, -1)
    near_l, away_r = crossed(near, 1, -1), crossed(away, 1, 1)
    near_2, away_2 = crossed(near_r, 1, 1), crossed(away_l, 1, -1)
    return [near, away, near_r, away_r, near_l, away_l, near_2, away_2], first, second


def place_of(place, i, j):
    x, y, c = place[0], place[1], place[2]
    first, second = OFFSETS[i] + 4, OFFSETS[j] + 4
    dx = jnp.where(c == 0, first, second)
    dy = jnp.where(c == 0, second, first)
    return lax.rem(y + dy, NY), lax.rem(x + dx, NX)


def load_operands(place, pieces, weights, columns, tok, w, sems):
    x, y, c = place[0], place[1], place[2]
    for rel, d in enumerate(OFFSETS):
        yy = lax.rem(y + (d + NY), NY)
        for number, (core, lane, width, to) in enumerate(columns):
            pltpu.make_async_copy(
                weights.at[:, 1 - c if core else c, rel, :, pl.ds(lane, width)],
                w.at[:, yy, :, pl.ds(to, width)],
                sems.at[4 + rel * len(columns) + number],
            ).start()

    def fetch(i, j, chunk):
        yy, xx = place_of(place, i, j)
        pltpu.make_async_copy(
            pieces[j * 2 + i // 2].at[i % 2],
            tok.at[
                pl.ds(pl.multiple_of(yy * HALF, HALF), HALF),
                pl.ds(pl.multiple_of(xx * (D // NX), D // NX), D // NX),
            ],
            sems.at[chunk],
        ).start()

    for core in range(2):

        @pl.when(c == core)
        def _():
            for chunk in range(4):
                for k in range(4):
                    i, j = (chunk, k) if core else (k, chunk)
                    fetch(i, j, chunk)


def wait_weights(weights, columns, w, sems):
    for rel in range(NY):
        for number, (core, lane, width, to) in enumerate(columns):
            pltpu.make_async_copy(
                weights.at[:, 0, rel, :, pl.ds(lane, width)],
                w.at[:, rel, :, pl.ds(to, width)],
                sems.at[4 + rel * len(columns) + number],
            ).wait()


def chunk_rows(place, chunk, tok, sems):
    yy = lax.rem(place[1] + (OFFSETS[chunk] + NY), NY)
    rows = tok.at[pl.ds(pl.multiple_of(yy * HALF, HALF), HALF), :]
    pltpu.make_async_copy(rows, rows, sems.at[chunk]).wait()
    return yy, rows[...]


def silu(v):
    return v / (1.0 + jnp.exp(-v))


FIRST = [(0, 0, CH, 0), (1, 0, CH, CH), (0, CH, 128, 2 * CH), (1, CH, 128, 2 * CH + 128)]
SECOND = [(0, 0, CH, 0), (1, 0, CH, CH)]


def project_first(place, *refs):
    pieces, weights = refs[:8], refs[8]
    outs, (tok, w, sems) = refs[9:17], refs[17:]
    load_operands(place, pieces, weights, FIRST, tok, w, sems)
    wait_weights(weights, FIRST, w, sems)
    for chunk in range(NY):
        yy, rows = chunk_rows(place, chunk, tok, sems)
        at = pl.ds(pl.multiple_of(yy * HALF, HALF), HALF)
        acc = jnp.dot(rows, w[...].reshape(D, 2 * CH + 256), preferred_element_type=F32)
        for core in range(2):
            x_ref, bc_ref, dt_ref, tail = outs[4 * core : 4 * core + 4]
            x = acc[:, core * CH : (core + 1) * CH].astype(BF)
            start = 2 * CH + 128 * core
            side = acc[:, start : start + 128].T
            bc = side[:64].astype(BF)
            x_ref[yy] = x
            bc_ref[:, at] = bc
            dt_ref[:, at] = side[64:72]

            @pl.when(yy == NY - 1)
            def _():
                tail[:64, :] = bc[:, HALF - Q :]
                tail[64:80, :] = x[HALF - 16 :, :Q]
                tail[80:, :] = x[HALF - 16 :, Q:]


def project_second(place, *refs):
    pieces, weights = refs[:8], refs[8]
    own, other, tok, w, sems = refs[9:]
    load_operands(place, pieces, weights, SECOND, tok, w, sems)
    wait_weights(weights, SECOND, w, sems)
    for chunk in range(NY):
        yy, rows = chunk_rows(place, chunk, tok, sems)
        acc = jnp.dot(rows, w[...].reshape(D, 2 * CH), preferred_element_type=F32)
        own[yy] = acc[:, :CH].astype(BF)
        other[yy] = acc[:, CH:].astype(BF)


def run_projection(kernel, place, pieces, weights, width, outs):
    return pl.pallas_call(
        kernel,
        out_shape=outs,
        in_specs=[SMEM] + [ANY] * 8 + [HBM],
        out_specs=[VMEM] * len(outs),
        scratch_shapes=[
            pltpu.VMEM((NY * HALF, D), BF),
            pltpu.VMEM((NZ, NY, 128, width), BF),
            pltpu.SemaphoreType.DMA((20,)),
        ],
        compiler_params=pltpu.CompilerParams(vmem_limit_bytes=52 * MIB),
        cost_estimate=SMALL,
    )(place, *pieces, weights)


def local_call(kernel, outs, *args, scratch=(), limit=20):
    return pl.pallas_call(
        kernel,
        out_shape=outs,
        in_specs=[SMEM] + [VMEM] * (len(args) - 1),
        out_specs=[VMEM] * len(outs),
        scratch_shapes=list(scratch),
        compiler_params=pltpu.CompilerParams(vmem_limit_bytes=limit * MIB),
        cost_estimate=SMALL,
    )(*args)


def half_start(place, k, other):
    half = 1 - place[2] if other else place[2]
    return pl.multiple_of(k * ROWS + half * HALF, HALF)


def conv_and_rates(
    place, own, other, halo_1, halo_2, taps, dt_own, dt_other, bias, a_log, *rest
):
    out_ref, run_ref, step_ref, full, raw_full = rest
    halo = (halo_1[64:, :] + halo_2[64:, :]).astype(F32)
    full[:16, :Q] = halo[:16]
    full[:16, Q:] = halo[16:]
    for k in range(NY):
        full[pl.ds(half_start(place, k, False) + 16, HALF), :] = own[k].astype(F32)
        full[pl.ds(half_start(place, k, True) + 16, HALF), :] = other[k].astype(F32)
        at = slice(k * HALF, (k + 1) * HALF)
        raw_full[:, pl.ds(half_start(place, k, False), HALF)] = dt_own[:, at]
        raw_full[:, pl.ds(half_start(place, k, True), HALF)] = dt_other[:, at]
    for block in range(NB):
        total = taps[3:4, :] * full[block * Q + 16 : block * Q + 16 + Q, :]
        for back in (1, 2, 3):
            start = block * Q + 16 - back
            total = total + taps[3 - back : 4 - back, :] * full[start : start + Q, :]
        out_ref[block * Q : (block + 1) * Q, :] = silu(total).astype(BF)
    lane = lax.broadcasted_iota(jnp.int32, (8, Q), 1)
    factor = -jnp.exp(a_log[...])
    for block in range(NB):
        at = slice(block * Q, (block + 1) * Q)
        raw = raw_full[:, at] + bias[...]
        step = jnp.maximum(raw, 0.0) + jnp.log1p(jnp.exp(-jnp.abs(raw)))
        running = step * factor
        for distance in (1, 2, 4, 8, 16, 32, 64):
            running = running + jnp.where(lane < distance, 0.0, pltpu.roll(running, distance, 1))
        run_ref[:, at] = running
        step_ref[:, at] = step


def convolve_side(place, own, other, halo_1, halo_2, taps, out_ref, full):
    full[:, :Q] = (halo_1[:64, :] + halo_2[:64, :]).astype(F32)
    for k in range(NY):
        at = slice(k * HALF, (k + 1) * HALF)
        full[:, pl.ds(pl.multiple_of(half_start(place, k, False) + Q, Q), HALF)] = own[
            :, at
        ].astype(F32)
        full[:, pl.ds(pl.multiple_of(half_start(place, k, True) + Q, Q), HALF)] = other[
            :, at
        ].astype(F32)
    lane = lax.broadcasted_iota(jnp.int32, (64, Q), 1)
    before = [pltpu.roll(full[:, :Q], back, 1) for back in (1, 2, 3)]
    for block in range(NB):
        now = full[:, (block + 1) * Q : (block + 2) * Q]
        turned = [pltpu.roll(now, back, 1) for back in (1, 2, 3)]
        total = taps[:, 3:4] * now
        for back in (1, 2, 3):
            moved = jnp.where(lane < back, before[back - 1], turned[back - 1])
            total = total + taps[:, 3 - back : 4 - back] * moved
        out_ref[:, block * Q : (block + 1) * Q] = silu(total).astype(BF)
        before = turned


def states(place, x_ref, run_ref, step_ref, *rest):
    parts, (bc_ref, local_ref, end_ref) = rest[:4], rest[4:]
    for part, d in zip(parts, OFFSETS):
        yy = lax.rem(place[1] + (d + NY), NY)
        bc_ref[pl.ds(pl.multiple_of(yy * 64, 64), 64), :] = part[...]
    state = [jnp.zeros((N, PS), F32) for _ in range(HD)]
    total_rate = jnp.zeros((8, Q), F32)
    for block in range(NB):
        at = slice(block * Q, (block + 1) * Q)
        b = bc_ref[:N, at].astype(F32)
        running, step = run_ref[:, at], step_ref[:, at]
        last = running[:, Q - 1 : Q]
        weight = jnp.exp(last - running) * step
        decay = jnp.exp(last)
        for h in range(HD):
            local_ref[block, :, h * PS : (h + 1) * PS] = state[h].astype(BF)
            scaled = (b * weight[h : h + 1, :]).astype(BF)
            increment = jnp.dot(
                scaled, x_ref[at, h * PS : (h + 1) * PS], preferred_element_type=F32
            )
            state[h] = decay[h : h + 1, :] * state[h] + increment
        total_rate = total_rate + last
    for h in range(HD):
        end_ref[:N, h * PS : (h + 1) * PS] = state[h].astype(BF)
    whole = jnp.exp(total_rate)
    high = whole.astype(BF)
    low = (whole - high.astype(F32)).astype(BF)
    row = jnp.concatenate([high, low], axis=0)
    end_ref[N:, :] = jnp.concatenate([row, row], axis=1)


def within(place, x_ref, bc_ref, run_ref, step_ref, skip, y_ref):
    below = lax.broadcasted_iota(jnp.int32, (Q, Q), 0) >= lax.broadcasted_iota(
        jnp.int32, (Q, Q), 1
    )
    for block in range(NB):
        at = slice(block * Q, (block + 1) * Q)
        running, step = run_ref[:, at], step_ref[:, at]
        columns = running.T
        scores = lax.dot_general(
            bc_ref[N:, at], bc_ref[:N, at], (((0,), (0,)), ((), ())), preferred_element_type=F32
        )
        for h in range(HD):
            spread = jnp.where(below, columns[:, h : h + 1] - running[h : h + 1, :], -1e30)
            mixing = (jnp.exp(spread) * step[h : h + 1, :] * scores).astype(BF)
            value = x_ref[at, h * PS : (h + 1) * PS]
            y = jnp.dot(mixing, value, preferred_element_type=F32)
            y_ref[at, h * PS : (h + 1) * PS] = (
                y + skip[:, h * PS : (h + 1) * PS] * value.astype(F32)
            )


def per_head(columns):
    return jnp.concatenate(
        [jnp.broadcast_to(columns[:, h : h + 1], (columns.shape[0], PS)) for h in range(HD)],
        axis=1,
    )


def over_channels(rows):
    return jnp.concatenate([rows[h : h + 1, :PS] for h in range(HD)], axis=1)


def carry(place, bc_ref, run_ref, local_ref, y_ref, z_own, z_other, *rest):
    arrived, outs, (z_full, sorted_rows) = rest[0], rest[1:9], rest[9:]
    for k in range(NY):
        z_full[pl.ds(half_start(place, k, False), HALF), :] = z_own[k]
        z_full[pl.ds(half_start(place, k, True), HALF), :] = z_other[k]
    state = jnp.zeros((N, CH), F32)
    for z in range(NZ - 1):
        decay = arrived[z, N : N + 8, :Q].astype(F32) + arrived[z, N + 8 :, :Q].astype(F32)
        grown = over_channels(decay) * state + arrived[z, :N, :].astype(F32)
        state = jnp.where(place[3] > z, grown, state)
    before = jnp.ones((1, CH), F32)
    for block in range(NB):
        at = slice(block * Q, (block + 1) * Q)
        running = run_ref[:, at]
        full = (local_ref[block].astype(F32) + before * state).astype(BF)
        carried = lax.dot_general(
            bc_ref[N:, at], full, (((0,), (0,)), ((), ())), preferred_element_type=F32
        )
        grown = jnp.exp(running)
        y = y_ref[at, :] + per_head(grown.T) * carried
        gate = silu(z_full[at, :].astype(F32))
        yy, half, part = block // 4, block // 2 % 2, block % 2
        core = jnp.where(place[2] == half, 0, 1)
        rel = lax.rem(yy + NY - place[1], NY)
        sorted_rows[core, rel, part * Q : (part + 1) * Q, :] = (y * gate).astype(BF)
        last = jnp.broadcast_to(grown[:, Q - 1 : Q], (8, Q))
        before = before * over_channels(last)
    for core in range(2):
        for rel in range(NY):
            outs[core * NY + rel][...] = sorted_rows[core, rel]


def normed(place, gain_own, gain_other, parts, hidden):
    for group, gain in enumerate((gain_own, gain_other)):
        refs = parts[group * NY : group * NY + NY]
        total = jnp.zeros((HALF, 1), F32)
        for ref in refs:
            value = ref[...].astype(F32)
            total = total + jnp.sum(value * value, axis=1, keepdims=True)
        scale = lax.rsqrt(total / (NY * CH) + EPSILON)
        for ref, d in zip(refs, OFFSETS):
            yy = lax.rem(place[1] + (d + NY), NY)
            lanes = pl.ds(pl.multiple_of(yy * CH, CH), CH)
            hidden[group, :, lanes] = (ref[...].astype(F32) * scale * gain[:, lanes]).astype(BF)


def project_out(place, gain_own, gain_other, w_own, w_other, *rest):
    parts, outs, hidden = rest[:8], rest[8:12], rest[12]
    step = pl.program_id(0)

    @pl.when(step == 0)
    def _():
        normed(place, gain_own, gain_other, parts, hidden)

    acc = jnp.dot(hidden[0], w_own[...], preferred_element_type=F32)
    acc = acc + jnp.dot(hidden[1], w_other[...], preferred_element_type=F32)
    for k, ref in enumerate(outs):

        @pl.when(step // 2 == k)
        def _():
            ref[...] = acc.astype(ref.dtype)


def run_out(place, gain_own, gain_other, w_own, w_other, parts):
    tile = 512
    ahead = lambda i: jnp.where(i < 2, 2, jnp.where(i < 4, 1, jnp.where(i < 6, 3, 0)))
    block = lambda i, p: (0, lax.rem(p[0] + ahead(i), NX) * 2 + lax.rem(i, 2))
    whole = lambda v: pl.BlockSpec(v.shape, lambda i, p: (0,) * v.ndim)

    def result(k):
        return pl.BlockSpec((HALF, tile), lambda i, p: (0, jnp.where(i > 2 * k, 1, 0)))

    w_spec = pl.BlockSpec((NY * CH, tile), block)
    return pl.pallas_call(
        project_out,
        out_shape=[SHAPE((HALF, D // NX), kind) for kind in (BF, BF, BF, F32)],
        grid_spec=pltpu.PrefetchScalarGridSpec(
            num_scalar_prefetch=1,
            grid=(8,),
            in_specs=[whole(gain_own)] * 2 + [w_spec] * 2 + [whole(v) for v in parts],
            out_specs=[result(k) for k in range(4)],
            scratch_shapes=[pltpu.VMEM((NC, HALF, NY * CH), BF)],
        ),
        compiler_params=pltpu.CompilerParams(vmem_limit_bytes=20 * MIB),
        cost_estimate=SMALL,
    )(place, gain_own, gain_other, w_own, w_other, *parts)


def finish(place, own, first, second, third, keep, give):
    lanes = lambda core: pl.ds(pl.multiple_of(core * 512, 512), 512)
    for core, ref in ((place[2], keep), (1 - place[2], give)):
        at = lanes(core)
        total = own[:, at] + first[:, at].astype(F32)
        total = total + second[:, at].astype(F32) + third[:, at].astype(F32)
        ref[...] = total.astype(BF)


def on_device(tokens, w_zx, w_bc, w_dt, conv_x, conv_bc, dt_bias, a_log, d_skip, norm_gain, w_out):
    y, c = lax.axis_index("y"), lax.axis_index("c")
    place = jnp.stack([lax.axis_index("x"), y, c, lax.axis_index("z")]).astype(jnp.int32)
    rows = w_zx.shape[0]

    def quarter(value, distance, width, dim=1):
        start = lax.rem(y + (distance + NY), NY) * width
        return lax.dynamic_slice_in_dim(value, start, width, dim)

    def for_y(distance):
        zero = jnp.zeros((rows, W1 - CH - 64 - HD), BF)
        return jnp.concatenate(
            [
                quarter(w_zx[:, 1], distance, CH),
                quarter(w_bc.reshape(rows, -1), distance, 64),
                quarter(w_dt, distance, HD),
                zero,
            ],
            axis=1,
        )

    mine = half_rows(tokens, c)
    gate = lambda d: quarter(w_zx[:, 0], d, CH)
    pieces, first, second = gather_tokens(
        mine, [for_y(d) for d in range(NY)], [gate(d) for d in range(NY)]
    )
    weights_1 = lax.all_gather(jnp.concatenate(first), ("z", "c"), axis=0, tiled=True)
    weights_1 = weights_1.reshape(NZ, NC, NY, rows, W1)
    weights_2 = lax.all_gather(jnp.concatenate(second), ("z", "c"), axis=0, tiled=True)
    weights_2 = weights_2.reshape(NZ, NC, NY, rows, CH)

    taps_x = quarter(conv_x, 0, CH).astype(F32)
    taps_bc = quarter(conv_bc.reshape(4, -1), 0, 64).T.astype(F32)
    column = lambda v: jnp.pad(quarter(v, 0, HD, 0), (0, 8 - HD)).reshape(8, 1)
    skip = jnp.repeat(quarter(d_skip, 0, HD, 0), PS).reshape(1, CH)
    gain = norm_gain.astype(F32).reshape(1, -1)

    near, w_late, gain_late = lax.optimization_barrier((pieces[:2], w_out, gain))
    pieces[:2] = near
    w_other, gain_other = sibling(w_late), sibling(gain_late)
    pieces, w_other, gain_other = lax.optimization_barrier((pieces, w_other, gain_other))

    kinds = [
        SHAPE((NY, HALF, CH), BF),
        SHAPE((64, NY * HALF), BF),
        SHAPE((8, NY * HALF), F32),
        SHAPE((96, Q), BF),
    ]
    first_outs = run_projection(project_first, place, pieces, weights_1, 768, kinds * 2)
    x_own, bc_own, dt_own, tail_own = first_outs[:4]
    x_give, bc_give, dt_give, tail_give = first_outs[4:]
    bc_got = sibling(bc_give)
    halo_own = routed(
        tail_own, lambda z, y, x, c: (z + 1, y, x, 1) if z + 1 < NZ and c == 1 else None
    )
    halo_give = routed(
        tail_give, lambda z, y, x, c: (z + 1, y, x, 0) if z + 1 < NZ and c == 1 else None
    )
    x_got, dt_got = sibling(x_give), sibling(dt_give)
    (bc,) = local_call(
        convolve_side,
        [SHAPE((64, T), BF)],
        place,
        bc_own,
        bc_got,
        halo_own,
        halo_give,
        taps_bc,
        scratch=[pltpu.VMEM((64, T + Q), F32)],
    )
    bc_parts = [bc] + [shifted(bc, "y", d) for d in (1, -1, 2)]
    x_conv, running, step = local_call(
        conv_and_rates,
        [SHAPE((T, CH), BF), SHAPE((8, T), F32), SHAPE((8, T), F32)],
        place,
        x_own,
        x_got,
        halo_own,
        halo_give,
        taps_x,
        dt_own,
        dt_got,
        column(dt_bias),
        column(a_log),
        scratch=[pltpu.VMEM((T + 16, CH), F32), pltpu.VMEM((8, T), F32)],
    )
    bc_conv, local, end = local_call(
        states,
        [SHAPE((2 * N, T), BF), SHAPE((NB, N, CH), BF), SHAPE((N + 16, CH), BF)],
        place,
        x_conv,
        running,
        step,
        *bc_parts,
    )
    place_2, end = lax.optimization_barrier((place, end))
    ends = lax.all_gather(end, "z")
    z_own, z_give = run_projection(project_second, place_2, pieces, weights_2, 512, kinds[:1] * 2)
    z_got = sibling(z_give)
    (y_within,) = local_call(
        within, [SHAPE((T, CH), F32)], place, x_conv, bc_conv, running, step, skip
    )
    sorted_rows = local_call(
        carry,
        [SHAPE((HALF, CH), BF)] * 8,
        place,
        bc_conv,
        running,
        local,
        y_within,
        z_own,
        z_got,
        ends,
        scratch=[pltpu.VMEM((T, CH), BF), pltpu.VMEM((NC, NY, HALF, CH), BF)],
    )
    keep, give = sorted_rows[:NY], [sibling(v) for v in sorted_rows[NY:]]

    parts = over_y(keep) + over_y(give)
    far, ahead, behind, stays = run_out(place, gain, gain_other, w_out, w_other, parts)
    stay, leave = local_call(
        finish,
        [SHAPE((HALF, 512), BF)] * 2,
        place,
        stays,
        shifted(ahead, "x", 1),
        shifted(behind, "x", -1),
        shifted(far, "x", 2),
    )
    got = sibling(leave)
    return jnp.where(c == 0, jnp.concatenate([stay, got]), jnp.concatenate([got, stay]))


def solution(mesh):
    fine = Mesh(mesh.devices.reshape(NZ, NY, NX, NC), ("z", "y", "x", "c"))
    seq, head = ("z", "y"), ("x", "c")
    return jax.shard_map(
        on_device,
        mesh=fine,
        in_specs=(
            P(seq, head),
            P(seq, None, head),
            P(seq, None, head),
            P(seq, head),
            P(None, head),
            P(None, None, head),
            P(head),
            P(head),
            P(head),
            P(head),
            P(head, None),
        ),
        out_specs=P(seq, head),
        check_vma=False,
    )
```

```python
import jax
import jax.numpy as jnp
from jax import lax
from jax.experimental import pallas as pl
from jax.experimental.pallas import tpu as pltpu
from jax.sharding import Mesh, PartitionSpec as P

EPSILON = 1e-05
BF = jnp.bfloat16
F32 = jnp.float32
MIB = 1024 * 1024

NZ, NY, NX, NC = 8, 4, 4, 2
ROWS = 512
HALF = ROWS // 2
FEAT = 512
D = 4096
T = ROWS * NY
CH = 256
HD = 4
PS = 64
N = 128
Q = 128
NB = T // Q
W1 = 384
OFFSETS = (0, -1, 1, 2)
ALL = ("z", "y", "x", "c")
VMEM = pl.BlockSpec(memory_space=pltpu.VMEM)
SMEM = pl.BlockSpec(memory_space=pltpu.SMEM)
ANY = pl.BlockSpec(memory_space=pl.ANY)
HBM = pl.BlockSpec(memory_space=pltpu.HBM)
SHAPE = jax.ShapeDtypeStruct
SMALL = pl.CostEstimate(flops=1000, bytes_accessed=1000, transcendentals=0)


def shifted(value, axis, distance):
    n = lax.axis_size(axis)
    return lax.ppermute(value, axis, [(i, (i + distance) % n) for i in range(n)])


def sibling(value):
    return lax.ppermute(value, "c", [(0, 1), (1, 0)])


def routed(value, target):
    pairs = []
    for source in range(NZ * NY * NX * NC):
        rest, c = divmod(source, NC)
        rest, x = divmod(rest, NX)
        z, y = divmod(rest, NY)
        goal = target(z, y, x, c)
        if goal is not None:
            z, y, x, c = goal
            pairs.append((source, ((z * NY + y) * NX + x) * NC + c))
    return lax.ppermute(value, ALL, pairs)


def crossed(value, along_x, distance):
    def target(z, y, x, c):
        if c == along_x:
            return z, y, (x + distance) % NX, c
        return z, (y + distance) % NY, x, c

    return routed(value, target)


def over_y(v):
    return [v[0], shifted(v[1], "y", 1), shifted(v[3], "y", -1), shifted(v[2], "y", 2)]


def half_rows(tokens, c):
    early, late = tokens[:HALF], tokens[HALF:]
    got = sibling(jnp.where(c == 0, late, early))
    return jnp.where(
        c == 0,
        jnp.concatenate([early, got], axis=1),
        jnp.concatenate([got, late], axis=1),
    )


def gather_tokens(mine, first, second):
    mine, first = lax.optimization_barrier((mine, first))
    right, left = crossed(mine, 0, 1), crossed(mine, 0, -1)
    first = over_y(first)
    right, left, first, second = lax.optimization_barrier((right, left, first, second))
    middle = HALF // 2
    opposite = [crossed(right[:middle], 0, 1), crossed(left[middle:], 0, -1)]
    second = over_y(second)
    near = jnp.stack([mine, right])
    away = jnp.stack([left, jnp.concatenate(opposite)])
    near, away, second = lax.optimization_barrier((near, away, second))
    near_r, away_l = crossed(near, 1, 1), crossed(away, 1, -1)
    near_l, away_r = crossed(near, 1, -1), crossed(away, 1, 1)
    near_2, away_2 = crossed(near_r, 1, 1), crossed(away_l, 1, -1)
    return [near, away, near_r, away_r, near_l, away_l, near_2, away_2], first, second


def place_of(place, i, j):
    x, y, c = place[0], place[1], place[2]
    first, second = OFFSETS[i] + 4, OFFSETS[j] + 4
    dx = jnp.where(c == 0, first, second)
    dy = jnp.where(c == 0, second, first)
    return lax.rem(y + dy, NY), lax.rem(x + dx, NX)


def load_operands(place, pieces, weights, groups, tok, w, sems):
    x, y, c = place[0], place[1], place[2]

    def fetch_weights(group):
        for core, lane, width, to in groups[group]:
            for rel, d in enumerate(OFFSETS):
                yy = lax.rem(y + (d + NY), NY)
                pltpu.make_async_copy(
                    weights.at[:, 1 - c if core else c, rel, :, pl.ds(lane, width)],
                    w.at[group, :, yy, :, pl.ds(to, width)],
                    sems.at[group],
                ).start()

    fetch_weights(0)
    for j in range(4):
        for i in range(4):
            yy, xx = place_of(place, i, j)
            pltpu.make_async_copy(
                pieces[j * 2 + i // 2].at[i % 2],
                tok.at[
                    pl.ds(pl.multiple_of(yy * HALF, HALF), HALF),
                    pl.ds(pl.multiple_of(xx * (D // NX), D // NX), D // NX),
                ],
                sems.at[3],
            ).start()
    for group in range(1, len(groups)):
        fetch_weights(group)
    pltpu.make_async_copy(tok, tok, sems.at[3]).wait()


def product(group, tok, w, sems):
    pltpu.make_async_copy(w.at[group], w.at[group], sems.at[group]).wait()
    return jnp.dot(tok[...], w[group].reshape(D, CH), preferred_element_type=F32)


def silu(v):
    return v / (1.0 + jnp.exp(-v))


GATES = [[(0, 0, CH, 0)], [(1, 0, CH, 0)]]
SIDES = [[(0, CH, 128, 0), (1, CH, 128, 128)]]


def project_first(place, *refs):
    pieces, weights = refs[:8], refs[8]
    outs, (tok, w, sems) = refs[9:17], refs[17:]
    load_operands(place, pieces, weights, SIDES + GATES, tok, w, sems)
    acc = product(0, tok, w, sems)
    for core in range(2):
        _, bc_ref, dt_ref, tail = outs[4 * core : 4 * core + 4]
        side = acc[:, core * 128 : core * 128 + 128].T
        bc_ref[...] = side[:64].astype(BF)
        dt_ref[...] = side[64:72]
        tail[:64, :] = side[:64, NY * HALF - Q :].astype(BF)
    for core in range(2):
        x_ref, _, _, tail = outs[4 * core : 4 * core + 4]
        x = product(1 + core, tok, w, sems).astype(BF)
        x_ref[...] = x.reshape(NY, HALF, CH)
        tail[64:80, :] = x[NY * HALF - 16 :, :Q]
        tail[80:, :] = x[NY * HALF - 16 :, Q:]


def project_second(place, *refs):
    pieces, weights = refs[:8], refs[8]
    outs, (tok, w, sems) = refs[9:11], refs[11:]
    load_operands(place, pieces, weights, GATES, tok, w, sems)
    for core in range(2):
        outs[core][...] = product(core, tok, w, sems).astype(BF).reshape(NY, HALF, CH)


def run_projection(kernel, place, pieces, weights, groups, outs):
    return pl.pallas_call(
        kernel,
        out_shape=outs,
        in_specs=[SMEM] + [ANY] * 8 + [HBM],
        out_specs=[VMEM] * len(outs),
        scratch_shapes=[
            pltpu.VMEM((NY * HALF, D), BF),
            pltpu.VMEM((groups, NZ, NY, 128, CH), BF),
            pltpu.SemaphoreType.DMA((4,)),
        ],
        compiler_params=pltpu.CompilerParams(vmem_limit_bytes=52 * MIB),
        cost_estimate=SMALL,
    )(place, *pieces, weights)


def local_call(kernel, outs, *args, scratch=(), limit=20):
    return pl.pallas_call(
        kernel,
        out_shape=outs,
        in_specs=[SMEM] + [VMEM] * (len(args) - 1),
        out_specs=[VMEM] * len(outs),
        scratch_shapes=list(scratch),
        compiler_params=pltpu.CompilerParams(vmem_limit_bytes=limit * MIB),
        cost_estimate=SMALL,
    )(*args)


def half_start(place, k, other):
    half = 1 - place[2] if other else place[2]
    return pl.multiple_of(k * ROWS + half * HALF, HALF)


def conv_and_rates(
    place, own, other, halo_1, halo_2, taps, dt_own, dt_other, bias, a_log, *rest
):
    out_ref, run_ref, step_ref, full, raw_full = rest
    halo = (halo_1[64:, :] + halo_2[64:, :]).astype(F32)
    full[:16, :Q] = halo[:16]
    full[:16, Q:] = halo[16:]
    for k in range(NY):
        full[pl.ds(half_start(place, k, False) + 16, HALF), :] = own[k].astype(F32)
        full[pl.ds(half_start(place, k, True) + 16, HALF), :] = other[k].astype(F32)
        at = slice(k * HALF, (k + 1) * HALF)
        raw_full[:, pl.ds(half_start(place, k, False), HALF)] = dt_own[:, at]
        raw_full[:, pl.ds(half_start(place, k, True), HALF)] = dt_other[:, at]
    for block in range(NB):
        total = taps[3:4, :] * full[block * Q + 16 : block * Q + 16 + Q, :]
        for back in (1, 2, 3):
            start = block * Q + 16 - back
            total = total + taps[3 - back : 4 - back, :] * full[start : start + Q, :]
        out_ref[block * Q : (block + 1) * Q, :] = silu(total).astype(BF)
    lane = lax.broadcasted_iota(jnp.int32, (8, Q), 1)
    factor = -jnp.exp(a_log[...])
    for block in range(NB):
        at = slice(block * Q, (block + 1) * Q)
        raw = raw_full[:, at] + bias[...]
        step = jnp.maximum(raw, 0.0) + jnp.log1p(jnp.exp(-jnp.abs(raw)))
        running = step * factor
        for distance in (1, 2, 4, 8, 16, 32, 64):
            running = running + jnp.where(lane < distance, 0.0, pltpu.roll(running, distance, 1))
        run_ref[:, at] = running
        step_ref[:, at] = step


def convolve_side(place, own, other, halo_1, halo_2, taps, out_ref, full):
    full[:, :Q] = (halo_1[:64, :] + halo_2[:64, :]).astype(F32)
    for k in range(NY):
        at = slice(k * HALF, (k + 1) * HALF)
        full[:, pl.ds(pl.multiple_of(half_start(place, k, False) + Q, Q), HALF)] = own[
            :, at
        ].astype(F32)
        full[:, pl.ds(pl.multiple_of(half_start(place, k, True) + Q, Q), HALF)] = other[
            :, at
        ].astype(F32)
    lane = lax.broadcasted_iota(jnp.int32, (64, Q), 1)
    before = [pltpu.roll(full[:, :Q], back, 1) for back in (1, 2, 3)]
    for block in range(NB):
        now = full[:, (block + 1) * Q : (block + 2) * Q]
        turned = [pltpu.roll(now, back, 1) for back in (1, 2, 3)]
        total = taps[:, 3:4] * now
        for back in (1, 2, 3):
            moved = jnp.where(lane < back, before[back - 1], turned[back - 1])
            total = total + taps[:, 3 - back : 4 - back] * moved
        out_ref[:, block * Q : (block + 1) * Q] = silu(total).astype(BF)
        before = turned


def states(place, x_ref, run_ref, step_ref, *rest):
    parts, (bc_ref, local_ref, end_ref) = rest[:4], rest[4:]
    for part, d in zip(parts, OFFSETS):
        yy = lax.rem(place[1] + (d + NY), NY)
        bc_ref[pl.ds(pl.multiple_of(yy * 64, 64), 64), :] = part[...]
    state = [jnp.zeros((N, PS), F32) for _ in range(HD)]
    total_rate = jnp.zeros((8, Q), F32)
    for block in range(NB):
        at = slice(block * Q, (block + 1) * Q)
        b = bc_ref[:N, at].astype(F32)
        running, step = run_ref[:, at], step_ref[:, at]
        last = running[:, Q - 1 : Q]
        weight = jnp.exp(last - running) * step
        decay = jnp.exp(last)
        for h in range(HD):
            local_ref[block, :, h * PS : (h + 1) * PS] = state[h].astype(BF)
            scaled = (b * weight[h : h + 1, :]).astype(BF)
            increment = jnp.dot(
                scaled, x_ref[at, h * PS : (h + 1) * PS], preferred_element_type=F32
            )
            state[h] = decay[h : h + 1, :] * state[h] + increment
        total_rate = total_rate + last
    for h in range(HD):
        end_ref[:N, h * PS : (h + 1) * PS] = state[h]
    whole = jnp.exp(total_rate)
    end_ref[N:, :] = jnp.concatenate([jnp.concatenate([whole] * 2, axis=0)] * 2, axis=1)


def within(place, x_ref, bc_ref, run_ref, step_ref, skip, y_ref):
    below = lax.broadcasted_iota(jnp.int32, (Q, Q), 0) >= lax.broadcasted_iota(
        jnp.int32, (Q, Q), 1
    )
    for block in range(NB):
        at = slice(block * Q, (block + 1) * Q)
        running, step = run_ref[:, at], step_ref[:, at]
        columns = running.T
        scores = lax.dot_general(
            bc_ref[N:, at], bc_ref[:N, at], (((0,), (0,)), ((), ())), preferred_element_type=F32
        )
        for h in range(HD):
            spread = jnp.where(below, columns[:, h : h + 1] - running[h : h + 1, :], -1e30)
            mixing = (jnp.exp(spread) * step[h : h + 1, :] * scores).astype(BF)
            value = x_ref[at, h * PS : (h + 1) * PS]
            y = jnp.dot(mixing, value, preferred_element_type=F32)
            y_ref[at, h * PS : (h + 1) * PS] = (
                y + skip[:, h * PS : (h + 1) * PS] * value.astype(F32)
            )


def per_head(columns):
    return jnp.concatenate(
        [jnp.broadcast_to(columns[:, h : h + 1], (columns.shape[0], PS)) for h in range(HD)],
        axis=1,
    )


def over_channels(rows):
    return jnp.concatenate([rows[h : h + 1, :PS] for h in range(HD)], axis=1)


def carry(place, bc_ref, run_ref, local_ref, y_ref, z_own, z_other, *rest):
    arrived, outs, (z_full, sorted_rows) = rest[0], rest[1:5], rest[5:]
    for k in range(NY):
        z_full[pl.ds(half_start(place, k, False), HALF), :] = z_own[k]
        z_full[pl.ds(half_start(place, k, True), HALF), :] = z_other[k]
    state = jnp.zeros((N, CH), F32)
    for z in range(NZ - 1):
        grown = over_channels(arrived[z, N : N + 8, :Q]) * state + arrived[z, :N, :]
        state = jnp.where(place[3] > z, grown, state)
    before = jnp.ones((1, CH), F32)
    for block in range(NB):
        at = slice(block * Q, (block + 1) * Q)
        running = run_ref[:, at]
        full = (local_ref[block].astype(F32) + before * state).astype(BF)
        carried = lax.dot_general(
            bc_ref[N:, at], full, (((0,), (0,)), ((), ())), preferred_element_type=F32
        )
        grown = jnp.exp(running)
        y = y_ref[at, :] + per_head(grown.T) * carried
        gate = silu(z_full[at, :].astype(F32))
        rel = lax.rem(block // 4 + NY - place[1], NY)
        part = block % 4
        sorted_rows[rel, part * Q : (part + 1) * Q, :] = (y * gate).astype(BF)
        last = jnp.broadcast_to(grown[:, Q - 1 : Q], (8, Q))
        before = before * over_channels(last)
    for rel in range(NY):
        outs[rel][...] = sorted_rows[rel]


def project_out_first(place, gain, w_ref, *rest):
    parts, (hidden, out_ref) = rest[:NY], rest[NY:]

    @pl.when(pl.program_id(0) == 0)
    def _():
        total = jnp.zeros((ROWS, 1), F32)
        for ref in parts:
            value = ref[...].astype(F32)
            total = total + jnp.sum(value * value, axis=1, keepdims=True)
        scale = lax.rsqrt(total / (NY * CH) + EPSILON)
        for ref, d in zip(parts, OFFSETS):
            yy = lax.rem(place[1] + (d + NY), NY)
            lanes = pl.ds(pl.multiple_of(yy * CH, CH), CH)
            hidden[:, lanes] = (ref[...].astype(F32) * scale * gain[:, lanes]).astype(BF)

    out_ref[...] = jnp.dot(hidden[...], w_ref[...], preferred_element_type=F32).astype(BF)


def project_out_second(place, gain, w_ref, hidden, out_ref):
    out_ref[...] = jnp.dot(hidden[...], w_ref[...], preferred_element_type=F32).astype(BF)


def run_out(place, gain, w_out, parts, other):
    def columns(i, p):
        ahead = jnp.where(i == 0, 2, jnp.where(i == 2, 3, jnp.where(i == 1, 1, 0)))
        return 0, lax.rem(p[0] + ahead, NX) * NC + (1 - p[2] if other else p[2])

    whole = lambda shape: pl.BlockSpec(shape, lambda i, p: (0,) * len(shape))
    product_spec = pl.BlockSpec((ROWS, FEAT), lambda i, p: (0, i))
    hidden = (ROWS, NY * CH)
    outs, specs = [SHAPE((ROWS, NX * FEAT), BF)], [product_spec]
    if other:
        outs, specs = [SHAPE(hidden, BF)] + outs, [whole(hidden)] + specs
    return pl.pallas_call(
        project_out_first if other else project_out_second,
        out_shape=outs,
        grid_spec=pltpu.PrefetchScalarGridSpec(
            num_scalar_prefetch=1,
            grid=(NX,),
            in_specs=[whole(gain.shape), pl.BlockSpec((NY * CH, FEAT), columns)]
            + [whole(v.shape) for v in parts],
            out_specs=specs,
        ),
        compiler_params=pltpu.CompilerParams(vmem_limit_bytes=20 * MIB),
        cost_estimate=SMALL,
    )(place, gain, w_out, *parts)


def merge(place, kept, got, far, ahead, behind, stays):
    for k, ref in enumerate((far, ahead, behind, stays)):
        at = slice(k * FEAT, (k + 1) * FEAT)
        ref[...] = (kept[:, at].astype(F32) + got[:, at].astype(F32)).astype(ref.dtype)


def finish(place, own, first, second, third, out_ref):
    total = own[...] + first[...].astype(F32)
    out_ref[...] = (total + second[...].astype(F32) + third[...].astype(F32)).astype(BF)


def on_device(tokens, w_zx, w_bc, w_dt, conv_x, conv_bc, dt_bias, a_log, d_skip, norm_gain, w_out):
    y, c = lax.axis_index("y"), lax.axis_index("c")
    place = jnp.stack([lax.axis_index("x"), y, c, lax.axis_index("z")]).astype(jnp.int32)
    rows = w_zx.shape[0]

    def quarter(value, distance, width, dim=1):
        start = lax.rem(y + (distance + NY), NY) * width
        return lax.dynamic_slice_in_dim(value, start, width, dim)

    def for_y(distance):
        zero = jnp.zeros((rows, W1 - CH - 64 - HD), BF)
        return jnp.concatenate(
            [
                quarter(w_zx[:, 1], distance, CH),
                quarter(w_bc.reshape(rows, -1), distance, 64),
                quarter(w_dt, distance, HD),
                zero,
            ],
            axis=1,
        )

    mine = half_rows(tokens, c)
    gate = lambda d: quarter(w_zx[:, 0], d, CH)
    pieces, first, second = gather_tokens(
        mine, [for_y(d) for d in range(NY)], [gate(d) for d in range(NY)]
    )
    weights_1 = lax.all_gather(jnp.concatenate(first), ("z", "c"), axis=0, tiled=True)
    weights_1 = weights_1.reshape(NZ, NC, NY, rows, W1)
    weights_2 = lax.all_gather(jnp.concatenate(second), ("z", "c"), axis=0, tiled=True)
    weights_2 = weights_2.reshape(NZ, NC, NY, rows, CH)

    taps_x = quarter(conv_x, 0, CH).astype(F32)
    taps_bc = quarter(conv_bc.reshape(4, -1), 0, 64).T.astype(F32)
    column = lambda v: jnp.pad(quarter(v, 0, HD, 0), (0, 8 - HD)).reshape(8, 1)
    skip = jnp.repeat(quarter(d_skip, 0, HD, 0), PS).reshape(1, CH)
    gain = norm_gain.astype(F32).reshape(1, -1)

    kinds = [
        SHAPE((NY, HALF, CH), BF),
        SHAPE((64, NY * HALF), BF),
        SHAPE((8, NY * HALF), F32),
        SHAPE((96, Q), BF),
    ]
    first_outs = run_projection(project_first, place, pieces, weights_1, 3, kinds * 2)
    x_own, bc_own, dt_own, tail_own = first_outs[:4]
    x_give, bc_give, dt_give, tail_give = first_outs[4:]
    bc_got = sibling(bc_give)
    halo_own = routed(
        tail_own, lambda z, y, x, c: (z + 1, y, x, 1) if z + 1 < NZ and c == 1 else None
    )
    halo_give = routed(
        tail_give, lambda z, y, x, c: (z + 1, y, x, 0) if z + 1 < NZ and c == 1 else None
    )
    x_got, dt_got = sibling(x_give), sibling(dt_give)
    (bc,) = local_call(
        convolve_side,
        [SHAPE((64, T), BF)],
        place,
        bc_own,
        bc_got,
        halo_own,
        halo_give,
        taps_bc,
        scratch=[pltpu.VMEM((64, T + Q), F32)],
    )
    bc_parts = [bc] + [shifted(bc, "y", d) for d in (1, -1, 2)]
    x_conv, running, step = local_call(
        conv_and_rates,
        [SHAPE((T, CH), BF), SHAPE((8, T), F32), SHAPE((8, T), F32)],
        place,
        x_own,
        x_got,
        halo_own,
        halo_give,
        taps_x,
        dt_own,
        dt_got,
        column(dt_bias),
        column(a_log),
        scratch=[pltpu.VMEM((T + 16, CH), F32), pltpu.VMEM((8, T), F32)],
    )
    bc_conv, local, end = local_call(
        states,
        [SHAPE((2 * N, T), BF), SHAPE((NB, N, CH), BF), SHAPE((N + 16, CH), F32)],
        place,
        x_conv,
        running,
        step,
        *bc_parts,
    )
    place_2, end = lax.optimization_barrier((place, end))
    ends = lax.all_gather(end, "z")
    z_own, z_give = run_projection(project_second, place_2, pieces, weights_2, 2, kinds[:1] * 2)
    z_got = sibling(z_give)
    (y_within,) = local_call(
        within, [SHAPE((T, CH), F32)], place, x_conv, bc_conv, running, step, skip
    )
    sorted_rows = local_call(
        carry,
        [SHAPE((ROWS, CH), BF)] * NY,
        place,
        bc_conv,
        running,
        local,
        y_within,
        z_own,
        z_got,
        ends,
        scratch=[pltpu.VMEM((T, CH), BF), pltpu.VMEM((NY, ROWS, CH), BF)],
    )
    hidden, give = run_out(place, gain, w_out, over_y(sorted_rows), True)
    got = sibling(give)
    (kept,) = run_out(place, gain, w_out, [hidden], False)
    block = (ROWS, FEAT)
    far, ahead, behind, stays = local_call(
        merge, [SHAPE(block, kind) for kind in (BF, BF, BF, F32)], place, kept, got
    )
    (out,) = local_call(
        finish,
        [SHAPE(block, BF)],
        place,
        stays,
        shifted(ahead, "x", 1),
        shifted(behind, "x", -1),
        shifted(far, "x", 2),
    )
    return out


def solution(mesh):
    fine = Mesh(mesh.devices.reshape(NZ, NY, NX, NC), ("z", "y", "x", "c"))
    seq, head = ("z", "y"), ("x", "c")
    return jax.shard_map(
        on_device,
        mesh=fine,
        in_specs=(
            P(seq, head),
            P(seq, None, head),
            P(seq, None, head),
            P(seq, head),
            P(None, head),
            P(None, None, head),
            P(head),
            P(head),
            P(head),
            P(head),
            P(head, None),
        ),
        out_specs=P(seq, head),
        check_vma=False,
    )
```

```python
import functools
import jax
import jax.numpy as jnp
from jax import lax
from jax.experimental import pallas as pl
from jax.experimental.pallas import tpu as pltpu
from jax.sharding import Mesh, PartitionSpec as P

EPSILON = 1e-05
BF = jnp.bfloat16
F32 = jnp.float32
MIB = 1024 * 1024

NZ, NY, NX, NC = 8, 4, 4, 2
ROWS = 512
HALF = ROWS // 2
FEAT = 512
D = 4096
T = ROWS * NY
CH = 256
HD = 4
PS = 64
N = 128
Q = 128
NB = T // Q
W1 = 384
OFFSETS = (0, -1, 1, 2)
ALL = ("z", "y", "x", "c")
VMEM = pl.BlockSpec(memory_space=pltpu.VMEM)
SMEM = pl.BlockSpec(memory_space=pltpu.SMEM)
ANY = pl.BlockSpec(memory_space=pl.ANY)
HBM = pl.BlockSpec(memory_space=pltpu.HBM)
SHAPE = jax.ShapeDtypeStruct
SMALL = pl.CostEstimate(flops=1000, bytes_accessed=1000, transcendentals=0)


def shifted(value, axis, distance):
    n = lax.axis_size(axis)
    return lax.ppermute(value, axis, [(i, (i + distance) % n) for i in range(n)])


def sibling(value):
    return lax.ppermute(value, "c", [(0, 1), (1, 0)])


def routed(value, target):
    pairs = []
    for source in range(NZ * NY * NX * NC):
        rest, c = divmod(source, NC)
        rest, x = divmod(rest, NX)
        z, y = divmod(rest, NY)
        goal = target(z, y, x, c)
        if goal is not None:
            z, y, x, c = goal
            pairs.append((source, ((z * NY + y) * NX + x) * NC + c))
    return lax.ppermute(value, ALL, pairs)


def crossed(value, along_x, distance):
    def target(z, y, x, c):
        if c == along_x:
            return z, y, (x + distance) % NX, c
        return z, (y + distance) % NY, x, c

    return routed(value, target)


def over_y(v):
    return [v[0], shifted(v[1], "y", 1), shifted(v[3], "y", -1), shifted(v[2], "y", 2)]


def half_rows(tokens, c):
    early, late = tokens[:HALF], tokens[HALF:]
    got = sibling(jnp.where(c == 0, late, early))
    return jnp.where(
        c == 0,
        jnp.concatenate([early, got], axis=1),
        jnp.concatenate([got, late], axis=1),
    )


def gather_tokens(mine, first, second):
    mine, first = lax.optimization_barrier((mine, first))
    right, left = crossed(mine, 0, 1), crossed(mine, 0, -1)
    first = over_y(first)
    right, left, first, second = lax.optimization_barrier((right, left, first, second))
    middle = HALF // 2
    opposite = [crossed(right[:middle], 0, 1), crossed(left[middle:], 0, -1)]
    second = over_y(second)
    near = jnp.stack([mine, right])
    away = jnp.stack([left, jnp.concatenate(opposite)])
    near, away, second = lax.optimization_barrier((near, away, second))
    near_r, away_l = crossed(near, 1, 1), crossed(away, 1, -1)
    near_l, away_r = crossed(near, 1, -1), crossed(away, 1, 1)
    near_2, away_2 = crossed(near_r, 1, 1), crossed(away_l, 1, -1)
    return [near, away, near_r, away_r, near_l, away_l, near_2, away_2], first, second


def place_of(place, i, j):
    x, y, c = place[0], place[1], place[2]
    first, second = OFFSETS[i] + 4, OFFSETS[j] + 4
    dx = jnp.where(c == 0, first, second)
    dy = jnp.where(c == 0, second, first)
    return lax.rem(y + dy, NY), lax.rem(x + dx, NX)


def load_operands(place, pieces, weights, columns, tok, w, sems):
    x, y, c = place[0], place[1], place[2]

    def fetch(i, j, block):
        yy, _ = place_of(place, i, j)
        pltpu.make_async_copy(
            pieces[j * 2 + i // 2].at[i % 2],
            tok.at[block, pl.ds(pl.multiple_of(yy * HALF, HALF), HALF), :],
            sems.at[block],
        ).start()

    for block, offset in enumerate(OFFSETS):
        first = lax.rem(x + (offset + NX), NX) * 2
        for core, lane, width, to in columns:
            for rel, d in enumerate(OFFSETS):
                yy = lax.rem(y + (d + NY), NY)
                pltpu.make_async_copy(
                    weights.at[pl.ds(first, 2), 1 - c if core else c, rel, :, pl.ds(lane, width)],
                    w.at[block, :, yy, :, pl.ds(to, width)],
                    sems.at[4 + block],
                ).start()

        @pl.when(c == 0)
        def _():
            for j in range(4):
                fetch(block, j, block)

        @pl.when(c == 1)
        def _():
            for i in range(4):
                fetch(i, block, block)


def products(tok, w, acc, sems):
    for block in range(4):
        pltpu.make_async_copy(tok.at[block], tok.at[block], sems.at[block]).wait()
        pltpu.make_async_copy(w.at[block], w.at[block], sems.at[4 + block]).wait()
        for k in range(NY):
            rows = slice(k * HALF, (k + 1) * HALF)
            part = jnp.dot(
                tok[block, rows, :],
                w[block].reshape(D // NX, w.shape[-1]),
                preferred_element_type=F32,
            )
            if block == 0:
                acc[rows, :] = part
            elif block < 3:
                acc[rows, :] += part
            else:
                yield k, acc[rows, :] + part


def silu(v):
    return v / (1.0 + jnp.exp(-v))


GATES = [(0, 0, CH, 0), (1, 0, CH, CH)]
SIDES = [(0, CH, 128, 2 * CH), (1, CH, 128, 2 * CH + 128)]


def project_first(place, *refs):
    pieces, weights = refs[:8], refs[8]
    outs, (tok, w, acc, sems) = refs[9:17], refs[17:]
    load_operands(place, pieces, weights, GATES + SIDES, tok, w, sems)
    for k, total in products(tok, w, acc, sems):
        rows = slice(k * HALF, (k + 1) * HALF)
        for core in range(2):
            x_ref, bc_ref, dt_ref, tail = outs[4 * core : 4 * core + 4]
            x = total[:, core * CH : (core + 1) * CH].astype(BF)
            start = 2 * CH + 128 * core
            side = total[:, start : start + 128].T
            x_ref[k] = x
            bc_ref[:, rows] = side[:64].astype(BF)
            dt_ref[:, rows] = side[64:72]
            if k == NY - 1:
                tail[:64, :] = side[:64, HALF - Q :].astype(BF)
                tail[64:80, :] = x[HALF - 16 :, :Q]
                tail[80:, :] = x[HALF - 16 :, Q:]


def project_second(place, *refs):
    pieces, weights = refs[:8], refs[8]
    outs, (tok, w, acc, sems) = refs[9:11], refs[11:]
    load_operands(place, pieces, weights, GATES, tok, w, sems)
    for k, total in products(tok, w, acc, sems):
        for core in range(2):
            outs[core][k] = total[:, core * CH : (core + 1) * CH].astype(BF)


def run_projection(kernel, place, pieces, weights, width, outs):
    return pl.pallas_call(
        kernel,
        out_shape=outs,
        in_specs=[SMEM] + [ANY] * 8 + [HBM],
        out_specs=[VMEM] * len(outs),
        scratch_shapes=[
            pltpu.VMEM((NX, NY * HALF, D // NX), BF),
            pltpu.VMEM((NX, NZ // NX, NY, 128, width), BF),
            pltpu.VMEM((NY * HALF, width), F32),
            pltpu.SemaphoreType.DMA((8,)),
        ],
        compiler_params=pltpu.CompilerParams(vmem_limit_bytes=52 * MIB),
        cost_estimate=SMALL,
    )(place, *pieces, weights)


def local_call(kernel, outs, *args, scratch=(), limit=20):
    return pl.pallas_call(
        kernel,
        out_shape=outs,
        in_specs=[SMEM] + [VMEM] * (len(args) - 1),
        out_specs=[VMEM] * len(outs),
        scratch_shapes=list(scratch),
        compiler_params=pltpu.CompilerParams(vmem_limit_bytes=limit * MIB),
        cost_estimate=SMALL,
    )(*args)


def half_start(place, k, other):
    half = 1 - place[2] if other else place[2]
    return pl.multiple_of(k * ROWS + half * HALF, HALF)


def conv_and_rates(
    place, own, other, halo_1, halo_2, taps, dt_own, dt_other, bias, a_log, *rest
):
    out_ref, run_ref, step_ref, full, raw_full = rest
    halo = (halo_1[64:, :] + halo_2[64:, :]).astype(F32)
    full[:16, :Q] = halo[:16]
    full[:16, Q:] = halo[16:]
    for k in range(NY):
        full[pl.ds(half_start(place, k, False) + 16, HALF), :] = own[k].astype(F32)
        full[pl.ds(half_start(place, k, True) + 16, HALF), :] = other[k].astype(F32)
        at = slice(k * HALF, (k + 1) * HALF)
        raw_full[:, pl.ds(half_start(place, k, False), HALF)] = dt_own[:, at]
        raw_full[:, pl.ds(half_start(place, k, True), HALF)] = dt_other[:, at]
    for block in range(NB):
        total = taps[3:4, :] * full[block * Q + 16 : block * Q + 16 + Q, :]
        for back in (1, 2, 3):
            start = block * Q + 16 - back
            total = total + taps[3 - back : 4 - back, :] * full[start : start + Q, :]
        out_ref[block * Q : (block + 1) * Q, :] = silu(total).astype(BF)
    lane = lax.broadcasted_iota(jnp.int32, (8, Q), 1)
    factor = -jnp.exp(a_log[...])
    for block in range(NB):
        at = slice(block * Q, (block + 1) * Q)
        raw = raw_full[:, at] + bias[...]
        step = jnp.maximum(raw, 0.0) + jnp.log1p(jnp.exp(-jnp.abs(raw)))
        running = step * factor
        for distance in (1, 2, 4, 8, 16, 32, 64):
            running = running + jnp.where(lane < distance, 0.0, pltpu.roll(running, distance, 1))
        run_ref[:, at] = running
        step_ref[:, at] = step


def convolve_side(place, own, other, halo_1, halo_2, taps, out_ref, full):
    full[:, :Q] = (halo_1[:64, :] + halo_2[:64, :]).astype(F32)
    for k in range(NY):
        at = slice(k * HALF, (k + 1) * HALF)
        full[:, pl.ds(pl.multiple_of(half_start(place, k, False) + Q, Q), HALF)] = own[
            :, at
        ].astype(F32)
        full[:, pl.ds(pl.multiple_of(half_start(place, k, True) + Q, Q), HALF)] = other[
            :, at
        ].astype(F32)
    lane = lax.broadcasted_iota(jnp.int32, (64, Q), 1)
    before = [pltpu.roll(full[:, :Q], back, 1) for back in (1, 2, 3)]
    for block in range(NB):
        now = full[:, (block + 1) * Q : (block + 2) * Q]
        turned = [pltpu.roll(now, back, 1) for back in (1, 2, 3)]
        total = taps[:, 3:4] * now
        for back in (1, 2, 3):
            moved = jnp.where(lane < back, before[back - 1], turned[back - 1])
            total = total + taps[:, 3 - back : 4 - back] * moved
        out_ref[:, block * Q : (block + 1) * Q] = silu(total).astype(BF)
        before = turned


def apart(value):
    lane = lax.broadcasted_iota(jnp.int32, value.shape, 1)
    zero = jnp.zeros_like(value)
    return jnp.concatenate(
        [jnp.where(lane < PS, value, zero), jnp.where(lane < PS, zero, value)], axis=0
    )


def of_pair(rows, pair):
    lane = lax.broadcasted_iota(jnp.int32, (1, Q), 1)
    return jnp.where(lane < PS, rows[2 * pair : 2 * pair + 1], rows[2 * pair + 1 : 2 * pair + 2])


def decay_rows(decay):
    wide = jnp.broadcast_to(decay, (8, CH))
    high = wide.astype(BF)
    return jnp.concatenate([high, (wide - high.astype(F32)).astype(BF)], axis=0)


def decay_of(ref):
    return ref[N : N + 1, :].astype(F32) + ref[N + 8 : N + 9, :].astype(F32)


def combine(place, late, early, out_ref):
    decay = decay_of(late)
    state = late[:N, :].astype(F32) + decay * early[:N, :].astype(F32)
    out_ref[:N, :] = state.astype(BF)
    out_ref[N:, :] = decay_rows(decay * decay_of(early))


def states(place, x_ref, run_ref, step_ref, *rest):
    parts, (bc_ref, local_ref, end_ref) = rest[:4], rest[4:]
    for part, d in zip(parts, OFFSETS):
        yy = lax.rem(place[1] + (d + NY), NY)
        bc_ref[pl.ds(pl.multiple_of(yy * 64, 64), 64), :] = part[...]
    state = [jnp.zeros((N, Q), F32) for _ in range(HD // 2)]
    total_rate = jnp.zeros((8, Q), F32)
    for block in range(NB):
        at = slice(block * Q, (block + 1) * Q)
        b = bc_ref[:N, at].astype(F32)
        running, step = run_ref[:, at], step_ref[:, at]
        last = running[:, Q - 1 : Q]
        weight = jnp.exp(last - running) * step
        decay = jnp.exp(last)
        for pair in range(HD // 2):
            lanes = slice(pair * Q, (pair + 1) * Q)
            local_ref[block, :, lanes] = state[pair].astype(BF)
            scaled = [(b * weight[h : h + 1, :]).astype(BF) for h in (2 * pair, 2 * pair + 1)]
            increment = jnp.dot(
                jnp.concatenate(scaled, axis=1),
                apart(x_ref[at, lanes]),
                preferred_element_type=F32,
            )
            state[pair] = of_pair(decay, pair) * state[pair] + increment
        total_rate = total_rate + last
    for pair in range(HD // 2):
        end_ref[:N, pair * Q : (pair + 1) * Q] = state[pair].astype(BF)
    end_ref[N:, :] = decay_rows(over_channels(jnp.exp(total_rate)))


def within(first, count, place, x_ref, bc_ref, run_ref, step_ref, skip, y_ref):
    below = lax.broadcasted_iota(jnp.int32, (Q, Q), 0) >= lax.broadcasted_iota(
        jnp.int32, (Q, Q), 1
    )
    for block in range(first, first + count):
        at = slice(block * Q, (block + 1) * Q)
        running, step = run_ref[:, at], step_ref[:, at]
        columns = running.T
        scores = lax.dot_general(
            bc_ref[N:, at], bc_ref[:N, at], (((0,), (0,)), ((), ())), preferred_element_type=F32
        )
        for pair in range(HD // 2):
            mixing = []
            for h in (2 * pair, 2 * pair + 1):
                spread = jnp.where(below, columns[:, h : h + 1] - running[h : h + 1, :], -1e30)
                mixing.append((jnp.exp(spread) * step[h : h + 1, :] * scores).astype(BF))
            lanes = slice(pair * Q, (pair + 1) * Q)
            value = x_ref[at, lanes]
            y = jnp.dot(
                jnp.concatenate(mixing, axis=1), apart(value), preferred_element_type=F32
            )
            out = slice((block - first) * Q, (block - first + 1) * Q)
            y_ref[out, lanes] = y + skip[:, lanes] * value.astype(F32)


def per_head(columns):
    return jnp.concatenate(
        [jnp.broadcast_to(columns[:, h : h + 1], (columns.shape[0], PS)) for h in range(HD)],
        axis=1,
    )


def over_channels(rows):
    return jnp.concatenate([rows[h : h + 1, :PS] for h in range(HD)], axis=1)


def carry(place, bc_ref, run_ref, local_ref, y_early, y_late, z_own, z_other, *rest):
    arrived, outs, (z_full, sorted_rows) = rest[:2], rest[2:6], rest[6:]
    for k in range(NY):
        z_full[pl.ds(half_start(place, k, False), HALF), :] = z_own[k]
        z_full[pl.ds(half_start(place, k, True), HALF), :] = z_other[k]
    last_4, earlier_4 = arrived
    state = last_4[:N, :].astype(F32) + decay_of(last_4) * earlier_4[:N, :].astype(F32)
    before = jnp.ones((1, CH), F32)
    for block in range(NB):
        at = slice(block * Q, (block + 1) * Q)
        running = run_ref[:, at]
        full = (local_ref[block].astype(F32) + before * state).astype(BF)
        carried = lax.dot_general(
            bc_ref[N:, at], full, (((0,), (0,)), ((), ())), preferred_element_type=F32
        )
        grown = jnp.exp(running)
        y_ref = y_early if block < NB // 2 else y_late
        y_at = slice(block % (NB // 2) * Q, (block % (NB // 2) + 1) * Q)
        y = y_ref[y_at, :] + per_head(grown.T) * carried
        gate = silu(z_full[at, :].astype(F32))
        rel = lax.rem(block // 4 + NY - place[1], NY)
        part = block % 4
        sorted_rows[rel, part * Q : (part + 1) * Q, :] = (y * gate).astype(BF)
        last = jnp.broadcast_to(grown[:, Q - 1 : Q], (8, Q))
        before = before * over_channels(last)
    for rel in range(NY):
        outs[rel][...] = sorted_rows[rel]


def project_out_first(place, gain, w_ref, *rest):
    parts, (hidden, out_ref) = rest[:NY], rest[NY:]

    @pl.when(pl.program_id(0) == 0)
    def _():
        total = jnp.zeros((ROWS, 1), F32)
        for ref in parts:
            value = ref[...].astype(F32)
            total = total + jnp.sum(value * value, axis=1, keepdims=True)
        scale = lax.rsqrt(total / (NY * CH) + EPSILON)
        for ref, d in zip(parts, OFFSETS):
            yy = lax.rem(place[1] + (d + NY), NY)
            lanes = pl.ds(pl.multiple_of(yy * CH, CH), CH)
            hidden[:, lanes] = (ref[...].astype(F32) * scale * gain[:, lanes]).astype(BF)

    out_ref[...] = jnp.dot(hidden[...], w_ref[...], preferred_element_type=F32).astype(BF)


def project_out_second(place, gain, w_ref, hidden, out_ref):
    out_ref[...] = jnp.dot(hidden[...], w_ref[...], preferred_element_type=F32).astype(BF)


def run_out(place, gain, w_out, parts, other):
    def columns(i, p):
        ahead = jnp.where(i == 0, 2, jnp.where(i == 2, 3, jnp.where(i == 1, 1, 0)))
        return 0, lax.rem(p[0] + ahead, NX) * NC + (1 - p[2] if other else p[2])

    whole = lambda shape: pl.BlockSpec(shape, lambda i, p: (0,) * len(shape))
    product_spec = pl.BlockSpec((ROWS, FEAT), lambda i, p: (0, i))
    hidden = (ROWS, NY * CH)
    outs, specs = [SHAPE((ROWS, NX * FEAT), BF)], [product_spec]
    if other:
        outs, specs = [SHAPE(hidden, BF)] + outs, [whole(hidden)] + specs
    return pl.pallas_call(
        project_out_first if other else project_out_second,
        out_shape=outs,
        grid_spec=pltpu.PrefetchScalarGridSpec(
            num_scalar_prefetch=1,
            grid=(NX,),
            in_specs=[whole(gain.shape), pl.BlockSpec((NY * CH, FEAT), columns)]
            + [whole(v.shape) for v in parts],
            out_specs=specs,
        ),
        compiler_params=pltpu.CompilerParams(vmem_limit_bytes=52 * MIB),
        cost_estimate=SMALL,
    )(place, gain, w_out, *parts)


def merge(place, kept, got, far, ahead, behind, stays):
    for k, ref in enumerate((far, ahead, behind, stays)):
        at = slice(k * FEAT, (k + 1) * FEAT)
        ref[...] = (kept[:, at].astype(F32) + got[:, at].astype(F32)).astype(ref.dtype)


def finish(place, own, first, second, third, out_ref):
    total = own[...] + first[...].astype(F32)
    out_ref[...] = (total + second[...].astype(F32) + third[...].astype(F32)).astype(BF)


def on_device(tokens, w_zx, w_bc, w_dt, conv_x, conv_bc, dt_bias, a_log, d_skip, norm_gain, w_out):
    y, c = lax.axis_index("y"), lax.axis_index("c")
    place = jnp.stack([lax.axis_index("x"), y, c, lax.axis_index("z")]).astype(jnp.int32)
    rows = w_zx.shape[0]

    def quarter(value, distance, width, dim=1):
        start = lax.rem(y + (distance + NY), NY) * width
        return lax.dynamic_slice_in_dim(value, start, width, dim)

    def for_y(distance):
        zero = jnp.zeros((rows, W1 - CH - 64 - HD), BF)
        return jnp.concatenate(
            [
                quarter(w_zx[:, 1], distance, CH),
                quarter(w_bc.reshape(rows, -1), distance, 64),
                quarter(w_dt, distance, HD),
                zero,
            ],
            axis=1,
        )

    mine = half_rows(tokens, c)
    gate = lambda d: quarter(w_zx[:, 0], d, CH)
    pieces, first, second = gather_tokens(
        mine, [for_y(d) for d in range(NY)], [gate(d) for d in range(NY)]
    )
    weights_1 = lax.all_gather(jnp.concatenate(first), ("z", "c"), axis=0, tiled=True)
    weights_1 = weights_1.reshape(NZ, NC, NY, rows, W1)
    weights_2 = lax.all_gather(jnp.concatenate(second), ("z", "c"), axis=0, tiled=True)
    weights_2 = weights_2.reshape(NZ, NC, NY, rows, CH)

    taps_x = quarter(conv_x, 0, CH).astype(F32)
    taps_bc = quarter(conv_bc.reshape(4, -1), 0, 64).T.astype(F32)
    column = lambda v: jnp.pad(quarter(v, 0, HD, 0), (0, 8 - HD)).reshape(8, 1)
    skip = jnp.repeat(quarter(d_skip, 0, HD, 0), PS).reshape(1, CH)
    gain = norm_gain.astype(F32).reshape(1, -1)

    kinds = [
        SHAPE((NY, HALF, CH), BF),
        SHAPE((64, NY * HALF), BF),
        SHAPE((8, NY * HALF), F32),
        SHAPE((96, Q), BF),
    ]
    first_outs = run_projection(project_first, place, pieces, weights_1, 768, kinds * 2)
    x_own, bc_own, dt_own, tail_own = first_outs[:4]
    x_give, bc_give, dt_give, tail_give = first_outs[4:]
    bc_got = sibling(bc_give)
    halo_own = routed(
        tail_own, lambda z, y, x, c: (z + 1, y, x, 1) if z + 1 < NZ and c == 1 else None
    )
    halo_give = routed(
        tail_give, lambda z, y, x, c: (z + 1, y, x, 0) if z + 1 < NZ and c == 1 else None
    )
    x_got, dt_got = sibling(x_give), sibling(dt_give)
    (bc,) = local_call(
        convolve_side,
        [SHAPE((64, T), BF)],
        place,
        bc_own,
        bc_got,
        halo_own,
        halo_give,
        taps_bc,
        scratch=[pltpu.VMEM((64, T + Q), F32)],
    )
    bc_parts = [bc] + [shifted(bc, "y", d) for d in (1, -1, 2)]
    x_conv, running, step = local_call(
        conv_and_rates,
        [SHAPE((T, CH), BF), SHAPE((8, T), F32), SHAPE((8, T), F32)],
        place,
        x_own,
        x_got,
        halo_own,
        halo_give,
        taps_x,
        dt_own,
        dt_got,
        column(dt_bias),
        column(a_log),
        scratch=[pltpu.VMEM((T + 16, CH), F32), pltpu.VMEM((8, T), F32)],
    )
    bc_conv, local, end = local_call(
        states,
        [SHAPE((2 * N, T), BF), SHAPE((NB, N, CH), BF), SHAPE((N + 16, CH), BF)],
        place,
        x_conv,
        running,
        step,
        *bc_parts,
    )
    later = lambda v, d: lax.ppermute(v, "z", [(i, i + d) for i in range(NZ - d)])
    window = [SHAPE((N + 16, CH), BF)]
    blocks = [SHAPE((T // 2, CH), F32)]
    part = lambda first, p: local_call(
        functools.partial(within, first, NB // 2), blocks, p, x_conv, bc_conv, running, step, skip
    )[0]
    near = later(end, 1)
    y_early = part(0, place)
    near, y_early = lax.optimization_barrier((near, y_early))
    (end_2,) = local_call(combine, window, place, end, near)
    place_2, end_2 = lax.optimization_barrier((place, end_2))
    near = later(end_2, 2)
    y_late = part(NB // 2, place_2)
    near, y_late = lax.optimization_barrier((near, y_late))
    (end_4,) = local_call(combine, window, place, end_2, near)
    place_3, end_4 = lax.optimization_barrier((place_2, end_4))
    last_4, earlier_4 = later(end_4, 1), later(end_4, 5)
    z_own, z_give = run_projection(project_second, place_3, pieces, weights_2, 512, kinds[:1] * 2)
    last_4, earlier_4, z_give = lax.optimization_barrier((last_4, earlier_4, z_give))
    z_got = sibling(z_give)
    sorted_rows = local_call(
        carry,
        [SHAPE((ROWS, CH), BF)] * NY,
        place,
        bc_conv,
        running,
        local,
        y_early,
        y_late,
        z_own,
        z_got,
        last_4,
        earlier_4,
        scratch=[pltpu.VMEM((T, CH), BF), pltpu.VMEM((NY, ROWS, CH), BF)],
    )
    hidden, give = run_out(place, gain, w_out, over_y(sorted_rows), True)
    got = sibling(give)
    (kept,) = run_out(place, gain, w_out, [hidden], False)
    block = (ROWS, FEAT)
    far, ahead, behind, stays = local_call(
        merge, [SHAPE(block, kind) for kind in (BF, BF, BF, F32)], place, kept, got
    )
    (out,) = local_call(
        finish,
        [SHAPE(block, BF)],
        place,
        stays,
        shifted(ahead, "x", 1),
        shifted(behind, "x", -1),
        shifted(far, "x", 2),
    )
    return out


def solution(mesh):
    fine = Mesh(mesh.devices.reshape(NZ, NY, NX, NC), ("z", "y", "x", "c"))
    seq, head = ("z", "y"), ("x", "c")
    return jax.shard_map(
        on_device,
        mesh=fine,
        in_specs=(
            P(seq, head),
            P(seq, None, head),
            P(seq, None, head),
            P(seq, head),
            P(None, head),
            P(None, None, head),
            P(head),
            P(head),
            P(head),
            P(head),
            P(head, None),
        ),
        out_specs=P(seq, head),
        check_vma=False,
    )
```

```python
import functools
import jax
import jax.numpy as jnp
from jax import lax
from jax.experimental import pallas as pl
from jax.experimental.pallas import tpu as pltpu
from jax.sharding import Mesh, PartitionSpec as P

EPSILON = 1e-05
BF = jnp.bfloat16
F32 = jnp.float32
MIB = 1024 * 1024

NZ, NY, NX, NC = 8, 4, 4, 2
ROWS = 512
HALF = ROWS // 2
FEAT = 512
D = 4096
T = ROWS * NY
CH = 256
HD = 4
PS = 64
N = 128
Q = 128
NB = T // Q
W1 = 384
OFFSETS = (0, -1, 1, 2)
ALL = ("z", "y", "x", "c")
VMEM = pl.BlockSpec(memory_space=pltpu.VMEM)
SMEM = pl.BlockSpec(memory_space=pltpu.SMEM)
ANY = pl.BlockSpec(memory_space=pl.ANY)
HBM = pl.BlockSpec(memory_space=pltpu.HBM)
SHAPE = jax.ShapeDtypeStruct
SMALL = pl.CostEstimate(flops=1000, bytes_accessed=1000, transcendentals=0)


def shifted(value, axis, distance):
    n = lax.axis_size(axis)
    return lax.ppermute(value, axis, [(i, (i + distance) % n) for i in range(n)])


def sibling(value):
    return lax.ppermute(value, "c", [(0, 1), (1, 0)])


def routed(value, target):
    pairs = []
    for source in range(NZ * NY * NX * NC):
        rest, c = divmod(source, NC)
        rest, x = divmod(rest, NX)
        z, y = divmod(rest, NY)
        goal = target(z, y, x, c)
        if goal is not None:
            z, y, x, c = goal
            pairs.append((source, ((z * NY + y) * NX + x) * NC + c))
    return lax.ppermute(value, ALL, pairs)


def crossed(value, along_x, distance):
    def target(z, y, x, c):
        if c == along_x:
            return z, y, (x + distance) % NX, c
        return z, (y + distance) % NY, x, c

    return routed(value, target)


def over_y(v):
    return [v[0], shifted(v[1], "y", 1), shifted(v[3], "y", -1), shifted(v[2], "y", 2)]


def half_rows(tokens, c):
    early, late = tokens[:HALF], tokens[HALF:]
    got = sibling(jnp.where(c == 0, late, early))
    return jnp.where(
        c == 0,
        jnp.concatenate([early, got], axis=1),
        jnp.concatenate([got, late], axis=1),
    )


def gather_tokens(mine, first, second):
    mine, first = lax.optimization_barrier((mine, first))
    right, left = crossed(mine, 0, 1), crossed(mine, 0, -1)
    first = over_y(first)
    right, left, first, second = lax.optimization_barrier((right, left, first, second))
    middle = HALF // 2
    opposite = [crossed(right[:middle], 0, 1), crossed(left[middle:], 0, -1)]
    second = over_y(second)
    near = jnp.stack([mine, right])
    away = jnp.stack([left, jnp.concatenate(opposite)])
    near, away, second = lax.optimization_barrier((near, away, second))
    near_r, away_l = crossed(near, 1, 1), crossed(away, 1, -1)
    near_l, away_r = crossed(near, 1, -1), crossed(away, 1, 1)
    near_2, away_2 = crossed(near_r, 1, 1), crossed(away_l, 1, -1)
    return [near, away, near_r, away_r, near_l, away_l, near_2, away_2], first, second


def place_of(place, i, j):
    x, y, c = place[0], place[1], place[2]
    first, second = OFFSETS[i] + 4, OFFSETS[j] + 4
    dx = jnp.where(c == 0, first, second)
    dy = jnp.where(c == 0, second, first)
    return lax.rem(y + dy, NY), lax.rem(x + dx, NX)


def load_operands(place, pieces, weights, columns, tok, w, sems):
    x, y, c = place[0], place[1], place[2]

    def fetch(i, j, block):
        yy, _ = place_of(place, i, j)
        pltpu.make_async_copy(
            pieces[j * 2 + i // 2].at[i % 2],
            tok.at[block, pl.ds(pl.multiple_of(yy * HALF, HALF), HALF), :],
            sems.at[block],
        ).start()

    for block, offset in enumerate(OFFSETS):
        first = lax.rem(x + (offset + NX), NX) * 2
        for core, lane, width, to in columns:
            for rel, d in enumerate(OFFSETS):
                yy = lax.rem(y + (d + NY), NY)
                pltpu.make_async_copy(
                    weights.at[pl.ds(first, 2), 1 - c if core else c, rel, :, pl.ds(lane, width)],
                    w.at[block, :, yy, :, pl.ds(to, width)],
                    sems.at[4 + block],
                ).start()

        @pl.when(c == 0)
        def _():
            for j in range(4):
                fetch(block, j, block)

        @pl.when(c == 1)
        def _():
            for i in range(4):
                fetch(i, block, block)


def products(tok, w, acc, sems):
    for block in range(4):
        pltpu.make_async_copy(tok.at[block], tok.at[block], sems.at[block]).wait()
        pltpu.make_async_copy(w.at[block], w.at[block], sems.at[4 + block]).wait()
        for k in range(NY):
            rows = slice(k * HALF, (k + 1) * HALF)
            part = jnp.dot(
                tok[block, rows, :],
                w[block].reshape(D // NX, w.shape[-1]),
                preferred_element_type=F32,
            )
            if block == 0:
                acc[rows, :] = part
            elif block < 3:
                acc[rows, :] += part
            else:
                yield k, acc[rows, :] + part


def silu(v):
    return v / (1.0 + jnp.exp(-v))


GATES = [(0, 0, CH, 0), (1, 0, CH, CH)]
SIDES = [(0, CH, 128, 2 * CH), (1, CH, 128, 2 * CH + 128)]


def project_first(place, *refs):
    pieces, weights = refs[:8], refs[8]
    outs, (tok, w, acc, sems) = refs[9:17], refs[17:]
    load_operands(place, pieces, weights, GATES + SIDES, tok, w, sems)
    for k, total in products(tok, w, acc, sems):
        rows = slice(k * HALF, (k + 1) * HALF)
        for core in range(2):
            x_ref, bc_ref, dt_ref, tail = outs[4 * core : 4 * core + 4]
            x = total[:, core * CH : (core + 1) * CH].astype(BF)
            start = 2 * CH + 128 * core
            side = total[:, start : start + 128].T
            x_ref[k] = x
            bc_ref[:, rows] = side[:64].astype(BF)
            dt_ref[:, rows] = side[64:72]
            if k == NY - 1:
                tail[:64, :] = side[:64, HALF - Q :].astype(BF)
                tail[64:80, :] = x[HALF - 16 :, :Q]
                tail[80:, :] = x[HALF - 16 :, Q:]


def project_second(place, *refs):
    pieces, weights = refs[:8], refs[8]
    outs, (tok, w, acc, sems) = refs[9:11], refs[11:]
    load_operands(place, pieces, weights, GATES, tok, w, sems)
    for k, total in products(tok, w, acc, sems):
        for core in range(2):
            outs[core][k] = total[:, core * CH : (core + 1) * CH].astype(BF)


def run_projection(kernel, place, pieces, weights, width, outs):
    return pl.pallas_call(
        kernel,
        out_shape=outs,
        in_specs=[SMEM] + [ANY] * 8 + [HBM],
        out_specs=[VMEM] * len(outs),
        scratch_shapes=[
            pltpu.VMEM((NX, NY * HALF, D // NX), BF),
            pltpu.VMEM((NX, NZ // NX, NY, 128, width), BF),
            pltpu.VMEM((NY * HALF, width), F32),
            pltpu.SemaphoreType.DMA((8,)),
        ],
        compiler_params=pltpu.CompilerParams(vmem_limit_bytes=52 * MIB),
        cost_estimate=SMALL,
    )(place, *pieces, weights)


def local_call(kernel, outs, *args, scratch=(), limit=20):
    return pl.pallas_call(
        kernel,
        out_shape=outs,
        in_specs=[SMEM] + [VMEM] * (len(args) - 1),
        out_specs=[VMEM] * len(outs),
        scratch_shapes=list(scratch),
        compiler_params=pltpu.CompilerParams(vmem_limit_bytes=limit * MIB),
        cost_estimate=SMALL,
    )(*args)


def half_start(place, k, other):
    half = 1 - place[2] if other else place[2]
    return pl.multiple_of(k * ROWS + half * HALF, HALF)


def conv_and_rates(
    place, own, other, halo_1, halo_2, taps, dt_own, dt_other, bias, a_log, *rest
):
    out_ref, run_ref, step_ref, full, raw_full = rest
    halo = (halo_1[64:, :] + halo_2[64:, :]).astype(F32)
    full[:16, :Q] = halo[:16]
    full[:16, Q:] = halo[16:]
    for k in range(NY):
        full[pl.ds(half_start(place, k, False) + 16, HALF), :] = own[k].astype(F32)
        full[pl.ds(half_start(place, k, True) + 16, HALF), :] = other[k].astype(F32)
        at = slice(k * HALF, (k + 1) * HALF)
        raw_full[:, pl.ds(half_start(place, k, False), HALF)] = dt_own[:, at]
        raw_full[:, pl.ds(half_start(place, k, True), HALF)] = dt_other[:, at]
    for block in range(NB):
        total = taps[3:4, :] * full[block * Q + 16 : block * Q + 16 + Q, :]
        for back in (1, 2, 3):
            start = block * Q + 16 - back
            total = total + taps[3 - back : 4 - back, :] * full[start : start + Q, :]
        out_ref[block * Q : (block + 1) * Q, :] = silu(total).astype(BF)
    lane = lax.broadcasted_iota(jnp.int32, (8, Q), 1)
    factor = -jnp.exp(a_log[...])
    for block in range(NB):
        at = slice(block * Q, (block + 1) * Q)
        raw = raw_full[:, at] + bias[...]
        step = jnp.maximum(raw, 0.0) + jnp.log1p(jnp.exp(-jnp.abs(raw)))
        running = step * factor
        for distance in (1, 2, 4, 8, 16, 32, 64):
            running = running + jnp.where(lane < distance, 0.0, pltpu.roll(running, distance, 1))
        run_ref[:, at] = running
        step_ref[:, at] = step


def convolve_side(place, own, other, halo_1, halo_2, taps, out_ref, full):
    full[:, :Q] = (halo_1[:64, :] + halo_2[:64, :]).astype(F32)
    for k in range(NY):
        at = slice(k * HALF, (k + 1) * HALF)
        full[:, pl.ds(pl.multiple_of(half_start(place, k, False) + Q, Q), HALF)] = own[
            :, at
        ].astype(F32)
        full[:, pl.ds(pl.multiple_of(half_start(place, k, True) + Q, Q), HALF)] = other[
            :, at
        ].astype(F32)
    lane = lax.broadcasted_iota(jnp.int32, (64, Q), 1)
    before = [pltpu.roll(full[:, :Q], back, 1) for back in (1, 2, 3)]
    for block in range(NB):
        now = full[:, (block + 1) * Q : (block + 2) * Q]
        turned = [pltpu.roll(now, back, 1) for back in (1, 2, 3)]
        total = taps[:, 3:4] * now
        for back in (1, 2, 3):
            moved = jnp.where(lane < back, before[back - 1], turned[back - 1])
            total = total + taps[:, 3 - back : 4 - back] * moved
        out_ref[:, block * Q : (block + 1) * Q] = silu(total).astype(BF)
        before = turned


def apart(value):
    lane = lax.broadcasted_iota(jnp.int32, value.shape, 1)
    zero = jnp.zeros_like(value)
    return jnp.concatenate(
        [jnp.where(lane < PS, value, zero), jnp.where(lane < PS, zero, value)], axis=0
    )


def of_pair(rows, pair):
    lane = lax.broadcasted_iota(jnp.int32, (1, Q), 1)
    return jnp.where(lane < PS, rows[2 * pair : 2 * pair + 1], rows[2 * pair + 1 : 2 * pair + 2])


def decay_rows(decay):
    wide = jnp.broadcast_to(decay, (8, CH))
    high = wide.astype(BF)
    return jnp.concatenate([high, (wide - high.astype(F32)).astype(BF)], axis=0)


def decay_of(ref):
    return ref[N : N + 1, :].astype(F32) + ref[N + 8 : N + 9, :].astype(F32)


def chained(arrived):
    state, weight = arrived[0][:N, :].astype(F32), decay_of(arrived[0])
    for ref in arrived[1:]:
        state = state + weight * ref[:N, :].astype(F32)
        weight = weight * decay_of(ref)
    return state, weight


def combine(place, end, first, second, third, out_ref):
    state, _ = chained((first, second, third))
    out_ref[...] = (end[:N, :].astype(F32) + decay_of(end) * state).astype(BF)


def states(place, x_ref, run_ref, step_ref, *rest):
    parts, (bc_ref, local_ref, end_ref) = rest[:4], rest[4:]
    for part, d in zip(parts, OFFSETS):
        yy = lax.rem(place[1] + (d + NY), NY)
        bc_ref[pl.ds(pl.multiple_of(yy * 64, 64), 64), :] = part[...]
    state = [jnp.zeros((N, Q), F32) for _ in range(HD // 2)]
    total_rate = jnp.zeros((8, Q), F32)
    for block in range(NB):
        at = slice(block * Q, (block + 1) * Q)
        b = bc_ref[:N, at].astype(F32)
        running, step = run_ref[:, at], step_ref[:, at]
        last = running[:, Q - 1 : Q]
        weight = jnp.exp(last - running) * step
        decay = jnp.exp(last)
        for pair in range(HD // 2):
            lanes = slice(pair * Q, (pair + 1) * Q)
            local_ref[block, :, lanes] = state[pair].astype(BF)
            scaled = [(b * weight[h : h + 1, :]).astype(BF) for h in (2 * pair, 2 * pair + 1)]
            increment = jnp.dot(
                jnp.concatenate(scaled, axis=1),
                apart(x_ref[at, lanes]),
                preferred_element_type=F32,
            )
            state[pair] = of_pair(decay, pair) * state[pair] + increment
        total_rate = total_rate + last
    for pair in range(HD // 2):
        end_ref[:N, pair * Q : (pair + 1) * Q] = state[pair].astype(BF)
    end_ref[N:, :] = decay_rows(over_channels(jnp.exp(total_rate)))


def within(place, x_ref, bc_ref, run_ref, step_ref, skip, y_ref):
    below = lax.broadcasted_iota(jnp.int32, (Q, Q), 0) >= lax.broadcasted_iota(
        jnp.int32, (Q, Q), 1
    )
    for block in range(NB):
        at = slice(block * Q, (block + 1) * Q)
        running, step = run_ref[:, at], step_ref[:, at]
        columns = running.T
        scores = lax.dot_general(
            bc_ref[N:, at], bc_ref[:N, at], (((0,), (0,)), ((), ())), preferred_element_type=F32
        )
        for pair in range(HD // 2):
            mixing = []
            for h in (2 * pair, 2 * pair + 1):
                spread = jnp.where(below, columns[:, h : h + 1] - running[h : h + 1, :], -1e30)
                mixing.append((jnp.exp(spread) * step[h : h + 1, :] * scores).astype(BF))
            lanes = slice(pair * Q, (pair + 1) * Q)
            value = x_ref[at, lanes]
            y = jnp.dot(
                jnp.concatenate(mixing, axis=1), apart(value), preferred_element_type=F32
            )
            y_ref[at, lanes] = y + skip[:, lanes] * value.astype(F32)


def per_head(columns):
    return jnp.concatenate(
        [jnp.broadcast_to(columns[:, h : h + 1], (columns.shape[0], PS)) for h in range(HD)],
        axis=1,
    )


def over_channels(rows):
    return jnp.concatenate([rows[h : h + 1, :PS] for h in range(HD)], axis=1)


def carry(place, bc_ref, run_ref, local_ref, y_ref, z_own, z_other, *rest):
    arrived, outs, (z_full, sorted_rows) = rest[:4], rest[4:8], rest[8:]
    for k in range(NY):
        z_full[pl.ds(half_start(place, k, False), HALF), :] = z_own[k]
        z_full[pl.ds(half_start(place, k, True), HALF), :] = z_other[k]
    state, weight = chained(arrived[:3])
    state = state + weight * arrived[3][...].astype(F32)
    before = jnp.ones((1, CH), F32)
    for block in range(NB):
        at = slice(block * Q, (block + 1) * Q)
        running = run_ref[:, at]
        full = (local_ref[block].astype(F32) + before * state).astype(BF)
        carried = lax.dot_general(
            bc_ref[N:, at], full, (((0,), (0,)), ((), ())), preferred_element_type=F32
        )
        grown = jnp.exp(running)
        y = y_ref[at, :] + per_head(grown.T) * carried
        gate = silu(z_full[at, :].astype(F32))
        rel = lax.rem(block // 4 + NY - place[1], NY)
        part = block % 4
        sorted_rows[rel, part * Q : (part + 1) * Q, :] = (y * gate).astype(BF)
        last = jnp.broadcast_to(grown[:, Q - 1 : Q], (8, Q))
        before = before * over_channels(last)
    for rel in range(NY):
        outs[rel][...] = sorted_rows[rel]


def project_far(place, gain, w_ref, *rest):
    parts, (hidden, give, keep) = rest[:NY], rest[NY:]

    @pl.when(pl.program_id(0) == 0)
    def _():
        total = jnp.zeros((ROWS, 1), F32)
        for ref in parts:
            value = ref[...].astype(F32)
            total = total + jnp.sum(value * value, axis=1, keepdims=True)
        scale = lax.rsqrt(total / (NY * CH) + EPSILON)
        for ref, d in zip(parts, OFFSETS):
            yy = lax.rem(place[1] + (d + NY), NY)
            lanes = pl.ds(pl.multiple_of(yy * CH, CH), CH)
            hidden[:, lanes] = (ref[...].astype(F32) * scale * gain[:, lanes]).astype(BF)

    acc = jnp.dot(hidden[...], w_ref[...], preferred_element_type=F32).astype(BF)

    @pl.when(pl.program_id(0) == 0)
    def _():
        give[...] = acc

    @pl.when(pl.program_id(0) == 1)
    def _():
        keep[...] = acc


def project_rest(place, w_ref, hidden, out_ref):
    out_ref[...] = jnp.dot(hidden[...], w_ref[...], preferred_element_type=F32).astype(BF)


def output_call(kernel, place, columns, steps, more, w_out, parts, outs, specs):
    whole = lambda v: pl.BlockSpec(v.shape, lambda i, p: (0,) * v.ndim)
    return pl.pallas_call(
        kernel,
        out_shape=outs,
        grid_spec=pltpu.PrefetchScalarGridSpec(
            num_scalar_prefetch=1,
            grid=(steps,),
            in_specs=[whole(v) for v in more]
            + [pl.BlockSpec((NY * CH, FEAT), columns)]
            + [whole(v) for v in parts],
            out_specs=specs,
        ),
        compiler_params=pltpu.CompilerParams(vmem_limit_bytes=52 * MIB),
        cost_estimate=SMALL,
    )(place, *more, w_out, *parts)


def run_far(place, gain, w_out, parts):
    columns = lambda i, p: (0, lax.rem(p[0] + 2, NX) * NC + jnp.where(i == 0, 1 - p[2], p[2]))
    shapes = [(ROWS, NY * CH), (ROWS, FEAT), (ROWS, FEAT)]
    return output_call(
        project_far,
        place,
        columns,
        2,
        [gain],
        w_out,
        parts,
        [SHAPE(shape, BF) for shape in shapes],
        [pl.BlockSpec(shape, lambda i, p: (0, 0)) for shape in shapes],
    )


def run_rest(place, w_out, hidden, other):
    def columns(i, p):
        ahead = jnp.where(i == 0, 1, jnp.where(i == 1, 3, 0))
        return 0, lax.rem(p[0] + ahead, NX) * NC + (1 - p[2] if other else p[2])

    return output_call(
        project_rest,
        place,
        columns,
        3,
        [],
        w_out,
        [hidden],
        [SHAPE((ROWS, 3 * FEAT), BF)],
        [pl.BlockSpec((ROWS, FEAT), lambda i, p: (0, i))],
    )[0]


def merge(place, kept, got, *outs):
    for k, ref in enumerate(outs):
        at = slice(k * FEAT, (k + 1) * FEAT)
        ref[...] = (kept[:, at].astype(F32) + got[:, at].astype(F32)).astype(ref.dtype)


def finish(place, own, first, second, third, out_ref):
    total = own[...] + first[...].astype(F32)
    out_ref[...] = (total + second[...].astype(F32) + third[...].astype(F32)).astype(BF)


def on_device(tokens, w_zx, w_bc, w_dt, conv_x, conv_bc, dt_bias, a_log, d_skip, norm_gain, w_out):
    y, c = lax.axis_index("y"), lax.axis_index("c")
    place = jnp.stack([lax.axis_index("x"), y, c, lax.axis_index("z")]).astype(jnp.int32)
    rows = w_zx.shape[0]

    def quarter(value, distance, width, dim=1):
        start = lax.rem(y + (distance + NY), NY) * width
        return lax.dynamic_slice_in_dim(value, start, width, dim)

    def for_y(distance):
        zero = jnp.zeros((rows, W1 - CH - 64 - HD), BF)
        return jnp.concatenate(
            [
                quarter(w_zx[:, 1], distance, CH),
                quarter(w_bc.reshape(rows, -1), distance, 64),
                quarter(w_dt, distance, HD),
                zero,
            ],
            axis=1,
        )

    mine = half_rows(tokens, c)
    gate = lambda d: quarter(w_zx[:, 0], d, CH)
    pieces, first, second = gather_tokens(
        mine, [for_y(d) for d in range(NY)], [gate(d) for d in range(NY)]
    )
    weights_1 = lax.all_gather(jnp.concatenate(first), ("z", "c"), axis=0, tiled=True)
    weights_1 = weights_1.reshape(NZ, NC, NY, rows, W1)
    weights_2 = lax.all_gather(jnp.concatenate(second), ("z", "c"), axis=0, tiled=True)
    weights_2 = weights_2.reshape(NZ, NC, NY, rows, CH)

    taps_x = quarter(conv_x, 0, CH).astype(F32)
    taps_bc = quarter(conv_bc.reshape(4, -1), 0, 64).T.astype(F32)
    column = lambda v: jnp.pad(quarter(v, 0, HD, 0), (0, 8 - HD)).reshape(8, 1)
    skip = jnp.repeat(quarter(d_skip, 0, HD, 0), PS).reshape(1, CH)
    gain = norm_gain.astype(F32).reshape(1, -1)

    kinds = [
        SHAPE((NY, HALF, CH), BF),
        SHAPE((64, NY * HALF), BF),
        SHAPE((8, NY * HALF), F32),
        SHAPE((96, Q), BF),
    ]
    first_outs = run_projection(project_first, place, pieces, weights_1, 768, kinds * 2)
    x_own, bc_own, dt_own, tail_own = first_outs[:4]
    x_give, bc_give, dt_give, tail_give = first_outs[4:]
    bc_got = sibling(bc_give)
    halo_own = routed(
        tail_own, lambda z, y, x, c: (z + 1, y, x, 1) if z + 1 < NZ and c == 1 else None
    )
    halo_give = routed(
        tail_give, lambda z, y, x, c: (z + 1, y, x, 0) if z + 1 < NZ and c == 1 else None
    )
    x_got, dt_got = sibling(x_give), sibling(dt_give)
    (bc,) = local_call(
        convolve_side,
        [SHAPE((64, T), BF)],
        place,
        bc_own,
        bc_got,
        halo_own,
        halo_give,
        taps_bc,
        scratch=[pltpu.VMEM((64, T + Q), F32)],
    )
    bc_parts = [bc] + [shifted(bc, "y", d) for d in (1, -1, 2)]
    x_conv, running, step = local_call(
        conv_and_rates,
        [SHAPE((T, CH), BF), SHAPE((8, T), F32), SHAPE((8, T), F32)],
        place,
        x_own,
        x_got,
        halo_own,
        halo_give,
        taps_x,
        dt_own,
        dt_got,
        column(dt_bias),
        column(a_log),
        scratch=[pltpu.VMEM((T + 16, CH), F32), pltpu.VMEM((8, T), F32)],
    )
    bc_conv, local, end = local_call(
        states,
        [SHAPE((2 * N, T), BF), SHAPE((NB, N, CH), BF), SHAPE((N + 16, CH), BF)],
        place,
        x_conv,
        running,
        step,
        *bc_parts,
    )
    later = lambda v, d: lax.ppermute(v, "z", [(i, i + d) for i in range(NZ - d)])
    near = [later(end, d) for d in (1, 2, 3)]
    place_2, end = lax.optimization_barrier((place, end))
    z_own, z_give = run_projection(project_second, place_2, pieces, weights_2, 512, kinds[:1] * 2)
    near, z_give = lax.optimization_barrier((near, z_give))
    z_got = sibling(z_give)
    (window,) = local_call(combine, [SHAPE((N, CH), BF)], place, end, *near)
    place_3, window = lax.optimization_barrier((place, window))
    far_end = later(window, 4)
    (y_within,) = local_call(
        within, [SHAPE((T, CH), F32)], place_3, x_conv, bc_conv, running, step, skip
    )
    sorted_rows = local_call(
        carry,
        [SHAPE((ROWS, CH), BF)] * NY,
        place,
        bc_conv,
        running,
        local,
        y_within,
        z_own,
        z_got,
        *near,
        far_end,
        scratch=[pltpu.VMEM((T, CH), BF), pltpu.VMEM((NY, ROWS, CH), BF)],
    )
    block = (ROWS, FEAT)
    hidden, far_give, far_keep = run_far(place, gain, w_out, over_y(sorted_rows))
    far_got = sibling(far_give)
    (far,) = local_call(merge, [SHAPE(block, BF)], place, far_keep, far_got)
    place_4, far = lax.optimization_barrier((place, far))
    far_arrived = shifted(far, "x", 2)
    rest_give = run_rest(place_4, w_out, hidden, True)
    rest_got = sibling(rest_give)
    rest_keep = run_rest(place_4, w_out, hidden, False)
    far_arrived, rest_got = lax.optimization_barrier((far_arrived, rest_got))
    ahead, behind, stays = local_call(
        merge, [SHAPE(block, kind) for kind in (BF, BF, F32)], place, rest_keep, rest_got
    )
    (out,) = local_call(
        finish,
        [SHAPE(block, BF)],
        place,
        stays,
        shifted(ahead, "x", 1),
        shifted(behind, "x", -1),
        far_arrived,
    )
    return out


def solution(mesh):
    fine = Mesh(mesh.devices.reshape(NZ, NY, NX, NC), ("z", "y", "x", "c"))
    seq, head = ("z", "y"), ("x", "c")
    return jax.shard_map(
        on_device,
        mesh=fine,
        in_specs=(
            P(seq, head),
            P(seq, None, head),
            P(seq, None, head),
            P(seq, head),
            P(None, head),
            P(None, None, head),
            P(head),
            P(head),
            P(head),
            P(head),
            P(head, None),
        ),
        out_specs=P(seq, head),
        check_vma=False,
    )
```

```python
import functools
import jax
import jax.numpy as jnp
from jax import lax
from jax.experimental import pallas as pl
from jax.experimental.pallas import tpu as pltpu
from jax.sharding import Mesh, PartitionSpec as P

EPSILON = 1e-05
BF = jnp.bfloat16
F32 = jnp.float32
MIB = 1024 * 1024

NZ, NY, NX, NC = 8, 4, 4, 2
ROWS = 512
HALF = ROWS // 2
FEAT = 512
D = 4096
T = ROWS * NY
CH = 256
HD = 4
PS = 64
N = 128
Q = 128
NB = T // Q
W1 = 384
OFFSETS = (0, -1, 1, 2)
ALL = ("z", "y", "x", "c")
VMEM = pl.BlockSpec(memory_space=pltpu.VMEM)
SMEM = pl.BlockSpec(memory_space=pltpu.SMEM)
ANY = pl.BlockSpec(memory_space=pl.ANY)
HBM = pl.BlockSpec(memory_space=pltpu.HBM)
SHAPE = jax.ShapeDtypeStruct
SMALL = pl.CostEstimate(flops=1000, bytes_accessed=1000, transcendentals=0)


def shifted(value, axis, distance):
    n = lax.axis_size(axis)
    return lax.ppermute(value, axis, [(i, (i + distance) % n) for i in range(n)])


def sibling(value):
    return lax.ppermute(value, "c", [(0, 1), (1, 0)])


def routed(value, target):
    pairs = []
    for source in range(NZ * NY * NX * NC):
        rest, c = divmod(source, NC)
        rest, x = divmod(rest, NX)
        z, y = divmod(rest, NY)
        goal = target(z, y, x, c)
        if goal is not None:
            z, y, x, c = goal
            pairs.append((source, ((z * NY + y) * NX + x) * NC + c))
    return lax.ppermute(value, ALL, pairs)


def crossed(value, along_x, distance):
    def target(z, y, x, c):
        if c == along_x:
            return z, y, (x + distance) % NX, c
        return z, (y + distance) % NY, x, c

    return routed(value, target)


def over_y(v):
    return [v[0], shifted(v[1], "y", 1), shifted(v[3], "y", -1), shifted(v[2], "y", 2)]


def half_rows(tokens, c):
    early, late = tokens[:HALF], tokens[HALF:]
    got = sibling(jnp.where(c == 0, late, early))
    return jnp.where(
        c == 0,
        jnp.concatenate([early, got], axis=1),
        jnp.concatenate([got, late], axis=1),
    )


def gather_tokens(mine, first, second):
    mine, first = lax.optimization_barrier((mine, first))
    right, left = crossed(mine, 0, 1), crossed(mine, 0, -1)
    first = over_y(first)
    right, left, first, second = lax.optimization_barrier((right, left, first, second))
    middle = HALF // 2
    opposite = [crossed(right[:middle], 0, 1), crossed(left[middle:], 0, -1)]
    second = over_y(second)
    near = jnp.stack([mine, right])
    away = jnp.stack([left, jnp.concatenate(opposite)])
    near, away, second = lax.optimization_barrier((near, away, second))
    near_r, away_l = crossed(near, 1, 1), crossed(away, 1, -1)
    near_l, away_r = crossed(near, 1, -1), crossed(away, 1, 1)
    near_2, away_2 = crossed(near_r, 1, 1), crossed(away_l, 1, -1)
    return [near, away, near_r, away_r, near_l, away_l, near_2, away_2], first, second


def place_of(place, i, j):
    x, y, c = place[0], place[1], place[2]
    first, second = OFFSETS[i] + 4, OFFSETS[j] + 4
    dx = jnp.where(c == 0, first, second)
    dy = jnp.where(c == 0, second, first)
    return lax.rem(y + dy, NY), lax.rem(x + dx, NX)


def load_operands(place, pieces, weights, columns, tok, w, sems):
    x, y, c = place[0], place[1], place[2]

    def fetch(i, j, block):
        yy, _ = place_of(place, i, j)
        pltpu.make_async_copy(
            pieces[j * 2 + i // 2].at[i % 2],
            tok.at[block, pl.ds(pl.multiple_of(yy * HALF, HALF), HALF), :],
            sems.at[block],
        ).start()

    for block, offset in enumerate(OFFSETS):
        first = lax.rem(x + (offset + NX), NX) * 2
        for core, lane, width, to in columns:
            for rel, d in enumerate(OFFSETS):
                yy = lax.rem(y + (d + NY), NY)
                pltpu.make_async_copy(
                    weights.at[pl.ds(first, 2), 1 - c if core else c, rel, :, pl.ds(lane, width)],
                    w.at[block, :, yy, :, pl.ds(to, width)],
                    sems.at[4 + block],
                ).start()

        @pl.when(c == 0)
        def _():
            for j in range(4):
                fetch(block, j, block)

        @pl.when(c == 1)
        def _():
            for i in range(4):
                fetch(i, block, block)


def products(tok, w, acc, sems):
    for block in range(4):
        pltpu.make_async_copy(tok.at[block], tok.at[block], sems.at[block]).wait()
        pltpu.make_async_copy(w.at[block], w.at[block], sems.at[4 + block]).wait()
        for k in range(NY):
            rows = slice(k * HALF, (k + 1) * HALF)
            part = jnp.dot(
                tok[block, rows, :],
                w[block].reshape(D // NX, w.shape[-1]),
                preferred_element_type=F32,
            )
            if block == 0:
                acc[rows, :] = part
            elif block < 3:
                acc[rows, :] += part
            else:
                yield k, acc[rows, :] + part


def silu(v):
    return v / (1.0 + jnp.exp(-v))


GATES = [(0, 0, CH, 0), (1, 0, CH, CH)]
SIDES = [(0, CH, 128, 2 * CH), (1, CH, 128, 2 * CH + 128)]


def project_first(place, *refs):
    pieces, weights = refs[:8], refs[8]
    outs, (tok, w, acc, sems) = refs[9:17], refs[17:]
    load_operands(place, pieces, weights, GATES + SIDES, tok, w, sems)
    for k, total in products(tok, w, acc, sems):
        rows = slice(k * HALF, (k + 1) * HALF)
        for core in range(2):
            x_ref, bc_ref, dt_ref, tail = outs[4 * core : 4 * core + 4]
            x = total[:, core * CH : (core + 1) * CH].astype(BF)
            start = 2 * CH + 128 * core
            side = total[:, start : start + 128].T
            x_ref[k] = x
            bc_ref[:, rows] = side[:64].astype(BF)
            dt_ref[:, rows] = side[64:72]
            if k == NY - 1:
                tail[:64, :] = side[:64, HALF - Q :].astype(BF)
                tail[64:80, :] = x[HALF - 16 :, :Q]
                tail[80:, :] = x[HALF - 16 :, Q:]


def project_second(place, *refs):
    pieces, weights = refs[:8], refs[8]
    outs, (tok, w, acc, sems) = refs[9:11], refs[11:]
    load_operands(place, pieces, weights, GATES, tok, w, sems)
    for k, total in products(tok, w, acc, sems):
        for core in range(2):
            outs[core][k] = total[:, core * CH : (core + 1) * CH].astype(BF)


def run_projection(kernel, place, pieces, weights, width, outs):
    return pl.pallas_call(
        kernel,
        out_shape=outs,
        in_specs=[SMEM] + [ANY] * 8 + [HBM],
        out_specs=[VMEM] * len(outs),
        scratch_shapes=[
            pltpu.VMEM((NX, NY * HALF, D // NX), BF),
            pltpu.VMEM((NX, NZ // NX, NY, 128, width), BF),
            pltpu.VMEM((NY * HALF, width), F32),
            pltpu.SemaphoreType.DMA((8,)),
        ],
        compiler_params=pltpu.CompilerParams(vmem_limit_bytes=52 * MIB),
        cost_estimate=SMALL,
    )(place, *pieces, weights)


def local_call(kernel, outs, *args, scratch=(), limit=20, cost=SMALL):
    return pl.pallas_call(
        kernel,
        out_shape=outs,
        in_specs=[SMEM] + [VMEM] * (len(args) - 1),
        out_specs=[VMEM] * len(outs),
        scratch_shapes=list(scratch),
        compiler_params=pltpu.CompilerParams(vmem_limit_bytes=limit * MIB),
        cost_estimate=cost,
    )(*args)


def half_start(place, k, other):
    half = 1 - place[2] if other else place[2]
    return pl.multiple_of(k * ROWS + half * HALF, HALF)


def conv_and_rates(
    place, own, other, halo_1, halo_2, taps, dt_own, dt_other, bias, a_log, *rest
):
    out_ref, run_ref, step_ref, full, raw_full = rest
    halo = (halo_1[64:, :] + halo_2[64:, :]).astype(F32)
    full[:16, :Q] = halo[:16]
    full[:16, Q:] = halo[16:]
    for k in range(NY):
        full[pl.ds(half_start(place, k, False) + 16, HALF), :] = own[k].astype(F32)
        full[pl.ds(half_start(place, k, True) + 16, HALF), :] = other[k].astype(F32)
        at = slice(k * HALF, (k + 1) * HALF)
        raw_full[:, pl.ds(half_start(place, k, False), HALF)] = dt_own[:, at]
        raw_full[:, pl.ds(half_start(place, k, True), HALF)] = dt_other[:, at]
    for block in range(NB):
        total = taps[3:4, :] * full[block * Q + 16 : block * Q + 16 + Q, :]
        for back in (1, 2, 3):
            start = block * Q + 16 - back
            total = total + taps[3 - back : 4 - back, :] * full[start : start + Q, :]
        out_ref[block * Q : (block + 1) * Q, :] = silu(total).astype(BF)
    lane = lax.broadcasted_iota(jnp.int32, (8, Q), 1)
    factor = -jnp.exp(a_log[...])
    for block in range(NB):
        at = slice(block * Q, (block + 1) * Q)
        raw = raw_full[:, at] + bias[...]
        step = jnp.maximum(raw, 0.0) + jnp.log1p(jnp.exp(-jnp.abs(raw)))
        running = step * factor
        for distance in (1, 2, 4, 8, 16, 32, 64):
            running = running + jnp.where(lane < distance, 0.0, pltpu.roll(running, distance, 1))
        run_ref[:, at] = running
        step_ref[:, at] = step


def convolve_side(place, own, other, halo_1, halo_2, taps, b_ref, c_ref, full):
    full[:, :Q] = (halo_1[:64, :] + halo_2[:64, :]).astype(F32)
    for k in range(NY):
        at = slice(k * HALF, (k + 1) * HALF)
        full[:, pl.ds(pl.multiple_of(half_start(place, k, False) + Q, Q), HALF)] = own[
            :, at
        ].astype(F32)
        full[:, pl.ds(pl.multiple_of(half_start(place, k, True) + Q, Q), HALF)] = other[
            :, at
        ].astype(F32)
    lane = lax.broadcasted_iota(jnp.int32, (64, Q), 1)
    before = [pltpu.roll(full[:, :Q], back, 1) for back in (1, 2, 3)]
    for block in range(NB):
        now = full[:, (block + 1) * Q : (block + 2) * Q]
        turned = [pltpu.roll(now, back, 1) for back in (1, 2, 3)]
        total = taps[:, 3:4] * now
        for back in (1, 2, 3):
            moved = jnp.where(lane < back, before[back - 1], turned[back - 1])
            total = total + taps[:, 3 - back : 4 - back] * moved
        out = silu(total).astype(BF)
        b_ref[:, block * Q : (block + 1) * Q] = out[:32]
        c_ref[:, block * Q : (block + 1) * Q] = out[32:]
        before = turned


def apart(value):
    lane = lax.broadcasted_iota(jnp.int32, value.shape, 1)
    zero = jnp.zeros_like(value)
    return jnp.concatenate(
        [jnp.where(lane < PS, value, zero), jnp.where(lane < PS, zero, value)], axis=0
    )


def of_pair(rows, pair):
    lane = lax.broadcasted_iota(jnp.int32, (1, Q), 1)
    return jnp.where(lane < PS, rows[2 * pair : 2 * pair + 1], rows[2 * pair + 1 : 2 * pair + 2])


def decay_rows(decay):
    wide = jnp.broadcast_to(decay, (8, CH))
    high = wide.astype(BF)
    return jnp.concatenate([high, (wide - high.astype(F32)).astype(BF)], axis=0)


def decay_of(ref):
    return ref[N : N + 1, :].astype(F32) + ref[N + 8 : N + 9, :].astype(F32)


def chained(arrived):
    state, weight = arrived[0][:N, :].astype(F32), decay_of(arrived[0])
    for ref in arrived[1:]:
        state = state + weight * ref[:N, :].astype(F32)
        weight = weight * decay_of(ref)
    return state, weight


def combine(place, end, first, second, third, out_ref):
    state, _ = chained((first, second, third))
    out_ref[...] = (end[:N, :].astype(F32) + decay_of(end) * state).astype(BF)


def in_order(place, parts, full_ref):
    for part, d in zip(parts, OFFSETS):
        yy = lax.rem(place[1] + (d + NY), NY)
        full_ref[pl.ds(pl.multiple_of(yy * 32, 32), 32), :] = part[...]


def states(place, x_ref, run_ref, step_ref, *rest):
    parts, (b_full, local_ref, end_ref) = rest[:4], rest[4:]
    in_order(place, parts, b_full)
    state = [jnp.zeros((N, Q), F32) for _ in range(HD // 2)]
    total_rate = jnp.zeros((8, Q), F32)
    for block in range(NB):
        at = slice(block * Q, (block + 1) * Q)
        b = b_full[:, at].astype(F32)
        running, step = run_ref[:, at], step_ref[:, at]
        last = running[:, Q - 1 : Q]
        weight = jnp.exp(last - running) * step
        decay = jnp.exp(last)
        for pair in range(HD // 2):
            lanes = slice(pair * Q, (pair + 1) * Q)
            local_ref[block, :, lanes] = state[pair].astype(BF)
            scaled = [(b * weight[h : h + 1, :]).astype(BF) for h in (2 * pair, 2 * pair + 1)]
            increment = jnp.dot(
                jnp.concatenate(scaled, axis=1),
                apart(x_ref[at, lanes]),
                preferred_element_type=F32,
            )
            state[pair] = of_pair(decay, pair) * state[pair] + increment
        total_rate = total_rate + last
    for pair in range(HD // 2):
        end_ref[:N, pair * Q : (pair + 1) * Q] = state[pair].astype(BF)
    end_ref[N:, :] = decay_rows(over_channels(jnp.exp(total_rate)))


def within(place, x_ref, b_ref, run_ref, step_ref, skip, *rest):
    parts, (c_ref, y_ref) = rest[:4], rest[4:]
    in_order(place, parts, c_ref)
    below = lax.broadcasted_iota(jnp.int32, (Q, Q), 0) >= lax.broadcasted_iota(
        jnp.int32, (Q, Q), 1
    )
    for block in range(NB):
        at = slice(block * Q, (block + 1) * Q)
        running, step = run_ref[:, at], step_ref[:, at]
        columns = running.T
        scores = lax.dot_general(
            c_ref[:, at], b_ref[:, at], (((0,), (0,)), ((), ())), preferred_element_type=F32
        )
        for pair in range(HD // 2):
            mixing = []
            for h in (2 * pair, 2 * pair + 1):
                spread = jnp.where(below, columns[:, h : h + 1] - running[h : h + 1, :], -1e30)
                mixing.append((jnp.exp(spread) * step[h : h + 1, :] * scores).astype(BF))
            lanes = slice(pair * Q, (pair + 1) * Q)
            value = x_ref[at, lanes]
            y = jnp.dot(
                jnp.concatenate(mixing, axis=1), apart(value), preferred_element_type=F32
            )
            y_ref[at, lanes] = y + skip[:, lanes] * value.astype(F32)


def per_head(columns):
    return jnp.concatenate(
        [jnp.broadcast_to(columns[:, h : h + 1], (columns.shape[0], PS)) for h in range(HD)],
        axis=1,
    )


def over_channels(rows):
    return jnp.concatenate([rows[h : h + 1, :PS] for h in range(HD)], axis=1)


def carry(place, c_ref, run_ref, local_ref, y_ref, z_own, z_other, *rest):
    arrived, outs, (z_full, sorted_rows) = rest[:4], rest[4:8], rest[8:]
    for k in range(NY):
        z_full[pl.ds(half_start(place, k, False), HALF), :] = z_own[k]
        z_full[pl.ds(half_start(place, k, True), HALF), :] = z_other[k]
    state, weight = chained(arrived[:3])
    state = state + weight * arrived[3][...].astype(F32)
    before = jnp.ones((1, CH), F32)
    for block in range(NB):
        at = slice(block * Q, (block + 1) * Q)
        running = run_ref[:, at]
        full = (local_ref[block].astype(F32) + before * state).astype(BF)
        carried = lax.dot_general(
            c_ref[:, at], full, (((0,), (0,)), ((), ())), preferred_element_type=F32
        )
        grown = jnp.exp(running)
        y = y_ref[at, :] + per_head(grown.T) * carried
        gate = silu(z_full[at, :].astype(F32))
        rel = lax.rem(block // 4 + NY - place[1], NY)
        part = block % 4
        sorted_rows[rel, part * Q : (part + 1) * Q, :] = (y * gate).astype(BF)
        last = jnp.broadcast_to(grown[:, Q - 1 : Q], (8, Q))
        before = before * over_channels(last)
    for rel in range(NY):
        outs[rel][...] = sorted_rows[rel]


def project_far(place, gain, w_ref, *rest):
    parts, (hidden, give, keep) = rest[:NY], rest[NY:]

    @pl.when(pl.program_id(0) == 0)
    def _():
        total = jnp.zeros((ROWS, 1), F32)
        for ref in parts:
            value = ref[...].astype(F32)
            total = total + jnp.sum(value * value, axis=1, keepdims=True)
        scale = lax.rsqrt(total / (NY * CH) + EPSILON)
        for ref, d in zip(parts, OFFSETS):
            yy = lax.rem(place[1] + (d + NY), NY)
            lanes = pl.ds(pl.multiple_of(yy * CH, CH), CH)
            hidden[:, lanes] = (ref[...].astype(F32) * scale * gain[:, lanes]).astype(BF)

    acc = jnp.dot(hidden[...], w_ref[...], preferred_element_type=F32).astype(BF)

    @pl.when(pl.program_id(0) == 0)
    def _():
        give[...] = acc

    @pl.when(pl.program_id(0) == 1)
    def _():
        keep[...] = acc


def project_rest(place, w_ref, hidden, out_ref):
    out_ref[...] = jnp.dot(hidden[...], w_ref[...], preferred_element_type=F32).astype(BF)


def output_call(kernel, place, columns, steps, more, w_out, parts, outs, specs):
    whole = lambda v: pl.BlockSpec(v.shape, lambda i, p: (0,) * v.ndim)
    return pl.pallas_call(
        kernel,
        out_shape=outs,
        grid_spec=pltpu.PrefetchScalarGridSpec(
            num_scalar_prefetch=1,
            grid=(steps,),
            in_specs=[whole(v) for v in more]
            + [pl.BlockSpec((NY * CH, FEAT), columns)]
            + [whole(v) for v in parts],
            out_specs=specs,
        ),
        compiler_params=pltpu.CompilerParams(vmem_limit_bytes=52 * MIB),
        cost_estimate=SMALL,
    )(place, *more, w_out, *parts)


def run_far(place, gain, w_out, parts):
    columns = lambda i, p: (0, lax.rem(p[0] + 2, NX) * NC + jnp.where(i == 0, 1 - p[2], p[2]))
    shapes = [(ROWS, NY * CH), (ROWS, FEAT), (ROWS, FEAT)]
    return output_call(
        project_far,
        place,
        columns,
        2,
        [gain],
        w_out,
        parts,
        [SHAPE(shape, BF) for shape in shapes],
        [pl.BlockSpec(shape, lambda i, p: (0, 0)) for shape in shapes],
    )


def run_rest(place, w_out, hidden, other):
    def columns(i, p):
        ahead = jnp.where(i == 0, 1, jnp.where(i == 1, 3, 0))
        return 0, lax.rem(p[0] + ahead, NX) * NC + (1 - p[2] if other else p[2])

    return output_call(
        project_rest,
        place,
        columns,
        3,
        [],
        w_out,
        [hidden],
        [SHAPE((ROWS, 3 * FEAT), BF)],
        [pl.BlockSpec((ROWS, FEAT), lambda i, p: (0, i))],
    )[0]


def merge_far(place, kept, got, upper, lower):
    total = (kept[...].astype(F32) + got[...].astype(F32)).astype(BF)
    upper[...] = total[:HALF]
    lower[...] = total[HALF:]


def merge_rest(place, kept, got, from_left, from_right, ahead, behind, stays):
    for k, ref in enumerate((ahead, behind, stays)):
        at = slice(k * FEAT, (k + 1) * FEAT)
        upper = kept[:HALF, at].astype(F32) + got[:HALF, at].astype(F32)
        lower = kept[HALF:, at].astype(F32) + got[HALF:, at].astype(F32)
        if k == 0:
            upper = upper + from_left[...].astype(F32)
        if k == 1:
            lower = lower + from_right[...].astype(F32)
        ref[:HALF, :] = upper.astype(ref.dtype)
        ref[HALF:, :] = lower.astype(ref.dtype)


def finish(place, own, first, second, out_ref):
    out_ref[...] = (own[...] + first[...].astype(F32) + second[...].astype(F32)).astype(BF)


def on_device(tokens, w_zx, w_bc, w_dt, conv_x, conv_bc, dt_bias, a_log, d_skip, norm_gain, w_out):
    y, c = lax.axis_index("y"), lax.axis_index("c")
    place = jnp.stack([lax.axis_index("x"), y, c, lax.axis_index("z")]).astype(jnp.int32)
    rows = w_zx.shape[0]

    def quarter(value, distance, width, dim=1):
        start = lax.rem(y + (distance + NY), NY) * width
        return lax.dynamic_slice_in_dim(value, start, width, dim)

    def for_y(distance):
        zero = jnp.zeros((rows, W1 - CH - 64 - HD), BF)
        return jnp.concatenate(
            [
                quarter(w_zx[:, 1], distance, CH),
                quarter(w_bc[:, 0], distance, 32),
                quarter(w_bc[:, 1], distance, 32),
                quarter(w_dt, distance, HD),
                zero,
            ],
            axis=1,
        )

    mine = half_rows(tokens, c)
    gate = lambda d: quarter(w_zx[:, 0], d, CH)
    pieces, first, second = gather_tokens(
        mine, [for_y(d) for d in range(NY)], [gate(d) for d in range(NY)]
    )
    weights_1 = lax.all_gather(jnp.concatenate(first), ("z", "c"), axis=0, tiled=True)
    weights_1 = weights_1.reshape(NZ, NC, NY, rows, W1)
    weights_2 = lax.all_gather(jnp.concatenate(second), ("z", "c"), axis=0, tiled=True)
    weights_2 = weights_2.reshape(NZ, NC, NY, rows, CH)

    taps_x = quarter(conv_x, 0, CH).astype(F32)
    taps_bc = jnp.concatenate([quarter(conv_bc[:, k], 0, 32) for k in range(2)], axis=1)
    taps_bc = taps_bc.T.astype(F32)
    column = lambda v: jnp.pad(quarter(v, 0, HD, 0), (0, 8 - HD)).reshape(8, 1)
    skip = jnp.repeat(quarter(d_skip, 0, HD, 0), PS).reshape(1, CH)
    gain = norm_gain.astype(F32).reshape(1, -1)

    kinds = [
        SHAPE((NY, HALF, CH), BF),
        SHAPE((64, NY * HALF), BF),
        SHAPE((8, NY * HALF), F32),
        SHAPE((96, Q), BF),
    ]
    first_outs = run_projection(project_first, place, pieces, weights_1, 768, kinds * 2)
    x_own, bc_own, dt_own, tail_own = first_outs[:4]
    x_give, bc_give, dt_give, tail_give = first_outs[4:]
    bc_got = sibling(bc_give)
    halo_own = routed(
        tail_own, lambda z, y, x, c: (z + 1, y, x, 1) if z + 1 < NZ and c == 1 else None
    )
    halo_give = routed(
        tail_give, lambda z, y, x, c: (z + 1, y, x, 0) if z + 1 < NZ and c == 1 else None
    )
    x_got, dt_got = sibling(x_give), sibling(dt_give)
    b_own, c_own = local_call(
        convolve_side,
        [SHAPE((32, T), BF)] * 2,
        place,
        bc_own,
        bc_got,
        halo_own,
        halo_give,
        taps_bc,
        scratch=[pltpu.VMEM((64, T + Q), F32)],
    )
    b_parts = [b_own] + [shifted(b_own, "y", d) for d in (1, -1, 2)]
    x_conv, running, step = local_call(
        conv_and_rates,
        [SHAPE((T, CH), BF), SHAPE((8, T), F32), SHAPE((8, T), F32)],
        place,
        x_own,
        x_got,
        halo_own,
        halo_give,
        taps_x,
        dt_own,
        dt_got,
        column(dt_bias),
        column(a_log),
        scratch=[pltpu.VMEM((T + 16, CH), F32), pltpu.VMEM((8, T), F32)],
        cost=pl.CostEstimate(flops=10**9, bytes_accessed=8 * MIB, transcendentals=0),
    )
    b_parts, c_own, running = lax.optimization_barrier((b_parts, c_own, running))
    c_parts = [c_own] + [shifted(c_own, "y", d) for d in (1, -1, 2)]
    b_conv, local, end = local_call(
        states,
        [SHAPE((N, T), BF), SHAPE((NB, N, CH), BF), SHAPE((N + 16, CH), BF)],
        place,
        x_conv,
        running,
        step,
        *b_parts,
    )
    later = lambda v, d: lax.ppermute(v, "z", [(i, i + d) for i in range(NZ - d)])
    near = [later(end, d) for d in (1, 2, 3)]
    place_2, end, c_parts = lax.optimization_barrier((place, end, c_parts))
    z_own, z_give = run_projection(project_second, place_2, pieces, weights_2, 512, kinds[:1] * 2)
    near, z_give = lax.optimization_barrier((near, z_give))
    z_got = sibling(z_give)
    (window,) = local_call(combine, [SHAPE((N, CH), BF)], place, end, *near)
    place_3, window = lax.optimization_barrier((place, window))
    far_end = later(window, 4)
    c_conv, y_within = local_call(
        within,
        [SHAPE((N, T), BF), SHAPE((T, CH), F32)],
        place_3,
        x_conv,
        b_conv,
        running,
        step,
        skip,
        *c_parts,
    )
    sorted_rows = local_call(
        carry,
        [SHAPE((ROWS, CH), BF)] * NY,
        place,
        c_conv,
        running,
        local,
        y_within,
        z_own,
        z_got,
        *near,
        far_end,
        scratch=[pltpu.VMEM((T, CH), BF), pltpu.VMEM((NY, ROWS, CH), BF)],
    )
    block = (ROWS, FEAT)
    hidden, far_give, far_keep = run_far(place, gain, w_out, over_y(sorted_rows))
    far_got = sibling(far_give)
    half_block = (HALF, FEAT)
    upper, lower = local_call(merge_far, [SHAPE(half_block, BF)] * 2, place, far_keep, far_got)
    place_4, upper, lower = lax.optimization_barrier((place, upper, lower))
    from_left, from_right = shifted(upper, "x", 1), shifted(lower, "x", -1)
    rest_give = run_rest(place_4, w_out, hidden, True)
    rest_got = sibling(rest_give)
    rest_keep = run_rest(place_4, w_out, hidden, False)
    ahead, behind, stays = local_call(
        merge_rest,
        [SHAPE(block, kind) for kind in (BF, BF, F32)],
        place,
        rest_keep,
        rest_got,
        from_left,
        from_right,
    )
    (out,) = local_call(
        finish,
        [SHAPE(block, BF)],
        place,
        stays,
        shifted(ahead, "x", 1),
        shifted(behind, "x", -1),
    )
    return out


def solution(mesh):
    fine = Mesh(mesh.devices.reshape(NZ, NY, NX, NC), ("z", "y", "x", "c"))
    seq, head = ("z", "y"), ("x", "c")
    return jax.shard_map(
        on_device,
        mesh=fine,
        in_specs=(
            P(seq, head),
            P(seq, None, head),
            P(seq, None, head),
            P(seq, head),
            P(None, head),
            P(None, None, head),
            P(head),
            P(head),
            P(head),
            P(head),
            P(head, None),
        ),
        out_specs=P(seq, head),
        check_vma=False,
    )
```

```python
import functools
import jax
import jax.numpy as jnp
from jax import lax
from jax.experimental import pallas as pl
from jax.experimental.pallas import tpu as pltpu
from jax.sharding import Mesh, PartitionSpec as P

EPSILON = 1e-05
BF = jnp.bfloat16
F32 = jnp.float32
MIB = 1024 * 1024

NZ, NY, NX, NC = 8, 4, 4, 2
ROWS = 512
HALF = ROWS // 2
FEAT = 512
D = 4096
T = ROWS * NY
CH = 256
HD = 4
PS = 64
N = 128
Q = 128
NB = T // Q
W1 = 384
OFFSETS = (0, -1, 1, 2)
ALL = ("z", "y", "x", "c")
VMEM = pl.BlockSpec(memory_space=pltpu.VMEM)
SMEM = pl.BlockSpec(memory_space=pltpu.SMEM)
ANY = pl.BlockSpec(memory_space=pl.ANY)
HBM = pl.BlockSpec(memory_space=pltpu.HBM)
SHAPE = jax.ShapeDtypeStruct
SMALL = pl.CostEstimate(flops=1000, bytes_accessed=1000, transcendentals=0)


def shifted(value, axis, distance):
    n = lax.axis_size(axis)
    return lax.ppermute(value, axis, [(i, (i + distance) % n) for i in range(n)])


def sibling(value):
    return lax.ppermute(value, "c", [(0, 1), (1, 0)])


def routed(value, target):
    pairs = []
    for source in range(NZ * NY * NX * NC):
        rest, c = divmod(source, NC)
        rest, x = divmod(rest, NX)
        z, y = divmod(rest, NY)
        goal = target(z, y, x, c)
        if goal is not None:
            z, y, x, c = goal
            pairs.append((source, ((z * NY + y) * NX + x) * NC + c))
    return lax.ppermute(value, ALL, pairs)


def crossed(value, along_x, distance):
    def target(z, y, x, c):
        if c == along_x:
            return z, y, (x + distance) % NX, c
        return z, (y + distance) % NY, x, c

    return routed(value, target)


def over_y(v):
    return [v[0], shifted(v[1], "y", 1), shifted(v[3], "y", -1), shifted(v[2], "y", 2)]


def half_rows(tokens, c):
    early, late = tokens[:HALF], tokens[HALF:]
    got = sibling(jnp.where(c == 0, late, early))
    return jnp.where(
        c == 0,
        jnp.concatenate([early, got], axis=1),
        jnp.concatenate([got, late], axis=1),
    )


def gather_tokens(mine, first, second):
    mine, first = lax.optimization_barrier((mine, first))
    right, left = crossed(mine, 0, 1), crossed(mine, 0, -1)
    first = over_y(first)
    right, left, first, second = lax.optimization_barrier((right, left, first, second))
    middle = HALF // 2
    opposite = [crossed(right[:middle], 0, 1), crossed(left[middle:], 0, -1)]
    second = over_y(second)
    near = jnp.stack([mine, right])
    away = jnp.stack([left, jnp.concatenate(opposite)])
    near, away, second = lax.optimization_barrier((near, away, second))
    near_r, away_l = crossed(near, 1, 1), crossed(away, 1, -1)
    near_l, away_r = crossed(near, 1, -1), crossed(away, 1, 1)
    near_2, away_2 = crossed(near_r, 1, 1), crossed(away_l, 1, -1)
    return [near, away, near_r, away_r, near_l, away_l, near_2, away_2], first, second


def place_of(place, i, j):
    x, y, c = place[0], place[1], place[2]
    first, second = OFFSETS[i] + 4, OFFSETS[j] + 4
    dx = jnp.where(c == 0, first, second)
    dy = jnp.where(c == 0, second, first)
    return lax.rem(y + dy, NY), lax.rem(x + dx, NX)


def load_operands(place, pieces, weights, columns, tok, w, sems):
    x, y, c = place[0], place[1], place[2]

    def fetch(i, j, block):
        yy, _ = place_of(place, i, j)
        pltpu.make_async_copy(
            pieces[j * 2 + i // 2].at[i % 2],
            tok.at[block, pl.ds(pl.multiple_of(yy * HALF, HALF), HALF), :],
            sems.at[block],
        ).start()

    for block, offset in enumerate(OFFSETS):
        first = lax.rem(x + (offset + NX), NX) * 2
        for core, lane, width, to in columns:
            for rel, d in enumerate(OFFSETS):
                yy = lax.rem(y + (d + NY), NY)
                pltpu.make_async_copy(
                    weights.at[pl.ds(first, 2), 1 - c if core else c, rel, :, pl.ds(lane, width)],
                    w.at[block, :, yy, :, pl.ds(to, width)],
                    sems.at[4 + block],
                ).start()

        @pl.when(c == 0)
        def _():
            for j in range(4):
                fetch(block, j, block)

        @pl.when(c == 1)
        def _():
            for i in range(4):
                fetch(i, block, block)


def products(tok, w, acc, sems):
    for block in range(4):
        pltpu.make_async_copy(tok.at[block], tok.at[block], sems.at[block]).wait()
        pltpu.make_async_copy(w.at[block], w.at[block], sems.at[4 + block]).wait()
        for k in range(NY):
            rows = slice(k * HALF, (k + 1) * HALF)
            part = jnp.dot(
                tok[block, rows, :],
                w[block].reshape(D // NX, w.shape[-1]),
                preferred_element_type=F32,
            )
            if block == 0:
                acc[rows, :] = part
            elif block < 3:
                acc[rows, :] += part
            else:
                yield k, acc[rows, :] + part


def silu(v):
    return v / (1.0 + jnp.exp(-v))


GATES = [(0, 0, CH, 0), (1, 0, CH, CH)]
SIDES = [(0, CH, 128, 2 * CH), (1, CH, 128, 2 * CH + 128)]


def project_first(place, *refs):
    pieces, weights = refs[:8], refs[8]
    outs, (tok, w, acc, sems) = refs[9:17], refs[17:]
    load_operands(place, pieces, weights, GATES + SIDES, tok, w, sems)
    for k, total in products(tok, w, acc, sems):
        rows = slice(k * HALF, (k + 1) * HALF)
        for core in range(2):
            x_ref, bc_ref, dt_ref, tail = outs[4 * core : 4 * core + 4]
            x = total[:, core * CH : (core + 1) * CH].astype(BF)
            start = 2 * CH + 128 * core
            side = total[:, start : start + 128].T
            x_ref[k] = x
            bc_ref[:, rows] = side[:64].astype(BF)
            dt_ref[:, rows] = side[64:72]
            if k == NY - 1:
                tail[:64, :] = side[:64, HALF - Q :].astype(BF)
                tail[64:80, :] = x[HALF - 16 :, :Q]
                tail[80:, :] = x[HALF - 16 :, Q:]


def project_second(place, *refs):
    pieces, weights = refs[:8], refs[8]
    outs, (tok, w, acc, sems) = refs[9:11], refs[11:]
    load_operands(place, pieces, weights, GATES, tok, w, sems)
    for k, total in products(tok, w, acc, sems):
        for core in range(2):
            outs[core][k] = total[:, core * CH : (core + 1) * CH].astype(BF)


def run_projection(kernel, place, pieces, weights, width, outs):
    return pl.pallas_call(
        kernel,
        out_shape=outs,
        in_specs=[SMEM] + [ANY] * 8 + [HBM],
        out_specs=[VMEM] * len(outs),
        scratch_shapes=[
            pltpu.VMEM((NX, NY * HALF, D // NX), BF),
            pltpu.VMEM((NX, NZ // NX, NY, 128, width), BF),
            pltpu.VMEM((NY * HALF, width), F32),
            pltpu.SemaphoreType.DMA((8,)),
        ],
        compiler_params=pltpu.CompilerParams(vmem_limit_bytes=46 * MIB),
        cost_estimate=SMALL,
    )(place, *pieces, weights)


def local_call(kernel, outs, *args, scratch=(), limit=20, cost=SMALL):
    return pl.pallas_call(
        kernel,
        out_shape=outs,
        in_specs=[SMEM] + [VMEM] * (len(args) - 1),
        out_specs=[VMEM] * len(outs),
        scratch_shapes=list(scratch),
        compiler_params=pltpu.CompilerParams(vmem_limit_bytes=limit * MIB),
        cost_estimate=cost,
    )(*args)


def half_start(place, k, other):
    half = 1 - place[2] if other else place[2]
    return pl.multiple_of(k * ROWS + half * HALF, HALF)


def conv_and_rates(
    place, own, other, halo_1, halo_2, taps, dt_own, dt_other, bias, a_log, *rest
):
    out_ref, run_ref, step_ref, full, raw_full = rest
    halo = (halo_1[64:, :] + halo_2[64:, :]).astype(F32)
    full[:16, :Q] = halo[:16]
    full[:16, Q:] = halo[16:]
    for k in range(NY):
        full[pl.ds(half_start(place, k, False) + 16, HALF), :] = own[k].astype(F32)
        full[pl.ds(half_start(place, k, True) + 16, HALF), :] = other[k].astype(F32)
        at = slice(k * HALF, (k + 1) * HALF)
        raw_full[:, pl.ds(half_start(place, k, False), HALF)] = dt_own[:, at]
        raw_full[:, pl.ds(half_start(place, k, True), HALF)] = dt_other[:, at]
    for block in range(NB):
        total = taps[3:4, :] * full[block * Q + 16 : block * Q + 16 + Q, :]
        for back in (1, 2, 3):
            start = block * Q + 16 - back
            total = total + taps[3 - back : 4 - back, :] * full[start : start + Q, :]
        out_ref[block * Q : (block + 1) * Q, :] = silu(total).astype(BF)
    lane = lax.broadcasted_iota(jnp.int32, (8, Q), 1)
    factor = -jnp.exp(a_log[...])
    for block in range(NB):
        at = slice(block * Q, (block + 1) * Q)
        raw = raw_full[:, at] + bias[...]
        step = jnp.maximum(raw, 0.0) + jnp.log1p(jnp.exp(-jnp.abs(raw)))
        running = step * factor
        for distance in (1, 2, 4, 8, 16, 32, 64):
            running = running + jnp.where(lane < distance, 0.0, pltpu.roll(running, distance, 1))
        run_ref[:, at] = running
        step_ref[:, at] = step


def convolve_side(place, own, other, halo_1, halo_2, taps, out_ref, full):
    full[:, :Q] = (halo_1[:64, :] + halo_2[:64, :]).astype(F32)
    for k in range(NY):
        at = slice(k * HALF, (k + 1) * HALF)
        full[:, pl.ds(pl.multiple_of(half_start(place, k, False) + Q, Q), HALF)] = own[
            :, at
        ].astype(F32)
        full[:, pl.ds(pl.multiple_of(half_start(place, k, True) + Q, Q), HALF)] = other[
            :, at
        ].astype(F32)
    lane = lax.broadcasted_iota(jnp.int32, (64, Q), 1)
    before = [pltpu.roll(full[:, :Q], back, 1) for back in (1, 2, 3)]
    for block in range(NB):
        now = full[:, (block + 1) * Q : (block + 2) * Q]
        turned = [pltpu.roll(now, back, 1) for back in (1, 2, 3)]
        total = taps[:, 3:4] * now
        for back in (1, 2, 3):
            moved = jnp.where(lane < back, before[back - 1], turned[back - 1])
            total = total + taps[:, 3 - back : 4 - back] * moved
        out_ref[:, block * Q : (block + 1) * Q] = silu(total).astype(BF)
        before = turned


def apart(value):
    lane = lax.broadcasted_iota(jnp.int32, value.shape, 1)
    zero = jnp.zeros_like(value)
    return jnp.concatenate(
        [jnp.where(lane < PS, value, zero), jnp.where(lane < PS, zero, value)], axis=0
    )


def of_pair(rows, pair):
    lane = lax.broadcasted_iota(jnp.int32, (1, Q), 1)
    return jnp.where(lane < PS, rows[2 * pair : 2 * pair + 1], rows[2 * pair + 1 : 2 * pair + 2])


def decay_rows(decay):
    wide = jnp.broadcast_to(decay, (8, CH))
    high = wide.astype(BF)
    return jnp.concatenate([high, (wide - high.astype(F32)).astype(BF)], axis=0)


def decay_of(ref):
    return ref[N : N + 1, :].astype(F32) + ref[N + 8 : N + 9, :].astype(F32)


def chained(arrived):
    state, weight = arrived[0][:N, :].astype(F32), decay_of(arrived[0])
    for ref in arrived[1:]:
        state = state + weight * ref[:N, :].astype(F32)
        weight = weight * decay_of(ref)
    return state, weight


def combine(place, end, first, second, third, out_ref):
    state, _ = chained((first, second, third))
    out_ref[...] = (end[:N, :].astype(F32) + decay_of(end) * state).astype(BF)


def states(place, x_ref, run_ref, step_ref, *rest):
    parts, (b_full, c_full, local_ref, end_ref) = rest[:4], rest[4:]
    for part, d in zip(parts, OFFSETS):
        yy = lax.rem(place[1] + (d + NY), NY)
        at = pl.ds(pl.multiple_of(yy * 32, 32), 32)
        b_full[at, :] = part[:32]
        c_full[at, :] = part[32:]
    state = [jnp.zeros((N, Q), F32) for _ in range(HD // 2)]
    total_rate = jnp.zeros((8, Q), F32)
    for block in range(NB):
        at = slice(block * Q, (block + 1) * Q)
        b = b_full[:, at].astype(F32)
        running, step = run_ref[:, at], step_ref[:, at]
        last = running[:, Q - 1 : Q]
        weight = jnp.exp(last - running) * step
        decay = jnp.exp(last)
        for pair in range(HD // 2):
            lanes = slice(pair * Q, (pair + 1) * Q)
            local_ref[block, :, lanes] = state[pair].astype(BF)
            scaled = [(b * weight[h : h + 1, :]).astype(BF) for h in (2 * pair, 2 * pair + 1)]
            increment = jnp.dot(
                jnp.concatenate(scaled, axis=1),
                apart(x_ref[at, lanes]),
                preferred_element_type=F32,
            )
            state[pair] = of_pair(decay, pair) * state[pair] + increment
        total_rate = total_rate + last
    for pair in range(HD // 2):
        end_ref[:N, pair * Q : (pair + 1) * Q] = state[pair].astype(BF)
    end_ref[N:, :] = decay_rows(over_channels(jnp.exp(total_rate)))


def within(place, x_ref, b_ref, c_ref, run_ref, step_ref, skip, y_ref):
    below = lax.broadcasted_iota(jnp.int32, (Q, Q), 0) >= lax.broadcasted_iota(
        jnp.int32, (Q, Q), 1
    )
    for block in range(NB):
        at = slice(block * Q, (block + 1) * Q)
        running, step = run_ref[:, at], step_ref[:, at]
        columns = running.T
        scores = lax.dot_general(
            c_ref[:, at], b_ref[:, at], (((0,), (0,)), ((), ())), preferred_element_type=F32
        )
        for pair in range(HD // 2):
            mixing = []
            for h in (2 * pair, 2 * pair + 1):
                spread = jnp.where(below, columns[:, h : h + 1] - running[h : h + 1, :], -1e30)
                mixing.append((jnp.exp(spread) * step[h : h + 1, :] * scores).astype(BF))
            lanes = slice(pair * Q, (pair + 1) * Q)
            value = x_ref[at, lanes]
            y = jnp.dot(
                jnp.concatenate(mixing, axis=1), apart(value), preferred_element_type=F32
            )
            y_ref[at, lanes] = y + skip[:, lanes] * value.astype(F32)


def per_head(columns):
    return jnp.concatenate(
        [jnp.broadcast_to(columns[:, h : h + 1], (columns.shape[0], PS)) for h in range(HD)],
        axis=1,
    )


def over_channels(rows):
    return jnp.concatenate([rows[h : h + 1, :PS] for h in range(HD)], axis=1)


def carry(place, c_ref, run_ref, local_ref, y_ref, z_own, z_other, *rest):
    arrived, outs, (z_full, sorted_rows) = rest[:4], rest[4:8], rest[8:]
    for k in range(NY):
        z_full[pl.ds(half_start(place, k, False), HALF), :] = z_own[k]
        z_full[pl.ds(half_start(place, k, True), HALF), :] = z_other[k]
    state, weight = chained(arrived[:3])
    state = state + weight * arrived[3][...].astype(F32)
    before = jnp.ones((1, CH), F32)
    for block in range(NB):
        at = slice(block * Q, (block + 1) * Q)
        running = run_ref[:, at]
        full = (local_ref[block].astype(F32) + before * state).astype(BF)
        carried = lax.dot_general(
            c_ref[:, at], full, (((0,), (0,)), ((), ())), preferred_element_type=F32
        )
        grown = jnp.exp(running)
        y = y_ref[at, :] + per_head(grown.T) * carried
        gate = silu(z_full[at, :].astype(F32))
        rel = lax.rem(block // 4 + NY - place[1], NY)
        part = block % 4
        sorted_rows[rel, part * Q : (part + 1) * Q, :] = (y * gate).astype(BF)
        last = jnp.broadcast_to(grown[:, Q - 1 : Q], (8, Q))
        before = before * over_channels(last)
    for rel in range(NY):
        outs[rel][...] = sorted_rows[rel]


def project_far(place, gain, w_ref, *rest):
    parts, (hidden, give, keep) = rest[:NY], rest[NY:]

    @pl.when(pl.program_id(0) == 0)
    def _():
        total = jnp.zeros((ROWS, 1), F32)
        for ref in parts:
            value = ref[...].astype(F32)
            total = total + jnp.sum(value * value, axis=1, keepdims=True)
        scale = lax.rsqrt(total / (NY * CH) + EPSILON)
        for ref, d in zip(parts, OFFSETS):
            yy = lax.rem(place[1] + (d + NY), NY)
            lanes = pl.ds(pl.multiple_of(yy * CH, CH), CH)
            hidden[:, lanes] = (ref[...].astype(F32) * scale * gain[:, lanes]).astype(BF)

    acc = jnp.dot(hidden[...], w_ref[...], preferred_element_type=F32).astype(BF)

    @pl.when(pl.program_id(0) == 0)
    def _():
        give[...] = acc

    @pl.when(pl.program_id(0) == 1)
    def _():
        keep[...] = acc


def project_rest(place, w_ref, hidden, out_ref):
    out_ref[...] = jnp.dot(hidden[...], w_ref[...], preferred_element_type=F32).astype(BF)


def output_call(kernel, place, columns, steps, more, w_out, parts, outs, specs):
    whole = lambda v: pl.BlockSpec(v.shape, lambda i, p: (0,) * v.ndim)
    return pl.pallas_call(
        kernel,
        out_shape=outs,
        grid_spec=pltpu.PrefetchScalarGridSpec(
            num_scalar_prefetch=1,
            grid=(steps,),
            in_specs=[whole(v) for v in more]
            + [pl.BlockSpec((NY * CH, FEAT), columns)]
            + [whole(v) for v in parts],
            out_specs=specs,
        ),
        compiler_params=pltpu.CompilerParams(vmem_limit_bytes=46 * MIB),
        cost_estimate=SMALL,
    )(place, *more, w_out, *parts)


def run_far(place, gain, w_out, parts):
    columns = lambda i, p: (0, lax.rem(p[0] + 2, NX) * NC + jnp.where(i == 0, 1 - p[2], p[2]))
    shapes = [(ROWS, NY * CH), (ROWS, FEAT), (ROWS, FEAT)]
    return output_call(
        project_far,
        place,
        columns,
        2,
        [gain],
        w_out,
        parts,
        [SHAPE(shape, BF) for shape in shapes],
        [pl.BlockSpec(shape, lambda i, p: (0, 0)) for shape in shapes],
    )


def run_rest(place, w_out, hidden, other):
    def columns(i, p):
        ahead = jnp.where(i == 0, 1, jnp.where(i == 1, 3, 0))
        return 0, lax.rem(p[0] + ahead, NX) * NC + (1 - p[2] if other else p[2])

    return output_call(
        project_rest,
        place,
        columns,
        3,
        [],
        w_out,
        [hidden],
        [SHAPE((ROWS, 3 * FEAT), BF)],
        [pl.BlockSpec((ROWS, FEAT), lambda i, p: (0, i))],
    )[0]


def merge_far(place, kept, got, upper, lower):
    total = (kept[...].astype(F32) + got[...].astype(F32)).astype(BF)
    upper[...] = total[:HALF]
    lower[...] = total[HALF:]


def merge_rest(place, kept, got, from_left, from_right, ahead, behind, stays):
    for k, ref in enumerate((ahead, behind, stays)):
        at = slice(k * FEAT, (k + 1) * FEAT)
        upper = kept[:HALF, at].astype(F32) + got[:HALF, at].astype(F32)
        lower = kept[HALF:, at].astype(F32) + got[HALF:, at].astype(F32)
        if k == 0:
            upper = upper + from_left[...].astype(F32)
        if k == 1:
            lower = lower + from_right[...].astype(F32)
        ref[:HALF, :] = upper.astype(ref.dtype)
        ref[HALF:, :] = lower.astype(ref.dtype)


def finish(place, own, first, second, out_ref):
    out_ref[...] = (own[...] + first[...].astype(F32) + second[...].astype(F32)).astype(BF)


def on_device(tokens, w_zx, w_bc, w_dt, conv_x, conv_bc, dt_bias, a_log, d_skip, norm_gain, w_out):
    y, c = lax.axis_index("y"), lax.axis_index("c")
    place = jnp.stack([lax.axis_index("x"), y, c, lax.axis_index("z")]).astype(jnp.int32)
    rows = w_zx.shape[0]

    def quarter(value, distance, width, dim=1):
        start = lax.rem(y + (distance + NY), NY) * width
        return lax.dynamic_slice_in_dim(value, start, width, dim)

    def for_y(distance):
        zero = jnp.zeros((rows, W1 - CH - 64 - HD), BF)
        return jnp.concatenate(
            [
                quarter(w_zx[:, 1], distance, CH),
                quarter(w_bc[:, 0], distance, 32),
                quarter(w_bc[:, 1], distance, 32),
                quarter(w_dt, distance, HD),
                zero,
            ],
            axis=1,
        )

    mine = half_rows(tokens, c)
    gate = lambda d: quarter(w_zx[:, 0], d, CH)
    pieces, first, second = gather_tokens(
        mine, [for_y(d) for d in range(NY)], [gate(d) for d in range(NY)]
    )
    weights_1 = lax.all_gather(jnp.concatenate(first), ("z", "c"), axis=0, tiled=True)
    weights_1 = weights_1.reshape(NZ, NC, NY, rows, W1)
    weights_2 = lax.all_gather(jnp.concatenate(second), ("z", "c"), axis=0, tiled=True)
    weights_2 = weights_2.reshape(NZ, NC, NY, rows, CH)

    taps_x = quarter(conv_x, 0, CH).astype(F32)
    taps_bc = jnp.concatenate([quarter(conv_bc[:, k], 0, 32) for k in range(2)], axis=1)
    taps_bc = taps_bc.T.astype(F32)
    column = lambda v: jnp.pad(quarter(v, 0, HD, 0), (0, 8 - HD)).reshape(8, 1)
    skip = jnp.repeat(quarter(d_skip, 0, HD, 0), PS).reshape(1, CH)
    gain = norm_gain.astype(F32).reshape(1, -1)

    kinds = [
        SHAPE((NY, HALF, CH), BF),
        SHAPE((64, NY * HALF), BF),
        SHAPE((8, NY * HALF), F32),
        SHAPE((96, Q), BF),
    ]
    first_outs = run_projection(project_first, place, pieces, weights_1, 768, kinds * 2)
    x_own, bc_own, dt_own, tail_own = first_outs[:4]
    x_give, bc_give, dt_give, tail_give = first_outs[4:]
    bc_got = sibling(bc_give)
    halo_own = routed(
        tail_own, lambda z, y, x, c: (z + 1, y, x, 1) if z + 1 < NZ and c == 1 else None
    )
    halo_give = routed(
        tail_give, lambda z, y, x, c: (z + 1, y, x, 0) if z + 1 < NZ and c == 1 else None
    )
    x_got, dt_got = sibling(x_give), sibling(dt_give)
    (bc,) = local_call(
        convolve_side,
        [SHAPE((64, T), BF)],
        place,
        bc_own,
        bc_got,
        halo_own,
        halo_give,
        taps_bc,
        scratch=[pltpu.VMEM((64, T + Q), F32)],
    )
    x_conv, running, step = local_call(
        conv_and_rates,
        [SHAPE((T, CH), BF), SHAPE((8, T), F32), SHAPE((8, T), F32)],
        place,
        x_own,
        x_got,
        halo_own,
        halo_give,
        taps_x,
        dt_own,
        dt_got,
        column(dt_bias),
        column(a_log),
        scratch=[pltpu.VMEM((T + 16, CH), F32), pltpu.VMEM((8, T), F32)],
        cost=pl.CostEstimate(flops=10**9, bytes_accessed=8 * MIB, transcendentals=0),
    )
    bc_parts = [bc] + [shifted(bc, "y", d) for d in (1, -1, 2)]
    b_conv, c_conv, local, end = local_call(
        states,
        [SHAPE((N, T), BF), SHAPE((N, T), BF), SHAPE((NB, N, CH), BF), SHAPE((N + 16, CH), BF)],
        place,
        x_conv,
        running,
        step,
        *bc_parts,
    )
    later = lambda v, d: lax.ppermute(v, "z", [(i, i + d) for i in range(NZ - d)])
    near = [later(end, d) for d in (1, 2, 3)]
    place_2, end = lax.optimization_barrier((place, end))
    z_own, z_give = run_projection(project_second, place_2, pieces, weights_2, 512, kinds[:1] * 2)
    near, z_give = lax.optimization_barrier((near, z_give))
    z_got = sibling(z_give)
    (window,) = local_call(combine, [SHAPE((N, CH), BF)], place, end, *near)
    place_3, window = lax.optimization_barrier((place, window))
    far_end = later(window, 4)
    (y_within,) = local_call(
        within, [SHAPE((T, CH), F32)], place_3, x_conv, b_conv, c_conv, running, step, skip
    )
    sorted_rows = local_call(
        carry,
        [SHAPE((ROWS, CH), BF)] * NY,
        place,
        c_conv,
        running,
        local,
        y_within,
        z_own,
        z_got,
        *near,
        far_end,
        scratch=[pltpu.VMEM((T, CH), BF), pltpu.VMEM((NY, ROWS, CH), BF)],
    )
    block = (ROWS, FEAT)
    hidden, far_give, far_keep = run_far(place, gain, w_out, over_y(sorted_rows))
    far_got = sibling(far_give)
    half_block = (HALF, FEAT)
    upper, lower = local_call(merge_far, [SHAPE(half_block, BF)] * 2, place, far_keep, far_got)
    place_4, upper, lower = lax.optimization_barrier((place, upper, lower))
    from_left, from_right = shifted(upper, "x", 1), shifted(lower, "x", -1)
    rest_give = run_rest(place_4, w_out, hidden, True)
    rest_got = sibling(rest_give)
    rest_keep = run_rest(place_4, w_out, hidden, False)
    ahead, behind, stays = local_call(
        merge_rest,
        [SHAPE(block, kind) for kind in (BF, BF, F32)],
        place,
        rest_keep,
        rest_got,
        from_left,
        from_right,
    )
    (out,) = local_call(
        finish,
        [SHAPE(block, BF)],
        place,
        stays,
        shifted(ahead, "x", 1),
        shifted(behind, "x", -1),
    )
    return out


def solution(mesh):
    fine = Mesh(mesh.devices.reshape(NZ, NY, NX, NC), ("z", "y", "x", "c"))
    seq, head = ("z", "y"), ("x", "c")
    return jax.shard_map(
        on_device,
        mesh=fine,
        in_specs=(
            P(seq, head),
            P(seq, None, head),
            P(seq, None, head),
            P(seq, head),
            P(None, head),
            P(None, None, head),
            P(head),
            P(head),
            P(head),
            P(head),
            P(head, None),
        ),
        out_specs=P(seq, head),
        check_vma=False,
    )
```

```python
import functools
import jax
import jax.numpy as jnp
from jax import lax
from jax.experimental import pallas as pl
from jax.experimental.pallas import tpu as pltpu
from jax.sharding import Mesh, PartitionSpec as P

EPSILON = 1e-05
BF = jnp.bfloat16
F32 = jnp.float32
MIB = 1024 * 1024

NZ, NY, NX, NC = 8, 4, 4, 2
ROWS = 512
HALF = ROWS // 2
FEAT = 512
D = 4096
T = ROWS * NY
CH = 256
HD = 4
PS = 64
N = 128
Q = 128
NB = T // Q
W1 = 384
OFFSETS = (0, -1, 1, 2)
ALL = ("z", "y", "x", "c")
VMEM = pl.BlockSpec(memory_space=pltpu.VMEM)
SMEM = pl.BlockSpec(memory_space=pltpu.SMEM)
ANY = pl.BlockSpec(memory_space=pl.ANY)
HBM = pl.BlockSpec(memory_space=pltpu.HBM)
SHAPE = jax.ShapeDtypeStruct
SMALL = pl.CostEstimate(flops=1000, bytes_accessed=1000, transcendentals=0)


def shifted(value, axis, distance):
    n = lax.axis_size(axis)
    return lax.ppermute(value, axis, [(i, (i + distance) % n) for i in range(n)])


def sibling(value):
    return lax.ppermute(value, "c", [(0, 1), (1, 0)])


def routed(value, target):
    pairs = []
    for source in range(NZ * NY * NX * NC):
        rest, c = divmod(source, NC)
        rest, x = divmod(rest, NX)
        z, y = divmod(rest, NY)
        goal = target(z, y, x, c)
        if goal is not None:
            z, y, x, c = goal
            pairs.append((source, ((z * NY + y) * NX + x) * NC + c))
    return lax.ppermute(value, ALL, pairs)


def crossed(value, along_x, distance):
    def target(z, y, x, c):
        if c == along_x:
            return z, y, (x + distance) % NX, c
        return z, (y + distance) % NY, x, c

    return routed(value, target)


def over_y(v):
    return [v[0], shifted(v[1], "y", 1), shifted(v[3], "y", -1), shifted(v[2], "y", 2)]


def half_rows(tokens, c):
    early, late = tokens[:HALF], tokens[HALF:]
    got = sibling(jnp.where(c == 0, late, early))
    return jnp.where(
        c == 0,
        jnp.concatenate([early, got], axis=1),
        jnp.concatenate([got, late], axis=1),
    )


def gather_tokens(mine, first, second):
    mine, first = lax.optimization_barrier((mine, first))
    right, left = crossed(mine, 0, 1), crossed(mine, 0, -1)
    first = over_y(first)
    right, left, first, second = lax.optimization_barrier((right, left, first, second))
    middle = HALF // 2
    opposite = [crossed(right[:middle], 0, 1), crossed(left[middle:], 0, -1)]
    second = over_y(second)
    near = jnp.stack([mine, right])
    away = jnp.stack([left, jnp.concatenate(opposite)])
    near, away, second = lax.optimization_barrier((near, away, second))
    near_r, away_l = crossed(near, 1, 1), crossed(away, 1, -1)
    near_l, away_r = crossed(near, 1, -1), crossed(away, 1, 1)
    near_2, away_2 = crossed(near_r, 1, 1), crossed(away_l, 1, -1)
    return [near, away, near_r, away_r, near_l, away_l, near_2, away_2], first, second


def place_of(place, i, j):
    x, y, c = place[0], place[1], place[2]
    first, second = OFFSETS[i] + 4, OFFSETS[j] + 4
    dx = jnp.where(c == 0, first, second)
    dy = jnp.where(c == 0, second, first)
    return lax.rem(y + dy, NY), lax.rem(x + dx, NX)


def load_operands(place, pieces, weights, columns, tok, w, sems):
    x, y, c = place[0], place[1], place[2]

    def fetch(i, j, block):
        yy, _ = place_of(place, i, j)
        pltpu.make_async_copy(
            pieces[j * 2 + i // 2].at[i % 2],
            tok.at[block, pl.ds(pl.multiple_of(yy * HALF, HALF), HALF), :],
            sems.at[block],
        ).start()

    for block, offset in enumerate(OFFSETS):
        first = lax.rem(x + (offset + NX), NX) * 2
        for core, lane, width, to in columns:
            for rel, d in enumerate(OFFSETS):
                yy = lax.rem(y + (d + NY), NY)
                pltpu.make_async_copy(
                    weights.at[pl.ds(first, 2), 1 - c if core else c, rel, :, pl.ds(lane, width)],
                    w.at[block, :, yy, :, pl.ds(to, width)],
                    sems.at[4 + block],
                ).start()

        @pl.when(c == 0)
        def _():
            for j in range(4):
                fetch(block, j, block)

        @pl.when(c == 1)
        def _():
            for i in range(4):
                fetch(i, block, block)


def products(tok, w, acc, sems):
    for block in range(4):
        pltpu.make_async_copy(tok.at[block], tok.at[block], sems.at[block]).wait()
        pltpu.make_async_copy(w.at[block], w.at[block], sems.at[4 + block]).wait()
        for k in range(NY):
            rows = slice(k * HALF, (k + 1) * HALF)
            part = jnp.dot(
                tok[block, rows, :],
                w[block].reshape(D // NX, w.shape[-1]),
                preferred_element_type=F32,
            )
            if block == 0:
                acc[rows, :] = part
            elif block < 3:
                acc[rows, :] += part
            else:
                yield k, acc[rows, :] + part


def silu(v):
    return v / (1.0 + jnp.exp(-v))


GATES = [(0, 0, CH, 0), (1, 0, CH, CH)]
SIDES = [(0, CH, 128, 2 * CH), (1, CH, 128, 2 * CH + 128)]


def project_first(place, *refs):
    pieces, weights = refs[:8], refs[8]
    outs, (tok, w, acc, sems) = refs[9:17], refs[17:]
    load_operands(place, pieces, weights, GATES + SIDES, tok, w, sems)
    for k, total in products(tok, w, acc, sems):
        rows = slice(k * HALF, (k + 1) * HALF)
        for core in range(2):
            x_ref, bc_ref, dt_ref, tail = outs[4 * core : 4 * core + 4]
            x = total[:, core * CH : (core + 1) * CH].astype(BF)
            start = 2 * CH + 128 * core
            side = total[:, start : start + 128].T
            x_ref[k] = x
            bc_ref[:, rows] = side[:64].astype(BF)
            dt_ref[:, rows] = side[64:72]
            if k == NY - 1:
                tail[:64, :] = side[:64, HALF - Q :].astype(BF)
                tail[64:80, :] = x[HALF - 16 :, :Q]
                tail[80:, :] = x[HALF - 16 :, Q:]


def project_second(place, *refs):
    pieces, weights = refs[:8], refs[8]
    outs, (tok, w, acc, sems) = refs[9:11], refs[11:]
    load_operands(place, pieces, weights, GATES, tok, w, sems)
    for k, total in products(tok, w, acc, sems):
        for core in range(2):
            outs[core][k] = total[:, core * CH : (core + 1) * CH].astype(BF)


def run_projection(kernel, place, pieces, weights, width, outs):
    return pl.pallas_call(
        kernel,
        out_shape=outs,
        in_specs=[SMEM] + [ANY] * 8 + [HBM],
        out_specs=[VMEM] * len(outs),
        scratch_shapes=[
            pltpu.VMEM((NX, NY * HALF, D // NX), BF),
            pltpu.VMEM((NX, NZ // NX, NY, 128, width), BF),
            pltpu.VMEM((NY * HALF, width), F32),
            pltpu.SemaphoreType.DMA((8,)),
        ],
        compiler_params=pltpu.CompilerParams(vmem_limit_bytes=52 * MIB),
        cost_estimate=SMALL,
    )(place, *pieces, weights)


def local_call(kernel, outs, *args, scratch=(), limit=20, cost=SMALL):
    return pl.pallas_call(
        kernel,
        out_shape=outs,
        in_specs=[SMEM] + [VMEM] * (len(args) - 1),
        out_specs=[VMEM] * len(outs),
        scratch_shapes=list(scratch),
        compiler_params=pltpu.CompilerParams(vmem_limit_bytes=limit * MIB),
        cost_estimate=cost,
    )(*args)


def half_start(place, k, other):
    half = 1 - place[2] if other else place[2]
    return pl.multiple_of(k * ROWS + half * HALF, HALF)


def conv_and_rates(
    place, own, other, halo_1, halo_2, taps, dt_own, dt_other, bias, a_log, *rest
):
    out_ref, run_ref, step_ref, full, raw_full = rest
    halo = (halo_1[64:, :] + halo_2[64:, :]).astype(F32)
    full[:16, :Q] = halo[:16]
    full[:16, Q:] = halo[16:]
    for k in range(NY):
        full[pl.ds(half_start(place, k, False) + 16, HALF), :] = own[k].astype(F32)
        full[pl.ds(half_start(place, k, True) + 16, HALF), :] = other[k].astype(F32)
        at = slice(k * HALF, (k + 1) * HALF)
        raw_full[:, pl.ds(half_start(place, k, False), HALF)] = dt_own[:, at]
        raw_full[:, pl.ds(half_start(place, k, True), HALF)] = dt_other[:, at]
    for block in range(NB):
        total = taps[3:4, :] * full[block * Q + 16 : block * Q + 16 + Q, :]
        for back in (1, 2, 3):
            start = block * Q + 16 - back
            total = total + taps[3 - back : 4 - back, :] * full[start : start + Q, :]
        out_ref[block * Q : (block + 1) * Q, :] = silu(total).astype(BF)
    lane = lax.broadcasted_iota(jnp.int32, (8, Q), 1)
    factor = -jnp.exp(a_log[...])
    for block in range(NB):
        at = slice(block * Q, (block + 1) * Q)
        raw = raw_full[:, at] + bias[...]
        step = jnp.maximum(raw, 0.0) + jnp.log1p(jnp.exp(-jnp.abs(raw)))
        running = step * factor
        for distance in (1, 2, 4, 8, 16, 32, 64):
            running = running + jnp.where(lane < distance, 0.0, pltpu.roll(running, distance, 1))
        run_ref[:, at] = running
        step_ref[:, at] = step


def convolve_side(place, own, other, halo_1, halo_2, taps, out_ref, full):
    full[:, :Q] = (halo_1[:64, :] + halo_2[:64, :]).astype(F32)
    for k in range(NY):
        at = slice(k * HALF, (k + 1) * HALF)
        full[:, pl.ds(pl.multiple_of(half_start(place, k, False) + Q, Q), HALF)] = own[
            :, at
        ].astype(F32)
        full[:, pl.ds(pl.multiple_of(half_start(place, k, True) + Q, Q), HALF)] = other[
            :, at
        ].astype(F32)
    lane = lax.broadcasted_iota(jnp.int32, (64, Q), 1)
    before = [pltpu.roll(full[:, :Q], back, 1) for back in (1, 2, 3)]
    for block in range(NB):
        now = full[:, (block + 1) * Q : (block + 2) * Q]
        turned = [pltpu.roll(now, back, 1) for back in (1, 2, 3)]
        total = taps[:, 3:4] * now
        for back in (1, 2, 3):
            moved = jnp.where(lane < back, before[back - 1], turned[back - 1])
            total = total + taps[:, 3 - back : 4 - back] * moved
        out_ref[:, block * Q : (block + 1) * Q] = silu(total).astype(BF)
        before = turned


def apart(value):
    lane = lax.broadcasted_iota(jnp.int32, value.shape, 1)
    zero = jnp.zeros_like(value)
    return jnp.concatenate(
        [jnp.where(lane < PS, value, zero), jnp.where(lane < PS, zero, value)], axis=0
    )


def of_pair(rows, pair):
    lane = lax.broadcasted_iota(jnp.int32, (1, Q), 1)
    return jnp.where(lane < PS, rows[2 * pair : 2 * pair + 1], rows[2 * pair + 1 : 2 * pair + 2])


def decay_rows(decay):
    wide = jnp.broadcast_to(decay, (8, CH))
    high = wide.astype(BF)
    return jnp.concatenate([high, (wide - high.astype(F32)).astype(BF)], axis=0)


def decay_of(ref):
    return ref[N : N + 1, :].astype(F32) + ref[N + 8 : N + 9, :].astype(F32)


def chained(arrived):
    state, weight = arrived[0][:N, :].astype(F32), decay_of(arrived[0])
    for ref in arrived[1:]:
        state = state + weight * ref[:N, :].astype(F32)
        weight = weight * decay_of(ref)
    return state, weight


def combine(place, end, first, second, third, out_ref):
    state, _ = chained((first, second, third))
    out_ref[...] = (end[:N, :].astype(F32) + decay_of(end) * state).astype(BF)


def states(place, x_ref, run_ref, step_ref, *rest):
    parts, (b_full, c_full, local_ref, end_ref) = rest[:4], rest[4:]
    for part, d in zip(parts, OFFSETS):
        yy = lax.rem(place[1] + (d + NY), NY)
        at = pl.ds(pl.multiple_of(yy * 32, 32), 32)
        b_full[at, :] = part[:32]
        c_full[at, :] = part[32:]
    state = [jnp.zeros((N, Q), F32) for _ in range(HD // 2)]
    total_rate = jnp.zeros((8, Q), F32)
    for block in range(NB):
        at = slice(block * Q, (block + 1) * Q)
        b = b_full[:, at].astype(F32)
        running, step = run_ref[:, at], step_ref[:, at]
        last = running[:, Q - 1 : Q]
        weight = jnp.exp(last - running) * step
        decay = jnp.exp(last)
        for pair in range(HD // 2):
            lanes = slice(pair * Q, (pair + 1) * Q)
            local_ref[block, :, lanes] = state[pair].astype(BF)
            scaled = [(b * weight[h : h + 1, :]).astype(BF) for h in (2 * pair, 2 * pair + 1)]
            increment = jnp.dot(
                jnp.concatenate(scaled, axis=1),
                apart(x_ref[at, lanes]),
                preferred_element_type=F32,
            )
            state[pair] = of_pair(decay, pair) * state[pair] + increment
        total_rate = total_rate + last
    for pair in range(HD // 2):
        end_ref[:N, pair * Q : (pair + 1) * Q] = state[pair].astype(BF)
    end_ref[N:, :] = decay_rows(over_channels(jnp.exp(total_rate)))


def within(place, x_ref, b_ref, c_ref, run_ref, step_ref, skip, y_ref):
    below = lax.broadcasted_iota(jnp.int32, (Q, Q), 0) >= lax.broadcasted_iota(
        jnp.int32, (Q, Q), 1
    )
    for block in range(NB):
        at = slice(block * Q, (block + 1) * Q)
        running, step = run_ref[:, at], step_ref[:, at]
        columns = running.T
        scores = lax.dot_general(
            c_ref[:, at], b_ref[:, at], (((0,), (0,)), ((), ())), preferred_element_type=F32
        )
        for pair in range(HD // 2):
            mixing = []
            for h in (2 * pair, 2 * pair + 1):
                spread = jnp.where(below, columns[:, h : h + 1] - running[h : h + 1, :], -1e30)
                mixing.append((jnp.exp(spread) * step[h : h + 1, :] * scores).astype(BF))
            lanes = slice(pair * Q, (pair + 1) * Q)
            value = x_ref[at, lanes]
            y = jnp.dot(
                jnp.concatenate(mixing, axis=1), apart(value), preferred_element_type=F32
            )
            y_ref[at, lanes] = y + skip[:, lanes] * value.astype(F32)


def per_head(columns):
    return jnp.concatenate(
        [jnp.broadcast_to(columns[:, h : h + 1], (columns.shape[0], PS)) for h in range(HD)],
        axis=1,
    )


def over_channels(rows):
    return jnp.concatenate([rows[h : h + 1, :PS] for h in range(HD)], axis=1)


def carry(place, c_ref, run_ref, local_ref, y_ref, z_own, z_other, *rest):
    arrived, outs, (z_full, sorted_rows) = rest[:4], rest[4:8], rest[8:]
    for k in range(NY):
        z_full[pl.ds(half_start(place, k, False), HALF), :] = z_own[k]
        z_full[pl.ds(half_start(place, k, True), HALF), :] = z_other[k]
    state, weight = chained(arrived[:3])
    state = state + weight * arrived[3][...].astype(F32)
    before = jnp.ones((1, CH), F32)
    for block in range(NB):
        at = slice(block * Q, (block + 1) * Q)
        running = run_ref[:, at]
        full = (local_ref[block].astype(F32) + before * state).astype(BF)
        carried = lax.dot_general(
            c_ref[:, at], full, (((0,), (0,)), ((), ())), preferred_element_type=F32
        )
        grown = jnp.exp(running)
        y = y_ref[at, :] + per_head(grown.T) * carried
        gate = silu(z_full[at, :].astype(F32))
        rel = lax.rem(block // 4 + NY - place[1], NY)
        part = block % 4
        sorted_rows[rel, part * Q : (part + 1) * Q, :] = (y * gate).astype(BF)
        last = jnp.broadcast_to(grown[:, Q - 1 : Q], (8, Q))
        before = before * over_channels(last)
    for rel in range(NY):
        outs[rel][...] = sorted_rows[rel]


def project_far(place, gain, w_ref, *rest):
    parts, (hidden, give, keep) = rest[:NY], rest[NY:]

    @pl.when(pl.program_id(0) == 0)
    def _():
        total = jnp.zeros((ROWS, 1), F32)
        for ref in parts:
            value = ref[...].astype(F32)
            total = total + jnp.sum(value * value, axis=1, keepdims=True)
        scale = lax.rsqrt(total / (NY * CH) + EPSILON)
        for ref, d in zip(parts, OFFSETS):
            yy = lax.rem(place[1] + (d + NY), NY)
            lanes = pl.ds(pl.multiple_of(yy * CH, CH), CH)
            hidden[:, lanes] = (ref[...].astype(F32) * scale * gain[:, lanes]).astype(BF)

    acc = jnp.dot(hidden[...], w_ref[...], preferred_element_type=F32).astype(BF)

    @pl.when(pl.program_id(0) == 0)
    def _():
        give[...] = acc

    @pl.when(pl.program_id(0) == 1)
    def _():
        keep[...] = acc


def project_rest(place, w_ref, hidden, out_ref):
    out_ref[...] = jnp.dot(hidden[...], w_ref[...], preferred_element_type=F32).astype(BF)


def output_call(kernel, place, columns, steps, more, w_out, parts, outs, specs):
    whole = lambda v: pl.BlockSpec(v.shape, lambda i, p: (0,) * v.ndim)
    return pl.pallas_call(
        kernel,
        out_shape=outs,
        grid_spec=pltpu.PrefetchScalarGridSpec(
            num_scalar_prefetch=1,
            grid=(steps,),
            in_specs=[whole(v) for v in more]
            + [pl.BlockSpec((NY * CH, FEAT), columns)]
            + [whole(v) for v in parts],
            out_specs=specs,
        ),
        compiler_params=pltpu.CompilerParams(vmem_limit_bytes=46 * MIB),
        cost_estimate=SMALL,
    )(place, *more, w_out, *parts)


def run_far(place, gain, w_out, parts):
    columns = lambda i, p: (0, lax.rem(p[0] + 2, NX) * NC + jnp.where(i == 0, 1 - p[2], p[2]))
    shapes = [(ROWS, NY * CH), (ROWS, FEAT), (ROWS, FEAT)]
    return output_call(
        project_far,
        place,
        columns,
        2,
        [gain],
        w_out,
        parts,
        [SHAPE(shape, BF) for shape in shapes],
        [pl.BlockSpec(shape, lambda i, p: (0, 0)) for shape in shapes],
    )


def run_rest(place, w_out, hidden, other):
    def columns(i, p):
        ahead = jnp.where(i == 0, 1, jnp.where(i == 1, 3, 0))
        return 0, lax.rem(p[0] + ahead, NX) * NC + (1 - p[2] if other else p[2])

    return output_call(
        project_rest,
        place,
        columns,
        3,
        [],
        w_out,
        [hidden],
        [SHAPE((ROWS, 3 * FEAT), BF)],
        [pl.BlockSpec((ROWS, FEAT), lambda i, p: (0, i))],
    )[0]


def merge_far(place, kept, got, upper, lower):
    total = (kept[...].astype(F32) + got[...].astype(F32)).astype(BF)
    upper[...] = total[:HALF]
    lower[...] = total[HALF:]


def merge_rest(place, kept, got, from_left, from_right, ahead, behind, stays):
    for k, ref in enumerate((ahead, behind, stays)):
        at = slice(k * FEAT, (k + 1) * FEAT)
        upper = kept[:HALF, at].astype(F32) + got[:HALF, at].astype(F32)
        lower = kept[HALF:, at].astype(F32) + got[HALF:, at].astype(F32)
        if k == 0:
            upper = upper + from_left[...].astype(F32)
        if k == 1:
            lower = lower + from_right[...].astype(F32)
        ref[:HALF, :] = upper.astype(ref.dtype)
        ref[HALF:, :] = lower.astype(ref.dtype)


def finish(place, own, first, second, out_ref):
    out_ref[...] = (own[...] + first[...].astype(F32) + second[...].astype(F32)).astype(BF)


def on_device(tokens, w_zx, w_bc, w_dt, conv_x, conv_bc, dt_bias, a_log, d_skip, norm_gain, w_out):
    y, c = lax.axis_index("y"), lax.axis_index("c")
    place = jnp.stack([lax.axis_index("x"), y, c, lax.axis_index("z")]).astype(jnp.int32)
    rows = w_zx.shape[0]

    def quarter(value, distance, width, dim=1):
        start = lax.rem(y + (distance + NY), NY) * width
        return lax.dynamic_slice_in_dim(value, start, width, dim)

    def for_y(distance):
        zero = jnp.zeros((rows, W1 - CH - 64 - HD), BF)
        return jnp.concatenate(
            [
                quarter(w_zx[:, 1], distance, CH),
                quarter(w_bc[:, 0], distance, 32),
                quarter(w_bc[:, 1], distance, 32),
                quarter(w_dt, distance, HD),
                zero,
            ],
            axis=1,
        )

    mine = half_rows(tokens, c)
    gate = lambda d: quarter(w_zx[:, 0], d, CH)
    pieces, first, second = gather_tokens(
        mine, [for_y(d) for d in range(NY)], [gate(d) for d in range(NY)]
    )
    weights_1 = lax.all_gather(jnp.concatenate(first), ("z", "c"), axis=0, tiled=True)
    weights_1 = weights_1.reshape(NZ, NC, NY, rows, W1)
    weights_2 = lax.all_gather(jnp.concatenate(second), ("z", "c"), axis=0, tiled=True)
    weights_2 = weights_2.reshape(NZ, NC, NY, rows, CH)

    taps_x = quarter(conv_x, 0, CH).astype(F32)
    taps_bc = jnp.concatenate([quarter(conv_bc[:, k], 0, 32) for k in range(2)], axis=1)
    taps_bc = taps_bc.T.astype(F32)
    column = lambda v: jnp.pad(quarter(v, 0, HD, 0), (0, 8 - HD)).reshape(8, 1)
    skip = jnp.repeat(quarter(d_skip, 0, HD, 0), PS).reshape(1, CH)
    gain = norm_gain.astype(F32).reshape(1, -1)

    kinds = [
        SHAPE((NY, HALF, CH), BF),
        SHAPE((64, NY * HALF), BF),
        SHAPE((8, NY * HALF), F32),
        SHAPE((96, Q), BF),
    ]
    first_outs = run_projection(project_first, place, pieces, weights_1, 768, kinds * 2)
    x_own, bc_own, dt_own, tail_own = first_outs[:4]
    x_give, bc_give, dt_give, tail_give = first_outs[4:]
    bc_got = sibling(bc_give)
    halo_own = routed(
        tail_own, lambda z, y, x, c: (z + 1, y, x, 1) if z + 1 < NZ and c == 1 else None
    )
    halo_give = routed(
        tail_give, lambda z, y, x, c: (z + 1, y, x, 0) if z + 1 < NZ and c == 1 else None
    )
    x_got, dt_got = sibling(x_give), sibling(dt_give)
    (bc,) = local_call(
        convolve_side,
        [SHAPE((64, T), BF)],
        place,
        bc_own,
        bc_got,
        halo_own,
        halo_give,
        taps_bc,
        scratch=[pltpu.VMEM((64, T + Q), F32)],
    )
    x_conv, running, step = local_call(
        conv_and_rates,
        [SHAPE((T, CH), BF), SHAPE((8, T), F32), SHAPE((8, T), F32)],
        place,
        x_own,
        x_got,
        halo_own,
        halo_give,
        taps_x,
        dt_own,
        dt_got,
        column(dt_bias),
        column(a_log),
        scratch=[pltpu.VMEM((T + 16, CH), F32), pltpu.VMEM((8, T), F32)],
        cost=pl.CostEstimate(flops=10**9, bytes_accessed=8 * MIB, transcendentals=0),
    )
    bc_parts = [bc] + [shifted(bc, "y", d) for d in (1, -1, 2)]
    b_conv, c_conv, local, end = local_call(
        states,
        [SHAPE((N, T), BF), SHAPE((N, T), BF), SHAPE((NB, N, CH), BF), SHAPE((N + 16, CH), BF)],
        place,
        x_conv,
        running,
        step,
        *bc_parts,
    )
    later = lambda v, d: lax.ppermute(v, "z", [(i, i + d) for i in range(NZ - d)])
    near = [later(end, d) for d in (1, 2, 3)]
    place_2, end = lax.optimization_barrier((place, end))
    z_own, z_give = run_projection(project_second, place_2, pieces, weights_2, 512, kinds[:1] * 2)
    near, z_give = lax.optimization_barrier((near, z_give))
    z_got = sibling(z_give)
    (window,) = local_call(combine, [SHAPE((N, CH), BF)], place, end, *near)
    place_3, window = lax.optimization_barrier((place, window))
    far_end = later(window, 4)
    (y_within,) = local_call(
        within, [SHAPE((T, CH), F32)], place_3, x_conv, b_conv, c_conv, running, step, skip
    )
    sorted_rows = local_call(
        carry,
        [SHAPE((ROWS, CH), BF)] * NY,
        place,
        c_conv,
        running,
        local,
        y_within,
        z_own,
        z_got,
        *near,
        far_end,
        scratch=[pltpu.VMEM((T, CH), BF), pltpu.VMEM((NY, ROWS, CH), BF)],
    )
    block = (ROWS, FEAT)
    hidden, far_give, far_keep = run_far(place, gain, w_out, over_y(sorted_rows))
    far_got = sibling(far_give)
    half_block = (HALF, FEAT)
    upper, lower = local_call(merge_far, [SHAPE(half_block, BF)] * 2, place, far_keep, far_got)
    place_4, upper, lower = lax.optimization_barrier((place, upper, lower))
    from_left, from_right = shifted(upper, "x", 1), shifted(lower, "x", -1)
    rest_give = run_rest(place_4, w_out, hidden, True)
    rest_got = sibling(rest_give)
    rest_keep = run_rest(place_4, w_out, hidden, False)
    ahead, behind, stays = local_call(
        merge_rest,
        [SHAPE(block, kind) for kind in (BF, BF, F32)],
        place,
        rest_keep,
        rest_got,
        from_left,
        from_right,
    )
    (out,) = local_call(
        finish,
        [SHAPE(block, BF)],
        place,
        stays,
        shifted(ahead, "x", 1),
        shifted(behind, "x", -1),
    )
    return out


def solution(mesh):
    fine = Mesh(mesh.devices.reshape(NZ, NY, NX, NC), ("z", "y", "x", "c"))
    seq, head = ("z", "y"), ("x", "c")
    return jax.shard_map(
        on_device,
        mesh=fine,
        in_specs=(
            P(seq, head),
            P(seq, None, head),
            P(seq, None, head),
            P(seq, head),
            P(None, head),
            P(None, None, head),
            P(head),
            P(head),
            P(head),
            P(head),
            P(head, None),
        ),
        out_specs=P(seq, head),
        check_vma=False,
    )
```
